32 devices in a mesh: tok: 4 (over y, core), wide: 8 (over z, x).
Axes of the slice: x: 2, y: 2, z: 4, core: 2. Of those that a mesh axis runs over, the one named last changes fastest.
Arguments:
- tokens: bfloat16 [8192, 2048], P('tok', 'wide'), may hold values from -6 to 6
- cotangent: bfloat16 [8192, 2048], P('tok', 'wide'), may hold values from -6 to 6
- gain_attn: float32 [2048], P('wide'), may hold values from 0.5 to 1.5
- gain_ffn: float32 [2048], P('wide'), may hold values from 0.5 to 1.5
- w_query: bfloat16 [2048, 2048], P('wide'), may hold values from -0.125 to 0.125
- w_key: bfloat16 [2048, 256], P('wide'), may hold values from -0.125 to 0.125
- w_value: bfloat16 [2048, 256], P('wide'), may hold values from -0.125 to 0.125
- w_output: bfloat16 [2048, 2048], P('wide'), may hold values from -0.125 to 0.125
- w_gate: bfloat16 [2048, 5632], P('wide'), may hold values from -0.125 to 0.125
- w_up: bfloat16 [2048, 5632], P('wide'), may hold values from -0.125 to 0.125
- w_down: bfloat16 [5632, 2048], P('wide'), may hold values from -0.078125 to 0.078125
- adapt_main: float32 [2048, 96], P('wide'), may hold values from -0.125 to 0.125
- adapt_down: float32 [5632, 16], P('wide'), may hold values from -0.078125 to 0.078125
- adapt_outer: float32 [16, 17920], replicated, may hold values from -0.375 to 0.375
- magnitudes: float32 [17920], replicated, may hold values from 0.5 to 12
- main_first: float32 [2048, 96], P('wide', 'tok'), may hold values from -0.001953125 to 0.001953125
- main_second: float32 [2048, 96], P('wide', 'tok'), may hold values from 1.6910173e-09 to 6.7640693e-09
- down_first: float32 [5632, 16], P('wide', 'tok'), may hold values from -0.001953125 to 0.001953125
- down_second: float32 [5632, 16], P('wide', 'tok'), may hold values from 1.6910173e-09 to 6.7640693e-09
- outer_first: float32 [16, 17920], P(None, ('tok', 'wide')), may hold values from -0.001953125 to 0.001953125
- outer_second: float32 [16, 17920], P(None, ('tok', 'wide')), may hold values from 1.6910173e-09 to 6.7640693e-09
- mag_first: float32 [17920], P(('tok', 'wide')), may hold values from -0.0078125 to 0.0078125
- mag_second: float32 [17920], P(('tok', 'wide')), may hold values from 1.3528139e-09 to 5.4112554e-09
- segments: int32 [4, 2048], P('tok'), may hold values from 0 to 7, never falling along the last dimension, each value on 1 to 1024 neighbouring positions
Outputs:
- layer_out: bfloat16 [8192, 2048], P('tok', 'wide')
- grad_tokens: bfloat16 [8192, 2048], P('tok', 'wide')
- grad_norm: float32 [], replicated
- main_new: float32 [2048, 96], P('wide', 'tok')
- main_first_new: float32 [2048, 96], P('wide', 'tok')
- main_second_new: float32 [2048, 96], P('wide', 'tok')
- down_new: float32 [5632, 16], P('wide', 'tok')
- down_first_new: float32 [5632, 16], P('wide', 'tok')
- down_second_new: float32 [5632, 16], P('wide', 'tok')
- outer_new: float32 [16, 17920], P(None, ('tok', 'wide'))
- outer_first_new: float32 [16, 17920], P(None, ('tok', 'wide'))
- outer_second_new: float32 [16, 17920], P(None, ('tok', 'wide'))
- mag_new: float32 [17920], P(('tok', 'wide'))
- mag_clipped: float32 [17920], P(('tok', 'wide'))
- mag_second_new: float32 [17920], P(('tok', 'wide'))
The draws below stay inside these ranges and needn't reach their ends.
Inputs may be any that keep to these rules, and one draw needn't show every extreme that they name: `segments`: segment numbers along a row never fall; each segment holds 1 to 1024 positions, and one holds exactly that many.
All inputs are finite; a program needn't handle non-finite values.
Results may differ from the reference program's by a relative error of at most 0.023.
Values may be sent and summed in bfloat16 or wider, within the bound.
No kernel may reach another device: no remote copies, remote signals or barrier semaphores. Data moves between devices by JAX's collectives and lax.ppermute only.
A program may use at most 448 MiB of HBM per device.

```python
import math
import jax
import jax.numpy as jnp
import numpy as np
from jax import lax

D = 2048
HEADS = 32
HD = 64
KVH = 4
FF = 5632
RANK = 16
SEQ = 2048
SEGS = 8
STEP = 10
ROWS = 4
TOKENS = 8192
OUTS = 17920


def draw_magnitudes(key, part):
    columns = jnp.arange(OUTS, dtype=jnp.int32)
    output_begin = D + 2 * KVH * HD
    output_end = 2 * D + 2 * KVH * HD
    down_begin = 2 * D + 2 * KVH * HD + 2 * FF
    factors = jnp.where((columns >= output_begin) & (columns < output_end), 6.0, 1.0)
    factors = jnp.where(columns >= down_begin, 2.0, factors).astype(jnp.float32)
    drawn = jnp.exp(jax.random.uniform(key, (OUTS,), jnp.float32, math.log(0.5), math.log(2.0)))
    return (drawn * factors).astype(jnp.float32)


def level_of(stream_key, shape, shards, smallest, top_value):
    def one(axis_at, parts):
        heights = jax.random.uniform(jax.random.fold_in(jax.random.fold_in(stream_key, 6), axis_at), (parts,), jnp.float32, smallest / len(shards), top_value / len(shards))
        return jnp.repeat(jnp.exp(heights), shape[axis_at] // parts).reshape((-1,) + (1,) * (len(shape) - axis_at - 1))

    factor_of = one(*shards[0])
    for cut in shards[1:]:
        factor_of = factor_of * one(*cut)
    return factor_of


def split_up(amount, total, most, slope):
    loads = [(1 << 20) // math.isqrt(grade ** slope) + 1 for grade in range(2, amount + 1)]
    spare, counts = total - most - (amount - 1), [1] * (amount - 1)
    while spare > 0:
        movable = [i for i in range(amount - 1) if counts[i] < most]
        pool, left = sum([loads[i] for i in movable]), spare
        for i in movable:
            more = min(most - counts[i], max(1, left * loads[i] // pool), spare)
            counts[i] = counts[i] + more
            spare = spare - more
    return np.array([most] + counts)


def uneven(stream_key, number_of, total, reach, skew):
    if number_of == 2:
        one = jax.random.randint(stream_key, (), max(1, total - reach), min(reach, total - 1) + 1)
        return jnp.stack([one, total - one])
    sizes = jnp.asarray(split_up(number_of, total, reach, skew), jnp.int32)
    pairs = (number_of - 1) // 2
    donor, taker = sizes[1:1 + 2 * pairs:2], sizes[2:2 + 2 * pairs:2]
    margin = jnp.minimum(donor - 1, reach - taker)
    shifted = jax.random.randint(jax.random.fold_in(stream_key, 1), (pairs,), 0, 1 << 20) % (margin + 1)
    sizes = sizes.at[1:1 + 2 * pairs:2].set(donor - shifted).at[2:2 + 2 * pairs:2].set(taker + shifted)
    return sizes[jax.random.permutation(jax.random.fold_in(stream_key, 2), number_of)]


def noise(key, shape, width, most, shards=(), kind=jnp.bfloat16):
    array = jax.random.normal(key, shape, jnp.float32) * width
    if len(shards) > 0:
        array = level_of(key, shape, shards, -0.22, 0.18) * array
    return jnp.clip(array, min=-most, max=most).astype(kind)


def setup_inputs(seed: int = 0) -> dict:
    arg_keys = jax.random.split(jax.random.key(seed), 25)
    return {
        "tokens": noise(arg_keys[0], (TOKENS, D), 1.0, 6.0, ((0, 4), (1, 8))),
        "cotangent": noise(arg_keys[1], (TOKENS, D), 1.0, 6.0, ((0, 4), (1, 8))),
        "gain_attn": jnp.clip(1.0 + 0.1 * jax.random.normal(arg_keys[2], (D,), jnp.float32), 0.5, 1.5),
        "gain_ffn": jnp.clip(1.0 + 0.1 * jax.random.normal(arg_keys[3], (D,), jnp.float32), 0.5, 1.5),
        "w_query": noise(arg_keys[4], (D, D), D ** -0.5, 0.125, ((0, 8),)),
        "w_key": noise(arg_keys[5], (D, KVH * HD), D ** -0.5, 0.125, ((0, 8),)),
        "w_value": noise(arg_keys[6], (D, KVH * HD), D ** -0.5, 0.125, ((0, 8),)),
        "w_output": noise(arg_keys[7], (D, D), D ** -0.5, 0.125, ((0, 8),)),
        "w_gate": noise(arg_keys[8], (D, FF), D ** -0.5, 0.125, ((0, 8),)),
        "w_up": noise(arg_keys[9], (D, FF), D ** -0.5, 0.125, ((0, 8),)),
        "w_down": noise(arg_keys[10], (FF, D), FF ** -0.5, 0.078125, ((0, 8),)),
        "adapt_main": noise(arg_keys[11], (D, 6 * RANK), D ** -0.5, 0.125, ((0, 8),), jnp.float32),
        "adapt_down": noise(arg_keys[12], (FF, RANK), FF ** -0.5, 0.078125, ((0, 8),), jnp.float32),
        "adapt_outer": noise(arg_keys[13], (RANK, OUTS), (16 * RANK) ** -0.5, 0.375, (), jnp.float32),
        "magnitudes": draw_magnitudes(jax.random.fold_in(arg_keys[24], 71), 0),
        "main_first": noise(arg_keys[15], (D, 6 * RANK), (0.111 * (RANK * (6 * D + FF + OUTS) + OUTS) ** -0.5), 0.001953125, ((0, 8), (1, 4)), jnp.float32),
        "main_second": jnp.clip(jnp.exp(math.log(6.764069304665554e-09) - 1.3862944 * jax.random.uniform(arg_keys[16], (D, 6 * RANK), jnp.float32) ** level_of(arg_keys[16], (D, 6 * RANK), ((0, 8), (1, 4)), -0.2, 0.2)), 1.6910173261663886e-09, 6.764069304665554e-09),
        "down_first": noise(arg_keys[17], (FF, RANK), (0.111 * (RANK * (6 * D + FF + OUTS) + OUTS) ** -0.5), 0.001953125, ((0, 8), (1, 4)), jnp.float32),
        "down_second": jnp.clip(jnp.exp(math.log(6.764069304665554e-09) - 1.3862944 * jax.random.uniform(arg_keys[18], (FF, RANK), jnp.float32) ** level_of(arg_keys[18], (FF, RANK), ((0, 8), (1, 4)), -0.2, 0.2)), 1.6910173261663886e-09, 6.764069304665554e-09),
        "outer_first": noise(arg_keys[19], (RANK, OUTS), (0.111 * (RANK * (6 * D + FF + OUTS) + OUTS) ** -0.5), 0.001953125, ((1, 32),), jnp.float32),
        "outer_second": jnp.clip(jnp.exp(math.log(6.764069304665554e-09) - 1.3862944 * jax.random.uniform(arg_keys[20], (RANK, OUTS), jnp.float32) ** level_of(arg_keys[20], (RANK, OUTS), ((1, 32),), -0.2, 0.2)), 1.6910173261663886e-09, 6.764069304665554e-09),
        "mag_first": noise(arg_keys[21], (OUTS,), (0.444 * (RANK * (6 * D + FF + OUTS) + OUTS) ** -0.5), 0.0078125, ((0, 32),), jnp.float32),
        "mag_second": jnp.clip(jnp.exp(math.log(5.411255443732443e-09) - 1.3862944 * jax.random.uniform(arg_keys[22], (OUTS,), jnp.float32) ** level_of(arg_keys[22], (OUTS,), ((0, 32),), -0.2, 0.2)), 1.3528138609331108e-09, 5.411255443732443e-09),
        "segments": jax.vmap(lambda own: jnp.searchsorted(jnp.cumsum(uneven(own, SEGS, SEQ, SEQ // 2, 0)), jnp.arange(SEQ), side="right"))(jax.random.split(arg_keys[23], ROWS)).reshape((ROWS, SEQ)).astype(jnp.int32),
    }


EPS_NORM = 1e-05
ROPE_BASE = 10000.0
DORA_SCALE = 2.0
CLIP_MAX = 1.0
BETA_FIRST = 0.9
BETA_SECOND = 0.999
ADAM_EPS = 1e-08
WEIGHT_DECAY = 0.01
RATE_ADAPT = 0.02
RATE_OUTER = 0.05
RATE_MAGNITUDE = 0.4
PRECISE = lax.Precision.HIGHEST
MASKED = -1e+30

@jax.custom_vjp
def low(v):
    return lax.optimization_barrier(v.astype(jnp.bfloat16)).astype(jnp.float32)

@jax.custom_vjp
def low_back(v):
    return v

def low_keep(v):
    return (low(v), None)

def low_pass(kept, grad):
    return (grad,)

def back_keep(v):
    return (v, None)

def back_low(kept, grad):
    return (low(grad),)
low.defvjp(low_keep, low_pass)
low_back.defvjp(back_keep, back_low)

def column_spans():
    widths = [D, KVH * HD, KVH * HD, D, FF, FF, D]
    col_spans = []
    offset = 0
    for col_width in widths:
        col_spans.append((offset, col_width))
        offset = offset + col_width
    return col_spans

def rotary_tables(segment_row):
    length = segment_row.shape[0]
    places = jnp.arange(length, dtype=jnp.int32)
    earlier = jnp.concatenate([segment_row[:1] - 1, segment_row[:-1]])
    starts = lax.cummax(jnp.where(segment_row != earlier, places, 0), axis=0)
    offsets = (places - starts).astype(jnp.float32)
    half_dim = HD // 2
    frequency = ROPE_BASE ** (-2.0 * jnp.arange(half_dim, dtype=jnp.float32) / HD)
    angles = offsets[:, None] * frequency[None, :]
    allowed = (places[None, :] <= places[:, None]) & (segment_row[:, None] == segment_row[None, :])
    return (jnp.cos(angles), jnp.sin(angles), allowed)

def rotate(values, cosine_table, sine_table):
    half_dim = values.shape[-1] // 2
    first_half = values[..., :half_dim]
    second_half = values[..., half_dim:]
    cos_wide = cosine_table[:, None, :]
    sin_wide = sine_table[:, None, :]
    return jnp.concatenate([first_half * cos_wide - second_half * sin_wide, second_half * cos_wide + first_half * sin_wide], axis=-1)

def attend_row(pieces):
    query_row, key_row, value_row, segment_row = pieces
    length = query_row.shape[0]
    cosine_table, sine_table, allowed = rotary_tables(segment_row)
    queries = low(rotate(query_row.reshape(length, HEADS, HD), cosine_table, sine_table))
    keys_rot = low(rotate(key_row.reshape(length, KVH, HD), cosine_table, sine_table))
    values_low = low(value_row.reshape(length, KVH, HD))
    grouped = queries.reshape(length, KVH, HEADS // KVH, HD)
    scores = jnp.einsum('tkgd,skd->kgts', grouped, keys_rot, precision=PRECISE) * HD ** (-0.5)
    scores = low_back(scores)
    scores = jnp.where(allowed[None, None], scores, MASKED)
    weights = jax.nn.softmax(scores, axis=-1)
    mixed_heads = jnp.einsum('kgts,skd->tkgd', low(weights), values_low, precision=PRECISE)
    return mixed_heads.reshape(length, HEADS * HD)

def rms_norm(values, gain_row):
    return values * lax.rsqrt(lax.optimization_barrier(jnp.mean(values * values, axis=-1, keepdims=True)) + EPS_NORM) * gain_row

def adam(param, grad, first, second, rate, clip_factor):
    clipped = grad * clip_factor
    first_new = BETA_FIRST * first + (1.0 - BETA_FIRST) * clipped
    second_new = BETA_SECOND * second + (1.0 - BETA_SECOND) * clipped * clipped
    first_hat = first_new / (1.0 - BETA_FIRST ** STEP)
    second_hat = second_new / (1.0 - BETA_SECOND ** STEP)
    param_new = param - rate * (first_hat / (jnp.sqrt(second_hat) + ADAM_EPS) + WEIGHT_DECAY * param)
    return (param_new, first_new, second_new)

def reference(tokens, cotangent, gain_attn, gain_ffn, w_query, w_key, w_value, w_output, w_gate, w_up, w_down, adapt_main, adapt_down, adapt_outer, magnitudes, main_first, main_second, down_first, down_second, outer_first, outer_second, mag_first, mag_second, segments):
    bases = [weight.astype(jnp.float32) for weight in (w_query, w_key, w_value, w_output, w_gate, w_up, w_down)]
    col_spans = column_spans()

    def forward(inputs, a_main, a_down, outer, mags):
        adapters = [a_main[:, number * RANK:(number + 1) * RANK] for number in range(6)] + [a_down]
        norm_list = []
        for number in range(7):
            col_start, col_width = col_spans[number]
            merged = bases[number] + DORA_SCALE * jnp.dot(adapters[number], outer[:, col_start:col_start + col_width], precision=PRECISE)
            norm_list.append(jnp.sqrt(lax.optimization_barrier(jnp.sum(merged * merged, axis=0))))
        scales = mags / jnp.concatenate(norm_list)

        def project(number, inputs_low):
            col_start, col_width = col_spans[number]
            product = jnp.dot(inputs_low, bases[number], precision=PRECISE)
            reduced = jnp.dot(inputs_low, low(adapters[number]), precision=PRECISE)
            product = product + DORA_SCALE * jnp.dot(reduced, low(outer[:, col_start:col_start + col_width]), precision=PRECISE)
            return low_back(product) * scales[col_start:col_start + col_width]
        normed_one = low(rms_norm(inputs, gain_attn))
        query = project(0, normed_one)
        key = project(1, normed_one)
        value = project(2, normed_one)
        mixed_rows = lax.map(jax.checkpoint(attend_row), (query.reshape(-1, SEQ, HEADS * HD), key.reshape(-1, SEQ, KVH * HD), value.reshape(-1, SEQ, KVH * HD), segments))
        attended = low(low_back(mixed_rows.reshape(-1, HEADS * HD)))
        hidden_one = inputs + project(3, attended)
        normed_two = low(rms_norm(hidden_one, gain_ffn))
        gate_act = project(4, normed_two)
        up_act = project(5, normed_two)
        hidden = low(jax.nn.silu(gate_act) * up_act)
        return hidden_one + project(6, hidden)
    layer_sum, pullback = jax.vjp(forward, tokens.astype(jnp.float32), adapt_main, adapt_down, adapt_outer, magnitudes)
    grad_inputs, grad_main, grad_down, grad_outer, grad_mag = pullback(cotangent.astype(jnp.float32))
    grad_total = jnp.sum(grad_main * grad_main) + jnp.sum(grad_down * grad_down) + jnp.sum(grad_outer * grad_outer) + jnp.sum(grad_mag * grad_mag)
    grad_norm = jnp.sqrt(grad_total)
    clip_factor = CLIP_MAX / jnp.maximum(grad_norm, CLIP_MAX)
    main_new, main_first_new, main_second_new = adam(adapt_main, grad_main, main_first, main_second, RATE_ADAPT, clip_factor)
    down_new, down_first_new, down_second_new = adam(adapt_down, grad_down, down_first, down_second, RATE_ADAPT, clip_factor)
    outer_new, outer_first_new, outer_second_new = adam(adapt_outer, grad_outer, outer_first, outer_second, RATE_OUTER, clip_factor)
    mag_new, mag_first_new, mag_second_new = adam(magnitudes, grad_mag, mag_first, mag_second, RATE_MAGNITUDE, clip_factor)
    mag_clipped = grad_mag * clip_factor
    return (layer_sum.astype(jnp.bfloat16), grad_inputs.astype(jnp.bfloat16), grad_norm, main_new, main_first_new, main_second_new, down_new, down_first_new, down_second_new, outer_new, outer_first_new, outer_second_new, mag_new, mag_clipped, mag_second_new)
```

```python
import jax
import jax.numpy as jnp
from jax import lax
from jax.sharding import PartitionSpec as P

D = 2048
HEADS = 32
HD = 64
KVH = 4
FF = 5632
STEP = 10
RANK = 16
CHUNKS = 8
EXTRA = 128

EPS_NORM = 1e-05
ROPE_BASE = 10000.0
CLIP_MAX = 1.0
BETA_FIRST = 0.9
BETA_SECOND = 0.999
ADAM_EPS = 1e-08
WEIGHT_DECAY = 0.01
RATE_ADAPT = 0.02
RATE_OUTER = 0.05
RATE_MAGNITUDE = 0.4
PRECISE = lax.Precision.HIGHEST
MASKED = -1e30
BF = jnp.bfloat16
F32 = jnp.float32
WIDTHS = [D, KVH * HD, KVH * HD, D, FF, FF, D]
STARTS = [sum(WIDTHS[:number]) for number in range(7)]
OUTS = sum(WIDTHS)


def bits_of(count):
    return [1 << place for place in range(count.bit_length() - 1)]


def swap(array, axis, distance):
    count = lax.axis_size(axis)
    return lax.ppermute(array, axis, [(i, i ^ distance) for i in range(count)])


def mm(left, right):
    return jnp.dot(left, right, preferred_element_type=F32)


def mm_t(left, right):
    return lax.dot_general(left, right, (((1,), (1,)), ((), ())), preferred_element_type=F32)


def t_mm(left, right):
    return lax.dot_general(left, right, (((0,), (0,)), ((), ())), preferred_element_type=F32)


def two_parts(values):
    high = lax.reduce_precision(values, 8, 7)
    return high.astype(BF), (values - high).astype(BF)


def fold_parts(stacked, count):
    return stacked[:count] + stacked[count : 2 * count]


def adam(param, grad, first, second, rate, clip_factor):
    clipped = grad * clip_factor
    first_new = BETA_FIRST * first + (1.0 - BETA_FIRST) * clipped
    second_new = BETA_SECOND * second + (1.0 - BETA_SECOND) * clipped * clipped
    first_hat = first_new / (1.0 - BETA_FIRST**STEP)
    second_hat = second_new / (1.0 - BETA_SECOND**STEP)
    param_new = param - rate * (
        first_hat / (jnp.sqrt(second_hat) + ADAM_EPS) + WEIGHT_DECAY * param
    )
    return (param_new, first_new, second_new)


def squared_sum(values):
    return jnp.sum(values * values)


def all_sum(values, axes):
    for axis in axes:
        for bit in bits_of(lax.axis_size(axis)):
            values = values + swap(values, axis, bit)
    return values


def all_blocks(block, axis):
    stacked = block[None]
    index = lax.axis_index(axis)
    for bit in bits_of(lax.axis_size(axis)):
        upper = (index // bit) % 2 == 1
        received = swap(stacked, axis, bit)
        stacked = jnp.concatenate(
            [jnp.where(upper, received, stacked), jnp.where(upper, stacked, received)]
        )
    return stacked


def scatter_sum(blocks, axis, wire=F32):
    index = lax.axis_index(axis)
    for bit in reversed(bits_of(lax.axis_size(axis))):
        halves = blocks.reshape((2, bit) + blocks.shape[1:])
        side = (index // bit) % 2
        keep = lax.dynamic_index_in_dim(halves, side, 0, keepdims=False)
        send = lax.dynamic_index_in_dim(halves, 1 - side, 0, keepdims=False)
        blocks = keep + swap(send.astype(wire), axis, bit).astype(blocks.dtype)
    return blocks[0]


def gather_rows(shard, extra):
    count = lax.axis_size("wide")
    index = lax.axis_index("wide")
    rows = shard.shape[0]
    slots = {0: shard}
    for slot in range(1, count):
        low = slot & -slot
        slots[slot] = swap(slots[slot ^ low], "wide", low)
    whole = jnp.zeros((count * rows + extra.shape[0], shard.shape[1]), shard.dtype)
    whole = lax.dynamic_update_slice(whole, extra, (count * rows, 0))
    for slot, held in slots.items():
        whole = lax.dynamic_update_slice(whole, held, ((index ^ slot) * rows, 0))
    return whole


def rotate_half(values):
    half = HD // 2
    return jnp.concatenate([-values[..., half:], values[..., :half]], axis=-1)


def turn(values, cosine, sine):
    shaped = values.reshape(values.shape[0], -1, HD)
    turned = shaped * cosine[:, None, :] + rotate_half(shaped) * sine[:, None, :]
    return turned.reshape(values.shape)


def pad_rows(rows, count):
    return jnp.concatenate([rows, jnp.zeros((count - rows.shape[0], rows.shape[1]), rows.dtype)])


def extended(inputs, reduced):
    high, low = two_parts(reduced)
    parts = jnp.concatenate(
        [inputs, high, low, jnp.zeros((inputs.shape[0], EXTRA - 2 * reduced.shape[1]), BF)], axis=1
    )
    return parts


def block_rows(blocks):
    total = sum(block.shape[1] for block in blocks)
    rows = []
    start = 0
    for block in blocks:
        rows.append(jnp.pad(block, ((0, 0), (start, total - start - block.shape[1]))))
        start = start + block.shape[1]
    return jnp.concatenate(rows)


def extra_rows(outer_blocks):
    doubled = block_rows([2.0 * block.astype(BF) for block in outer_blocks]).astype(BF)
    return pad_rows(jnp.concatenate([doubled, doubled]), EXTRA)


def stacked_back(grad_low, weighted, weights):
    high, low = two_parts(weighted)
    return mm_t(jnp.concatenate([grad_low, high, low]), weights)


def attend(queries, keys, values, places, starts):
    count = queries.shape[0]
    grouped = queries.reshape(count, KVH, HEADS // KVH, HD)
    keys = keys.reshape(-1, KVH, HD)
    values = values.reshape(-1, KVH, HD)
    spots = jnp.arange(keys.shape[0], dtype=jnp.int32)
    allowed = (spots[None, :] <= places[:, None]) & (spots[None, :] >= starts[:, None])
    scores = jnp.einsum("tkgd,skd->kgts", grouped, keys, preferred_element_type=F32) * HD**-0.5
    scores = jnp.where(allowed[None, None], scores, MASKED)
    peak = jnp.max(scores, axis=-1, keepdims=True)
    powers = jnp.exp(scores - peak)
    total = jnp.sum(powers, axis=-1, keepdims=True)
    mixed = jnp.einsum(
        "kgts,skd->tkgd", (powers / total).astype(BF), values, preferred_element_type=F32
    )
    return mixed.reshape(count, HEADS * HD).astype(BF), peak + jnp.log(total)


def attend_back(queries, keys, values, places, starts, log_total, attended, grad_mixed):
    count = queries.shape[0]
    grouped = queries.reshape(count, KVH, HEADS // KVH, HD)
    grads = grad_mixed.reshape(count, KVH, HEADS // KVH, HD)
    keys = keys.reshape(-1, KVH, HD)
    values = values.reshape(-1, KVH, HD)
    spots = jnp.arange(keys.shape[0], dtype=jnp.int32)
    allowed = (spots[None, :] <= places[:, None]) & (spots[None, :] >= starts[:, None])
    scores = jnp.einsum("tkgd,skd->kgts", grouped, keys, preferred_element_type=F32) * HD**-0.5
    weights = jnp.where(allowed[None, None], jnp.exp(scores - log_total), 0.0)
    grad_weights = jnp.einsum("tkgd,skd->kgts", grads, values, preferred_element_type=F32)
    inner = jnp.sum(weights * grad_weights, axis=-1, keepdims=True)
    grad_scores = (weights * (grad_weights - inner)).astype(BF)
    grad_queries = jnp.einsum("kgts,skd->tkgd", grad_scores, keys, preferred_element_type=F32)
    grad_keys = jnp.einsum("kgts,tkgd->skd", grad_scores, grouped, preferred_element_type=F32)
    grad_values = jnp.einsum(
        "kgts,tkgd->skd", weights.astype(BF), grads, preferred_element_type=F32
    )
    return (
        grad_queries.reshape(count, HEADS * HD) * HD**-0.5,
        grad_keys.reshape(-1, KVH * HD) * HD**-0.5,
        grad_values.reshape(-1, KVH * HD),
    )


def shards(
    tokens,
    cotangent,
    gain_attn,
    gain_ffn,
    w_query,
    w_key,
    w_value,
    w_output,
    w_gate,
    w_up,
    w_down,
    adapt_main,
    adapt_down,
    adapt_outer,
    magnitudes,
    main_first,
    main_second,
    down_first,
    down_second,
    outer_first,
    outer_second,
    mag_first,
    mag_second,
    segments,
):
    wide_count = lax.axis_size("wide")
    tok_count = lax.axis_size("tok")
    wide = lax.axis_index("wide")
    tok = lax.axis_index("tok")
    core = tok % 2
    length, share = tokens.shape
    hidden_share = w_down.shape[0]
    part = hidden_share // 4
    block = length // (wide_count * CHUNKS)
    count = CHUNKS * block
    block_cols = wide_count * part

    def partner(array):
        return swap(array, "tok", 2)

    def other_core(array):
        return swap(array, "tok", 1)

    def to_tokens(features):
        pieces = features.reshape(CHUNKS, wide_count, block, share)
        whole = jnp.zeros((count, D), features.dtype)
        for slot in range(wide_count):
            piece = lax.dynamic_index_in_dim(pieces, wide ^ slot, 1, keepdims=False)
            piece = piece.reshape(count, share)
            if slot:
                piece = swap(piece, "wide", slot)
            whole = lax.dynamic_update_slice(whole, piece, (0, (wide ^ slot) * share))
        return whole

    def from_tokens(rows):
        whole = jnp.zeros((CHUNKS, wide_count, block, share), rows.dtype)
        for slot in range(wide_count):
            piece = lax.dynamic_slice(rows, (0, (wide ^ slot) * share), (count, share))
            if slot:
                piece = swap(piece, "wide", slot)
            piece = piece.reshape(CHUNKS, 1, block, share)
            whole = lax.dynamic_update_slice(whole, piece, (0, wide ^ slot, 0, 0))
        return whole.reshape(length, share)

    residual = to_tokens(tokens).astype(F32)
    gains = all_blocks(jnp.stack([gain_attn, gain_ffn]), "wide")
    gains = jnp.swapaxes(gains, 0, 1).reshape(2, D)

    bases = [w_query, w_key, w_value, w_output, w_gate, w_up, w_down]
    own_main = [adapt_main[:, n * RANK : (n + 1) * RANK] for n in range(6)] + [adapt_down]
    outers = [adapt_outer[:, STARTS[n] : STARTS[n] + WIDTHS[n]] for n in range(7)]
    norm_parts = []
    cross_parts = []
    for n in range(7):
        cols = WIDTHS[n] // tok_count
        merged = lax.dynamic_slice_in_dim(bases[n], tok * cols, cols, 1).astype(F32) + 2.0 * jnp.dot(
            own_main[n], lax.dynamic_slice_in_dim(outers[n], tok * cols, cols, 1), precision=PRECISE
        )
        norm_parts.append(jnp.sum(merged * merged, axis=0))
        cross_parts.append(
            lax.dot_general(own_main[n], merged, (((0,), (0,)), ((), ())), precision=PRECISE)
        )

    def by_matrix(blocks):
        pieces = []
        start = 0
        for n in range(7):
            cols = WIDTHS[n] // tok_count
            piece = blocks[..., start : start + cols]
            start = start + cols
            pieces.append(jnp.moveaxis(piece, 0, -2).reshape(piece.shape[1:-1] + (WIDTHS[n],)))
        return jnp.concatenate(pieces, axis=-1)

    norm_block = all_sum(jnp.concatenate(norm_parts)[None], ["wide"])
    col_norms = jnp.sqrt(by_matrix(all_blocks(norm_block, "tok"))[0])
    scales = magnitudes / col_norms
    cross_block = all_sum(jnp.concatenate(cross_parts, axis=1), ["wide"])
    cross = by_matrix(all_blocks(cross_block, "tok"))
    norm_slope = -magnitudes / (col_norms * col_norms * col_norms)

    first_main = all_blocks(adapt_main, "wide").reshape(D, 6 * RANK)
    first_down = all_blocks(adapt_down, "wide").reshape(wide_count, 4, part, RANK)
    low_main = first_main.astype(BF)

    def columns(array, n):
        return array[..., STARTS[n] : STARTS[n] + WIDTHS[n]]

    def hidden_part(array, quarter, axis=-1):
        shape = array.shape[:-1] + (wide_count, 4, part)
        picked = lax.dynamic_index_in_dim(
            array.reshape(shape), quarter, len(shape) - 2, keepdims=False
        )
        return picked.reshape(array.shape[:-1] + (block_cols,))

    quarters = [tok % 4, (tok % 4) ^ 1]
    halves = [core, 1 - core]

    qkv_cols = WIDTHS[0] + WIDTHS[1] + WIDTHS[2]
    qkv_half = qkv_cols // 2
    out_half = D // 2
    qkv_shard = lax.dynamic_slice_in_dim(
        jnp.concatenate([w_query, w_key, w_value], axis=1), core * qkv_half, qkv_half, 1
    )
    qkv_extra = lax.dynamic_slice_in_dim(extra_rows(outers[:3]), core * qkv_half, qkv_half, 1)
    qkv_weights = [gather_rows(qkv_shard, qkv_extra)]
    qkv_weights.append(other_core(qkv_weights[0]))
    out_shard = lax.dynamic_slice_in_dim(w_output, core * out_half, out_half, 1)
    out_extra = lax.dynamic_slice_in_dim(extra_rows(outers[3:4]), core * out_half, out_half, 1)
    out_weights = [gather_rows(out_shard, out_extra)]
    out_weights.append(other_core(out_weights[0]))
    down_shard = lax.dynamic_slice_in_dim(w_down, quarters[0] * part, part, 0)
    down_weights = [gather_rows(down_shard, extra_rows(outers[6:]))]
    down_weights.append(other_core(down_weights[0]))
    mlp_shard = jnp.concatenate(
        [hidden_part(w_gate, quarters[0]), hidden_part(w_up, quarters[0])], axis=1
    )
    mlp_extra = extra_rows([hidden_part(outers[4], quarters[0]), hidden_part(outers[5], quarters[0])])
    mlp_weights = [gather_rows(mlp_shard, mlp_extra)]
    mlp_weights.append(other_core(mlp_weights[0]))

    def in_order(blocks):
        return jnp.where(
            core == 0, jnp.concatenate(blocks, axis=1), jnp.concatenate(blocks[::-1], axis=1)
        )

    def half_of(array, side):
        width = array.shape[-1] // 2
        return lax.dynamic_slice_in_dim(array, side * width, width, array.ndim - 1)

    def norm_rows(values, gain_row):
        inverse = lax.rsqrt(jnp.mean(values * values, axis=1, keepdims=True) + EPS_NORM)
        return (values * inverse * gain_row[None, :]).astype(BF), inverse

    def norm_rows_back(values, gain_row, inverse, grad_normed):
        inner = jnp.sum(values * gain_row[None, :] * grad_normed, axis=1, keepdims=True)
        return (
            grad_normed * gain_row[None, :] * inverse
            - values * (inverse * inverse * inverse * inner / D)
        )

    own_places = (
        jnp.arange(CHUNKS, dtype=jnp.int32)[:, None] * (wide_count * block)
        + wide * block
        + jnp.arange(block, dtype=jnp.int32)[None, :]
    ).reshape(count)
    segment_row = segments[0]
    own_segment = lax.dynamic_index_in_dim(
        segment_row.reshape(CHUNKS, wide_count, block), wide, 1, keepdims=False
    ).reshape(count)
    own_starts = jnp.sum(
        (segment_row[None, :] < own_segment[:, None]).astype(jnp.int32), axis=1
    )
    frequency = ROPE_BASE ** (-2.0 * jnp.arange(HD // 2, dtype=F32) / HD)
    angles = (own_places - own_starts).astype(F32)[:, None] * frequency[None, :]
    cosine = jnp.tile(jnp.cos(angles), (1, 2))
    sine = jnp.tile(jnp.sin(angles), (1, 2))

    normed_one, inverse_one = norm_rows(residual, gains[0])
    reduced_qkv = mm(normed_one, low_main[:, : 3 * RANK])
    inputs_one = extended(normed_one, reduced_qkv)
    qkv_z = in_order([mm(inputs_one, weights) for weights in qkv_weights])
    qkv = qkv_z * scales[None, :qkv_cols]
    queries = turn(qkv[:, :D], cosine, sine).astype(BF)
    keys_low = turn(qkv[:, D : D + KVH * HD], cosine, sine).astype(BF)
    values_low = qkv[:, D + KVH * HD :].astype(BF)
    both = all_blocks(jnp.concatenate([keys_low, values_low], axis=1), "wide")
    both = jnp.swapaxes(both.reshape(wide_count, CHUNKS, block, -1), 0, 1).reshape(length, -1)
    all_keys, all_values = both[:, : KVH * HD], both[:, KVH * HD :]
    attended, log_total = attend(queries, all_keys, all_values, own_places, own_starts)
    reduced_out = mm(attended, low_main[:, 3 * RANK : 4 * RANK])
    inputs_out = extended(attended, reduced_out)
    output_z = in_order([mm(inputs_out, weights) for weights in out_weights])
    hidden_one = residual + output_z * columns(scales, 3)[None, :]

    normed_own, inverse_two = norm_rows(hidden_one, gains[1])
    normed_two = jnp.concatenate([normed_own, partner(normed_own)])
    reduced_mlp = mm(normed_two, low_main[:, 4 * RANK :])
    inputs_two = extended(normed_two, reduced_mlp)
    upstream = to_tokens(cotangent).astype(F32)
    down_low = (upstream * columns(scales, 6)[None, :]).astype(BF)
    down_low = jnp.concatenate([down_low, partner(down_low)])
    low_down = [
        lax.dynamic_index_in_dim(first_down, quarter, 1, keepdims=False)
        .reshape(block_cols, RANK)
        for quarter in quarters
    ]
    mlp_scales = []
    mlp_slopes = []
    mlp_outers = []
    for quarter in quarters:
        mlp_scales.append([hidden_part(columns(scales, n), quarter) for n in (4, 5)])
        mlp_slopes.append([hidden_part(columns(norm_slope, n), quarter) for n in (4, 5)])
        mlp_outers.append([hidden_part(outers[n], quarter) for n in (4, 5)])
    hiddens = []
    reduced_down = jnp.zeros((2 * count, RANK), F32)
    kept = []
    for k in range(2):
        z = mm(inputs_two, mlp_weights[k])
        gate_z, up_z = z[:, :block_cols], z[:, block_cols:]
        gate_act = gate_z * mlp_scales[k][0][None, :]
        up_act = up_z * mlp_scales[k][1][None, :]
        hidden = (jax.nn.silu(gate_act) * up_act).astype(BF)
        hiddens.append(hidden)
        kept.append((gate_z, up_z, gate_act, up_act))
        reduced_down = reduced_down + mm(hidden, low_down[k].astype(BF))
    down_sum = mm(extended(hiddens[0], reduced_down), down_weights[0]) + mm(
        hiddens[1], down_weights[1][:block_cols]
    )
    down_z = down_sum[:count] + partner(down_sum[count:].astype(BF)).astype(F32)
    layer_out = from_tokens((hidden_one + down_z * columns(scales, 6)[None, :]).astype(BF))

    scale_down = jnp.sum(upstream * down_z, axis=0)
    narrow_mlp = jnp.zeros((2 * count, 2 * RANK), F32)
    grad_normed = jnp.zeros((2 * count, D), F32)
    first_mlp = jnp.zeros((2 * RANK, D), F32)
    mid_mlp = [jnp.zeros((RANK, RANK), F32) for _ in range(2)]
    outer_mlp = []
    scale_mlp = []
    first_down_parts = []
    reduced_mlp_parts = jnp.concatenate(two_parts(reduced_mlp), axis=1)
    for k in range(2):
        gate_z, up_z, gate_act, up_act = kept[k]
        through = mm_t(down_low, down_weights[k])
        narrow_down = through[:, block_cols : block_cols + RANK]
        narrow_parts = jnp.concatenate(two_parts(narrow_down), axis=1)
        low_twice = jnp.concatenate([low_down[k].astype(BF)] * 2, axis=1)
        grad_hidden = through[:, :block_cols] + mm_t(narrow_parts, low_twice)
        first_down_parts.append(fold_parts(t_mm(narrow_parts, hiddens[k]), RANK))
        gate_sigmoid = jax.nn.sigmoid(gate_act)
        grad_up = grad_hidden * gate_act * gate_sigmoid
        grad_gate = grad_hidden * up_act * gate_sigmoid * (1.0 + gate_act * (1.0 - gate_sigmoid))
        scale_pair = [jnp.sum(grad_gate * gate_z, axis=0), jnp.sum(grad_up * up_z, axis=0)]
        scale_mlp.append(scale_pair)
        mlp_low = jnp.concatenate(
            [
                (grad_gate * mlp_scales[k][0][None, :]).astype(BF),
                (grad_up * mlp_scales[k][1][None, :]).astype(BF),
            ],
            axis=1,
        )
        weighted = [
            (scale_pair[i] * mlp_slopes[k][i])[None, :] * mlp_outers[k][i] for i in range(2)
        ]
        back = stacked_back(mlp_low, block_rows(weighted), mlp_weights[k])
        grad_normed = grad_normed + back[: 2 * count, :D]
        narrow_mlp = narrow_mlp + back[: 2 * count, D : D + 2 * RANK]
        first_mlp = first_mlp + fold_parts(back[2 * count :, :D], 2 * RANK)
        mid_mlp = [
            mid_mlp[i]
            + lax.dot_general(
                weighted[i], mlp_outers[k][i], (((1,), (1,)), ((), ())), precision=PRECISE
            )
            for i in range(2)
        ]
        pair_grads = 2.0 * fold_parts(t_mm(reduced_mlp_parts, mlp_low), 2 * RANK)
        outer_mlp.append([pair_grads[:RANK, :block_cols], pair_grads[RANK:, block_cols:]])
    narrow_parts = jnp.concatenate(two_parts(narrow_mlp), axis=1)
    low_twice = jnp.concatenate([low_main[:, 4 * RANK :]] * 2, axis=1)
    grad_normed = grad_normed + mm_t(narrow_parts, low_twice)
    first_mlp_product = fold_parts(t_mm(narrow_parts, normed_two), 2 * RANK)
    grad_normed = grad_normed[:count] + partner(grad_normed[count:].astype(BF)).astype(F32)
    grad_mid = upstream + norm_rows_back(hidden_one, gains[1], inverse_two, grad_normed)

    def first_term(product, weight_term, middles, first_cols):
        mids = jnp.concatenate(
            [
                jnp.dot(middle, first.T, precision=PRECISE)
                for middle, first in zip(middles, first_cols)
            ]
        )
        return product + 2.0 * (weight_term + 2.0 * mids)

    def main_cols(n):
        return first_main[:, n * RANK : (n + 1) * RANK]

    first_grad_mlp = first_term(
        first_mlp_product, first_mlp, mid_mlp, [main_cols(4), main_cols(5)]
    )

    pair_down = scale_down + partner(scale_down[None])[0]
    weighted = (pair_down * columns(norm_slope, 6))[None, :] * outers[6]
    middle = lax.dot_general(weighted, outers[6], (((1,), (1,)), ((), ())), precision=PRECISE)
    weighted_parts = jnp.concatenate(two_parts(weighted))
    first_grad_down = []
    for k in range(2):
        term = fold_parts(mm_t(weighted_parts, down_weights[k])[:, :block_cols], RANK)
        first_grad_down.append(
            first_term(first_down_parts[k], term, [middle], [low_down[k]])
        )
    outer_down = 2.0 * fold_parts(
        t_mm(jnp.concatenate(two_parts(reduced_down), axis=1), down_low), RANK
    )

    scale_out = jnp.sum(grad_mid * output_z, axis=0)
    out_low = (grad_mid * columns(scales, 3)[None, :]).astype(BF)
    weighted = (scale_out * columns(norm_slope, 3))[None, :] * outers[3]
    middle = lax.dot_general(weighted, outers[3], (((1,), (1,)), ((), ())), precision=PRECISE)
    back = sum(
        stacked_back(half_of(out_low, halves[k]), half_of(weighted, halves[k]), out_weights[k])
        for k in range(2)
    )
    narrow_parts = jnp.concatenate(two_parts(back[:count, D : D + RANK]), axis=1)
    low_twice = jnp.concatenate([low_main[:, 3 * RANK : 4 * RANK]] * 2, axis=1)
    grad_mixed = (back[:count, :D] + mm_t(narrow_parts, low_twice)).astype(BF)
    first_grad_out = first_term(
        fold_parts(t_mm(narrow_parts, attended), RANK),
        fold_parts(back[count:, :D], RANK),
        [middle],
        [main_cols(3)],
    )
    outer_out = 2.0 * fold_parts(
        t_mm(jnp.concatenate(two_parts(reduced_out), axis=1), out_low), RANK
    )

    grad_queries, grad_keys, grad_values = attend_back(
        queries, all_keys, all_values, own_places, own_starts, log_total, attended, grad_mixed
    )
    partial = jnp.concatenate([grad_keys, grad_values], axis=1)
    partial = jnp.swapaxes(partial.reshape(CHUNKS, wide_count, block, -1), 0, 1)
    partial = scatter_sum(partial.reshape(wide_count, count, -1), "wide", BF)
    query_grad = turn(grad_queries, cosine, -sine)
    key_grad = turn(partial[:, : KVH * HD], cosine, -sine)
    value_grad = partial[:, KVH * HD :]
    qkv_grad = jnp.concatenate([query_grad, key_grad, value_grad], axis=1)
    scale_qkv = jnp.sum(qkv_grad * qkv_z, axis=0)
    qkv_low = (qkv_grad * scales[None, :qkv_cols]).astype(BF)
    qkv_outers = outers[:3]
    weighted = [
        (columns(scale_qkv, n) * columns(norm_slope, n))[None, :] * outers[n] for n in range(3)
    ]
    middles = [
        lax.dot_general(weighted[n], outers[n], (((1,), (1,)), ((), ())), precision=PRECISE)
        for n in range(3)
    ]
    weighted_rows = block_rows(weighted)
    back = sum(
        stacked_back(half_of(qkv_low, halves[k]), half_of(weighted_rows, halves[k]), qkv_weights[k])
        for k in range(2)
    )
    narrow_parts = jnp.concatenate(two_parts(back[:count, D : D + 3 * RANK]), axis=1)
    low_twice = jnp.concatenate([low_main[:, : 3 * RANK]] * 2, axis=1)
    grad_normed = back[:count, :D] + mm_t(narrow_parts, low_twice)
    first_grad_qkv = first_term(
        fold_parts(t_mm(narrow_parts, normed_one), 3 * RANK),
        fold_parts(back[count:, :D], 3 * RANK),
        middles,
        [main_cols(n) for n in range(3)],
    )
    all_outer = 2.0 * fold_parts(
        t_mm(jnp.concatenate(two_parts(reduced_qkv), axis=1), qkv_low), 3 * RANK
    )
    outer_qkv = [
        columns(all_outer, n)[n * RANK : (n + 1) * RANK] for n in range(3)
    ]
    grad_tokens = from_tokens(
        (grad_mid + norm_rows_back(residual, gains[0], inverse_one, grad_normed)).astype(BF)
    )

    def spread_hidden(pair):
        rows = pair[0].shape[0]
        whole = jnp.zeros((rows, wide_count, 4, part), F32)
        for quarter, values in zip(quarters, pair):
            whole = lax.dynamic_update_slice(
                whole, values.reshape(rows, wide_count, 1, part), (0, 0, quarter, 0)
            )
        return whole.reshape(rows, FF)

    main_rows = jnp.concatenate([first_grad_qkv, first_grad_out, first_grad_mlp])
    down_rows = spread_hidden(first_grad_down)
    outer_cols = jnp.concatenate(
        outer_qkv
        + [
            outer_out,
            spread_hidden([outer_mlp[k][0] for k in range(2)]),
            spread_hidden([outer_mlp[k][1] for k in range(2)]),
            outer_down,
        ],
        axis=1,
    )
    scale_all = jnp.concatenate(
        [
            scale_qkv,
            scale_out,
            spread_hidden([scale_mlp[k][0][None] for k in range(2)])[0],
            spread_hidden([scale_mlp[k][1][None] for k in range(2)])[0],
            scale_down,
        ]
    )
    outer_cols = outer_cols + 2.0 * (scale_all * norm_slope)[None, :] * cross
    outer_cols = jnp.concatenate([outer_cols, scale_all[None]])

    main_width = 6 * RANK // tok_count
    down_width = RANK // tok_count
    outer_share = OUTS // (tok_count * wide_count)

    def to_owner(rows, tok_rows, wide_cols):
        shaped = rows.reshape(tok_count, tok_rows, wide_count, wide_cols)
        summed = scatter_sum(shaped, "tok")
        return scatter_sum(jnp.swapaxes(summed, 0, 1), "wide")

    main_part = to_owner(main_rows, main_width, share).T
    down_part = to_owner(down_rows, down_width, hidden_share).T
    outer_blocks = jnp.moveaxis(
        outer_cols.reshape(RANK + 1, tok_count, wide_count, outer_share), 0, 2
    )
    outer_sum = scatter_sum(scatter_sum(outer_blocks, "tok"), "wide")
    outer_part = outer_sum[:RANK]
    block_start = (tok * wide_count + wide) * outer_share
    mag_part = outer_sum[RANK] / lax.dynamic_slice_in_dim(col_norms, block_start, outer_share)

    local_squares = (
        squared_sum(main_part)
        + squared_sum(down_part)
        + squared_sum(outer_part)
        + squared_sum(mag_part)
    )
    grad_total = all_sum(jnp.full((8, 128), local_squares), ["tok", "wide"])[0, 0]
    grad_norm = jnp.sqrt(grad_total)
    clip_factor = CLIP_MAX / jnp.maximum(grad_norm, CLIP_MAX)
    main_param = lax.dynamic_slice_in_dim(adapt_main, tok * main_width, main_width, 1)
    down_param = lax.dynamic_slice_in_dim(adapt_down, tok * down_width, down_width, 1)
    outer_param = lax.dynamic_slice_in_dim(adapt_outer, block_start, outer_share, 1)
    mag_param = lax.dynamic_slice_in_dim(magnitudes, block_start, outer_share, 0)
    main_new, main_first_new, main_second_new = adam(
        main_param, main_part, main_first, main_second, RATE_ADAPT, clip_factor
    )
    down_new, down_first_new, down_second_new = adam(
        down_param, down_part, down_first, down_second, RATE_ADAPT, clip_factor
    )
    outer_new, outer_first_new, outer_second_new = adam(
        outer_param, outer_part, outer_first, outer_second, RATE_OUTER, clip_factor
    )
    mag_new, mag_first_new, mag_second_new = adam(
        mag_param, mag_part, mag_first, mag_second, RATE_MAGNITUDE, clip_factor
    )
    mag_clipped = mag_part * clip_factor
    return (
        layer_out,
        grad_tokens,
        grad_norm,
        main_new,
        main_first_new,
        main_second_new,
        down_new,
        down_first_new,
        down_second_new,
        outer_new,
        outer_first_new,
        outer_second_new,
        mag_new,
        mag_clipped,
        mag_second_new,
    )


def solution(mesh):
    return jax.shard_map(
        shards,
        mesh=mesh,
        in_specs=(
            P("tok", "wide"),
            P("tok", "wide"),
            P("wide"),
            P("wide"),
            P("wide", None),
            P("wide", None),
            P("wide", None),
            P("wide", None),
            P("wide", None),
            P("wide", None),
            P("wide", None),
            P("wide", None),
            P("wide", None),
            P(),
            P(),
            P("wide", "tok"),
            P("wide", "tok"),
            P("wide", "tok"),
            P("wide", "tok"),
            P(None, ("tok", "wide")),
            P(None, ("tok", "wide")),
            P(("tok", "wide")),
            P(("tok", "wide")),
            P("tok", None),
        ),
        out_specs=(
            P("tok", "wide"),
            P("tok", "wide"),
            P(),
            P("wide", "tok"),
            P("wide", "tok"),
            P("wide", "tok"),
            P("wide", "tok"),
            P("wide", "tok"),
            P("wide", "tok"),
            P(None, ("tok", "wide")),
            P(None, ("tok", "wide")),
            P(None, ("tok", "wide")),
            P(("tok", "wide")),
            P(("tok", "wide")),
            P(("tok", "wide")),
        ),
        check_vma=False,
    )
```

```python
import functools

import jax
import jax.numpy as jnp
from jax import lax
from jax.experimental import pallas as pl
from jax.experimental.pallas import tpu as pltpu
from jax.sharding import PartitionSpec as P

D = 2048
HEADS = 32
HD = 64
KVH = 4
FF = 5632
STEP = 10
RANK = 16
CHUNKS = 8
EXTRA = 128
COST = 1 << 10

EPS_NORM = 1e-05
ROPE_BASE = 10000.0
CLIP_MAX = 1.0
BETA_FIRST = 0.9
BETA_SECOND = 0.999
ADAM_EPS = 1e-08
WEIGHT_DECAY = 0.01
RATE_ADAPT = 0.02
RATE_OUTER = 0.05
RATE_MAGNITUDE = 0.4
PRECISE = lax.Precision.HIGHEST
MASKED = -1e30
NT = (((1,), (1,)), ((), ()))
GROUP = HEADS // KVH
FWD = 4
BWD = 4
BF = jnp.bfloat16
F32 = jnp.float32
WIDTHS = [D, KVH * HD, KVH * HD, D, FF, FF, D]
STARTS = [sum(WIDTHS[:number]) for number in range(7)]
OUTS = sum(WIDTHS)


def bits_of(count):
    return [1 << place for place in range(count.bit_length() - 1)]


def swap(array, axis, distance):
    count = lax.axis_size(axis)
    return lax.ppermute(array, axis, [(i, i ^ distance) for i in range(count)])


def mm(left, right):
    return jnp.dot(left, right, preferred_element_type=F32)


def mm_t(left, right):
    return lax.dot_general(left, right, (((1,), (1,)), ((), ())), preferred_element_type=F32)


def t_mm(left, right):
    return lax.dot_general(left, right, (((0,), (0,)), ((), ())), preferred_element_type=F32)


def two_parts(values):
    high = lax.reduce_precision(values, 8, 7)
    return high.astype(BF), (values - high).astype(BF)


def fold_parts(stacked, count):
    return stacked[:count] + stacked[count : 2 * count]


def adam(param, grad, first, second, rate, clip_factor):
    clipped = grad * clip_factor
    first_new = BETA_FIRST * first + (1.0 - BETA_FIRST) * clipped
    second_new = BETA_SECOND * second + (1.0 - BETA_SECOND) * clipped * clipped
    first_hat = first_new / (1.0 - BETA_FIRST**STEP)
    second_hat = second_new / (1.0 - BETA_SECOND**STEP)
    param_new = param - rate * (
        first_hat / (jnp.sqrt(second_hat) + ADAM_EPS) + WEIGHT_DECAY * param
    )
    return (param_new, first_new, second_new)


def squared_sum(values):
    return jnp.sum(values * values)


def all_sum(values, axes):
    for axis in axes:
        for bit in bits_of(lax.axis_size(axis)):
            values = values + swap(values, axis, bit)
    return values


def all_blocks(block, axis):
    stacked = block[None]
    index = lax.axis_index(axis)
    for bit in bits_of(lax.axis_size(axis)):
        upper = (index // bit) % 2 == 1
        received = swap(stacked, axis, bit)
        stacked = jnp.concatenate(
            [jnp.where(upper, received, stacked), jnp.where(upper, stacked, received)]
        )
    return stacked


def scatter_sum(blocks, axis, wire=F32, order=None):
    index = lax.axis_index(axis)
    bits = bits_of(lax.axis_size(axis))
    shape = blocks.shape[1:]
    left = list(reversed(bits))
    blocks = blocks.reshape((2,) * len(bits) + shape)
    for bit in order or bits:
        dim = left.index(bit)
        side = (index // bit) % 2
        keep = lax.dynamic_index_in_dim(blocks, side, dim, keepdims=False)
        send = lax.dynamic_index_in_dim(blocks, 1 - side, dim, keepdims=False)
        blocks = keep + swap(send.astype(wire), axis, bit).astype(blocks.dtype)
        left.remove(bit)
    return blocks


def after(value, *others):
    return lax.optimization_barrier((value,) + others)[0]


def gather_slots(shard, turned=False):
    slots = {0: shard}
    count = lax.axis_size("wide")
    for slot in sorted(range(1, count), key=lambda i: bin(i).count("1")):
        low = slot & -slot
        if turned and slot == count - 1:
            low = count // 4
        slots[slot] = swap(slots[slot ^ low], "wide", low)
    return slots


def near(slots):
    return [held for slot, held in slots.items() if bin(slot).count("1") == 1]


def put_rows(slots, extra):
    count = lax.axis_size("wide")
    index = lax.axis_index("wide")
    rows, cols = slots[0].shape
    whole = jnp.zeros((count * rows + extra.shape[0], cols), extra.dtype)
    whole = lax.dynamic_update_slice(whole, extra, (count * rows, 0))
    for slot, held in slots.items():
        whole = lax.dynamic_update_slice(whole, held, ((index ^ slot) * rows, 0))
    return whole


def rotate_half(values):
    half = HD // 2
    return jnp.concatenate([values[..., half:], values[..., :half]], axis=-1)


def turn(values, cosine, sine):
    shaped = values.reshape(values.shape[0], -1, HD)
    turned = shaped * cosine[:, None, :] + rotate_half(shaped) * sine[:, None, :]
    return turned.reshape(values.shape)


def pad_rows(rows, count):
    return jnp.concatenate([rows, jnp.zeros((count - rows.shape[0], rows.shape[1]), rows.dtype)])


def lanes_of(reduced):
    high, low = two_parts(reduced)
    return jnp.pad(
        jnp.concatenate([high, low], axis=1), ((0, 0), (0, EXTRA - 2 * reduced.shape[1]))
    )


def twice_low(rows):
    doubled = 2.0 * rows.astype(BF)
    return pad_rows(jnp.concatenate([doubled, doubled]), EXTRA)


def gram_of(left, right):
    return lax.dot_general(left, right, (((1,), (1,)), ((), ())), precision=PRECISE)


def turn_lanes(values, cosine, sine):
    lane = lax.broadcasted_iota(jnp.int32, values.shape, 1) % HD
    swapped = jnp.where(
        lane < HD // 2,
        pltpu.roll(values, 2 * HD - HD // 2, 1),
        pltpu.roll(values, HD // 2, 1),
    )
    return values * cosine + swapped * sine


def head_rows(pairs, low_side):
    rows = []
    for pair in pairs:
        lane = lax.broadcasted_iota(jnp.int32, pair.shape, 1)
        moved = pltpu.roll(pair, HD, 1)
        if low_side:
            rows.append(jnp.where(lane < HD, pair, 0.0))
            rows.append(jnp.where(lane < HD, moved, 0.0))
        else:
            rows.append(jnp.where(lane >= HD, moved, 0.0))
            rows.append(jnp.where(lane >= HD, pair, 0.0))
    return jnp.concatenate(rows, axis=0).astype(BF)


def pairs_of(columns, block):
    turned = jnp.concatenate([columns, columns], axis=0).T
    lane = lax.broadcasted_iota(jnp.int32, (block, 2 * HD), 1)
    out = []
    for pair in range(GROUP // 2):
        first = turned[2 * pair * block : (2 * pair + 1) * block]
        second = turned[(2 * pair + 1) * block : (2 * pair + 2) * block]
        out.append(jnp.where(lane < HD, first, second))
    return out


def forward_kernel(
    first_ref, z_ref, scale_ref, cos_ref, sin_ref, place_ref, start_ref, kv_ref, kvt_ref,
    query_ref, out_ref, log_ref, *, block, span, groups,
):
    rows = GROUP * block
    width = GROUP * HD

    def chunk_body(chunk, carry):
        at = pl.ds(pl.multiple_of(chunk * block, block), block)
        cosine = cos_ref[at, :]
        sine = sin_ref[at, :]
        query_rows = []
        for group in range(groups):
            pairs = []
            for pair in range(GROUP // 2):
                lanes = slice(group * width + pair * 2 * HD, group * width + (pair + 1) * 2 * HD)
                turned = turn_lanes(z_ref[at, lanes] * scale_ref[:, lanes], cosine, sine)
                low = turned.astype(BF)
                query_ref[at, lanes] = low
                pairs.append(low.astype(F32) * HD**-0.5)
            query_rows.append(head_rows(pairs, True))
        place = place_ref[chunk]
        start = start_ref[chunk]

        def key_body(step, state):
            key_block = chunk - step
            keys = pl.ds(pl.multiple_of(key_block * span, span), span)
            spot = key_block * span + lax.broadcasted_iota(jnp.int32, (span, rows), 0)
            allowed = (spot <= place) & (spot >= start)
            out = []
            all_scores = [
                lax.dot_general(
                    kv_ref[keys, group * 2 * HD : (group + 1) * 2 * HD], query_rows[group], NT, preferred_element_type=F32
                )
                for group in range(groups)
            ]
            for group in range(groups):
                peak, total, mixed = state[group]
                scores = jnp.where(allowed, all_scores[group], MASKED)
                peak_new = jnp.maximum(peak, jnp.max(scores, axis=0, keepdims=True))
                powers = jnp.exp(scores - peak_new)
                shrink = jnp.exp(peak - peak_new)
                total = total * shrink + jnp.sum(powers, axis=0, keepdims=True)
                mixed = mixed * shrink + jnp.dot(
                    kvt_ref[group, HD:, keys], powers.astype(BF), preferred_element_type=F32
                )
                out.append((peak_new, total, mixed))
            return tuple(out)

        start_state = tuple(
            (
                jnp.full((1, rows), MASKED, F32),
                jnp.zeros((1, rows), F32),
                jnp.zeros((HD, rows), F32),
            )
            for _ in range(groups)
        )
        state = lax.fori_loop(0, chunk + 1 - first_ref[chunk], key_body, start_state)
        for group in range(groups):
            peak, total, mixed = state[group]
            log_ref[group, chunk] = peak + jnp.log(total)
            for pair, value in enumerate(pairs_of(mixed / total, block)):
                low_lane = group * width + pair * 2 * HD
                out_ref[at, low_lane : low_lane + 2 * HD] = value.astype(BF)
        return carry

    lax.fori_loop(0, CHUNKS, chunk_body, 0)


def backward_kernel(
    first_ref, query_ref, cos_ref, sin_ref, place_ref, start_ref, kv_ref, kvt_ref, log_ref,
    out_ref, grad_ref, query_grad_ref, kv_grad_ref, sums, *, block, span, groups,
):
    rows = GROUP * block
    width = GROUP * HD
    sums[...] = jnp.zeros_like(sums)

    def chunk_body(chunk, carry):
        at = pl.ds(pl.multiple_of(chunk * block, block), block)
        tiles = []
        for group in range(groups):
            queries = []
            grads = []
            product_rows = []
            for pair in range(GROUP // 2):
                lanes = slice(group * width + pair * 2 * HD, group * width + (pair + 1) * 2 * HD)
                queries.append(query_ref[at, lanes].astype(F32) * HD**-0.5)
                grad = grad_ref[at, lanes].astype(F32)
                grads.append(grad)
                product = grad * out_ref[at, lanes].astype(F32)
                lane = lax.broadcasted_iota(jnp.int32, product.shape, 1)
                product_rows.append(jnp.where(lane < HD, product, 0.0))
                product_rows.append(jnp.where(lane >= HD, product, 0.0))
            inner = jnp.sum(jnp.concatenate(product_rows, axis=0).T, axis=0, keepdims=True)
            query_rows = head_rows(queries, True)
            grad_rows = head_rows(grads, False)
            tiles.append((query_rows, grad_rows, inner, log_ref[group, chunk]))
        place = place_ref[chunk]
        start = start_ref[chunk]

        def key_body(key_block, query_grads):
            keys = pl.ds(pl.multiple_of(key_block * span, span), span)
            spot = key_block * span + lax.broadcasted_iota(jnp.int32, (span, rows), 0)
            allowed = (spot <= place) & (spot >= start)
            out = []
            products = []
            for group in range(groups):
                query_rows, grad_rows, inner, log_total = tiles[group]
                kv = kv_ref[keys, group * 2 * HD : (group + 1) * 2 * HD]
                products.append(
                    (
                        lax.dot_general(kv, query_rows, NT, preferred_element_type=F32),
                        lax.dot_general(kv, grad_rows, NT, preferred_element_type=F32),
                    )
                )
            for group in range(groups):
                query_rows, grad_rows, inner, log_total = tiles[group]
                scores, grad_weights = products[group]
                weights = jnp.exp(jnp.where(allowed, scores - log_total, MASKED))
                grad_scores = (weights * (grad_weights - inner)).astype(BF)
                sums[group, keys, :] += jnp.dot(
                    grad_scores, query_rows, preferred_element_type=F32
                ) + jnp.dot(weights.astype(BF), grad_rows, preferred_element_type=F32)
                out.append(
                    query_grads[group]
                    + jnp.dot(kvt_ref[group, :HD, keys], grad_scores, preferred_element_type=F32)
                )
            return tuple(out)

        query_grads = lax.fori_loop(
            first_ref[chunk],
            chunk + 1,
            key_body,
            tuple(jnp.zeros((HD, rows), F32) for _ in range(groups)),
        )
        cosine = cos_ref[at, :]
        sine = sin_ref[at, :]
        for group in range(groups):
            for pair, value in enumerate(pairs_of(query_grads[group] * HD**-0.5, block)):
                low_lane = group * width + pair * 2 * HD
                query_grad_ref[at, low_lane : low_lane + 2 * HD] = turn_lanes(
                    value, cosine, -sine
                )
        return carry

    lax.fori_loop(0, CHUNKS, chunk_body, 0)
    for group in range(groups):
        kv_grad_ref[:, group * 2 * HD : (group + 1) * 2 * HD] = sums[group].astype(BF)


def attend(first_block, z, scale, cosine, sine, places, starts, kv, kvt):
    count = z.shape[0]
    block = count // CHUNKS
    length = kv.shape[0]
    span = length // CHUNKS
    rows = GROUP * block
    width = FWD * GROUP * HD
    grid_spec = pltpu.PrefetchScalarGridSpec(
        num_scalar_prefetch=1,
        grid=(KVH // FWD,),
        in_specs=[
            pl.BlockSpec((count, width), lambda g, s: (0, g)),
            pl.BlockSpec((1, width), lambda g, s: (0, g)),
            pl.BlockSpec((count, 2 * HD), lambda g, s: (0, 0)),
            pl.BlockSpec((count, 2 * HD), lambda g, s: (0, 0)),
            pl.BlockSpec((CHUNKS, 1, rows), lambda g, s: (0, 0, 0)),
            pl.BlockSpec((CHUNKS, 1, rows), lambda g, s: (0, 0, 0)),
            pl.BlockSpec((length, FWD * 2 * HD), lambda g, s: (0, g)),
            pl.BlockSpec((FWD, 2 * HD, length), lambda g, s: (g, 0, 0)),
        ],
        out_specs=[
            pl.BlockSpec((count, width), lambda g, s: (0, g)),
            pl.BlockSpec((count, width), lambda g, s: (0, g)),
            pl.BlockSpec((FWD, CHUNKS, 1, rows), lambda g, s: (g, 0, 0, 0)),
        ],
    )
    return pl.pallas_call(
        functools.partial(forward_kernel, block=block, span=span, groups=FWD),
        grid_spec=grid_spec,
        out_shape=[
            jax.ShapeDtypeStruct((count, HEADS * HD), BF),
            jax.ShapeDtypeStruct((count, HEADS * HD), BF),
            jax.ShapeDtypeStruct((KVH, CHUNKS, 1, rows), F32),
        ],
        compiler_params=pltpu.CompilerParams(vmem_limit_bytes=40 << 20),
        cost_estimate=pl.CostEstimate(flops=COST, bytes_accessed=COST, transcendentals=0),
    )(first_block, z, scale, cosine, sine, places, starts, kv, kvt)


def attend_back(
    first_block, queries, cosine, sine, places, starts, kv, kvt, log_total, attended, grads
):
    count = queries.shape[0]
    block = count // CHUNKS
    length = kv.shape[0]
    span = length // CHUNKS
    rows = GROUP * block
    width = BWD * GROUP * HD
    grid_spec = pltpu.PrefetchScalarGridSpec(
        num_scalar_prefetch=1,
        grid=(KVH // BWD,),
        in_specs=[
            pl.BlockSpec((count, width), lambda g, s: (0, g)),
            pl.BlockSpec((count, 2 * HD), lambda g, s: (0, 0)),
            pl.BlockSpec((count, 2 * HD), lambda g, s: (0, 0)),
            pl.BlockSpec((CHUNKS, 1, rows), lambda g, s: (0, 0, 0)),
            pl.BlockSpec((CHUNKS, 1, rows), lambda g, s: (0, 0, 0)),
            pl.BlockSpec((length, BWD * 2 * HD), lambda g, s: (0, g)),
            pl.BlockSpec((BWD, 2 * HD, length), lambda g, s: (g, 0, 0)),
            pl.BlockSpec((BWD, CHUNKS, 1, rows), lambda g, s: (g, 0, 0, 0)),
            pl.BlockSpec((count, width), lambda g, s: (0, g)),
            pl.BlockSpec((count, width), lambda g, s: (0, g)),
        ],
        out_specs=[
            pl.BlockSpec((count, width), lambda g, s: (0, g)),
            pl.BlockSpec((length, BWD * 2 * HD), lambda g, s: (0, g)),
        ],
        scratch_shapes=[pltpu.VMEM((BWD, length, 2 * HD), F32)],
    )
    return pl.pallas_call(
        functools.partial(backward_kernel, block=block, span=span, groups=BWD),
        grid_spec=grid_spec,
        out_shape=[
            jax.ShapeDtypeStruct((count, HEADS * HD), F32),
            jax.ShapeDtypeStruct((length, KVH * 2 * HD), BF),
        ],
        compiler_params=pltpu.CompilerParams(vmem_limit_bytes=40 << 20),
        cost_estimate=pl.CostEstimate(flops=COST, bytes_accessed=COST, transcendentals=0),
    )(first_block, queries, cosine, sine, places, starts, kv, kvt, log_total, attended, grads)


def place_of(place_ref, slot, rows):
    return pl.multiple_of((place_ref[0] ^ slot) * rows, rows)


def half_place(place_ref, half, tiles, pair_tiles):
    return (place_ref[1] ^ half) * pair_tiles + tiles


def set_rows(outer, offset):
    rank, cols = outer.shape
    parts = [outer]
    if offset:
        parts = [jnp.zeros((offset, cols), outer.dtype)] + parts
    if EXTRA - rank - offset:
        parts = parts + [jnp.zeros((EXTRA - rank - offset, cols), outer.dtype)]
    return jnp.concatenate(parts, axis=0)


def split_parts(values):
    high = values.astype(BF)
    return high, (values - high.astype(F32)).astype(BF)


def low_rank(reduced, outer, offset):
    high, low = split_parts(reduced)
    rows = set_rows(2.0 * outer.astype(BF).astype(F32), offset).astype(BF)
    return jnp.dot(high, rows, preferred_element_type=F32) + jnp.dot(
        low, rows, preferred_element_type=F32
    )


def slot_kernel(place_ref, inputs_ref, first_ref, outer_ref, *refs, offset):
    slots, out_ref, reduced_ref = refs[:-2], refs[-2], refs[-1]
    each = len(slots) // 2
    rows = slots[0].shape[0]

    @pl.when((pl.program_id(0) == 0) & (pl.program_id(1) == 0))
    def _():
        reduced_ref[...] = jnp.dot(inputs_ref[...], first_ref[...], preferred_element_type=F32)

    def total(chosen):
        result = low_rank(reduced_ref[...], outer_ref[...], offset)
        for slot, ref in enumerate(chosen):
            result = result + jnp.dot(
                inputs_ref[:, pl.ds(place_of(place_ref, slot, rows), rows)],
                ref[...],
                preferred_element_type=F32,
            )
        out_ref[...] = result

    for half in range(2):

        @pl.when(pl.program_id(0) == half)
        def _():
            total(slots[half * each : (half + 1) * each])


def slot_mm(place, inputs, first, outer, offset, slots, tile=256):
    rows = slots[0][0].shape[0]
    cols = outer.shape[1]
    tiles = cols // 2 // tile

    def held(half):
        def spot(h, n, s):
            return (0, jnp.where(h == half, n, (tiles - 1) * (1 - half)))

        return pl.BlockSpec((rows, tile), spot)

    return pl.pallas_call(
        functools.partial(slot_kernel, offset=offset),
        grid_spec=pltpu.PrefetchScalarGridSpec(
            num_scalar_prefetch=1,
            grid=(2, tiles),
            in_specs=[
                pl.BlockSpec(inputs.shape, lambda h, n, s: (0, 0)),
                pl.BlockSpec(first.shape, lambda h, n, s: (0, 0)),
                pl.BlockSpec(
                    (outer.shape[0], tile), lambda h, n, s: (0, half_place(s, h, n, tiles))
                ),
            ]
            + [held(half) for half in range(2) for _ in slots[half]],
            out_specs=[
                pl.BlockSpec(
                    (inputs.shape[0], tile), lambda h, n, s: (0, half_place(s, h, n, tiles))
                ),
                pl.BlockSpec((inputs.shape[0], EXTRA), lambda h, n, s: (0, 0)),
            ],
        ),
        out_shape=[
            jax.ShapeDtypeStruct((inputs.shape[0], cols), F32),
            jax.ShapeDtypeStruct((inputs.shape[0], EXTRA), F32),
        ],
        compiler_params=pltpu.CompilerParams(vmem_limit_bytes=40 << 20),
        cost_estimate=pl.CostEstimate(flops=COST, bytes_accessed=COST, transcendentals=0),
    )(place, inputs, first, outer, *slots[0], *slots[1])


def finish_kernel(*refs, count, sizes, offset, summed):
    raws = refs[: len(sizes)]
    narrow_ref, middle_ref, first_ref, inputs_ref, grad_ref, out_ref = refs[len(sizes) :]
    first = first_ref[...]
    narrow_high, narrow_low = split_parts(narrow_ref[...])
    total = lax.dot_general(narrow_high, first, NT, preferred_element_type=F32)
    total = total + lax.dot_general(narrow_low, first, NT, preferred_element_type=F32)
    weighted = []
    for ref, size in zip(raws, sizes):
        total = total + ref[:count, :]
        weighted.append(ref[count : count + size, :] + ref[count + size :, :])
    grad_ref[...] = total
    weighted = sum(weighted) if summed else jnp.concatenate(weighted, axis=0)
    middle_high, middle_low = split_parts(middle_ref[...])
    middle = lax.dot_general(middle_high, first, NT, preferred_element_type=F32)
    middle = middle + lax.dot_general(middle_low, first, NT, preferred_element_type=F32)
    under = (((0,), (0,)), ((), ()))
    inputs = inputs_ref[...]
    product = lax.dot_general(narrow_high, inputs, under, preferred_element_type=F32)
    product = product + lax.dot_general(narrow_low, inputs, under, preferred_element_type=F32)
    out_ref[...] = (
        product[offset : offset + weighted.shape[0]] + 2.0 * (weighted + 2.0 * middle)
    )


def finish_back(raws, sizes, narrow, middle, first, inputs, offset, summed=False, tile=512):
    count = inputs.shape[0]
    rank = middle.shape[0]
    tiled = lambda rows: pl.BlockSpec((rows, tile), lambda n: (0, n))
    return pl.pallas_call(
        functools.partial(
            finish_kernel, count=count, sizes=sizes, offset=offset, summed=summed
        ),
        grid=(D // tile,),
        in_specs=[tiled(raw.shape[0]) for raw in raws]
        + [
            pl.BlockSpec(narrow.shape, lambda n: (0, 0)),
            pl.BlockSpec(middle.shape, lambda n: (0, 0)),
            pl.BlockSpec((tile, EXTRA), lambda n: (n, 0)),
            tiled(count),
        ],
        out_specs=[tiled(count), tiled(rank)],
        out_shape=[
            jax.ShapeDtypeStruct((count, D), F32),
            jax.ShapeDtypeStruct((rank, D), F32),
        ],
        compiler_params=pltpu.CompilerParams(vmem_limit_bytes=40 << 20),
        cost_estimate=pl.CostEstimate(flops=COST, bytes_accessed=COST, transcendentals=0),
    )(*raws, narrow, middle, first, inputs)


def slot_back_kernel(place_ref, grad_ref, *refs):
    slots, out_ref, held, arrived = refs[:-3], refs[-3], refs[-2], refs[-1]
    each = len(slots) // 2
    rows, cols = held.shape[1:]
    copies = [
        pltpu.make_async_copy(ref.at[:, pl.ds(0, cols)], held.at[slot], arrived.at[slot])
        for slot, ref in enumerate(slots)
    ]
    for slot in range(each):
        copies[slot].start()
        copies[each + slot].start()
    grads = [
        grad_ref[:, pl.ds(pl.multiple_of((place_ref[1] ^ half) * cols, cols), cols)]
        for half in range(2)
    ]
    for slot in range(each):
        copies[slot].wait()
        copies[each + slot].wait()
        out_ref[:, pl.ds(place_of(place_ref, slot, rows), rows)] = lax.dot_general(
            grads[0], held[slot], NT, preferred_element_type=F32
        ) + lax.dot_general(grads[1], held[each + slot], NT, preferred_element_type=F32)


def slot_back(place, grads, slots):
    rows = slots[0][0].shape[0]
    count, cols = grads.shape
    many = 2 * len(slots[0])
    return pl.pallas_call(
        slot_back_kernel,
        grid_spec=pltpu.PrefetchScalarGridSpec(
            num_scalar_prefetch=1,
            grid=(1,),
            in_specs=[pl.BlockSpec((count, cols), lambda n, s: (0, 0))]
            + [pl.BlockSpec(memory_space=pl.ANY) for _ in range(many)],
            out_specs=pl.BlockSpec((count, D), lambda n, s: (0, 0)),
            scratch_shapes=[
                pltpu.VMEM((many, rows, cols // 2), BF),
                pltpu.SemaphoreType.DMA((many,)),
            ],
        ),
        out_shape=jax.ShapeDtypeStruct((count, D), F32),
        compiler_params=pltpu.CompilerParams(vmem_limit_bytes=40 << 20),
        cost_estimate=pl.CostEstimate(flops=COST, bytes_accessed=COST, transcendentals=0),
    )(place, grads, *slots[0], *slots[1])


def slot_back_wide(place, grads, slots):
    rows = slots[0].shape[0]
    out = jnp.zeros((grads.shape[0], len(slots) * rows), F32)
    for slot, held in enumerate(slots):
        out = lax.dynamic_update_slice(out, mm_t(grads, held), (0, (place[0] ^ slot) * rows))
    return out


def pad_to(rows, count):
    return jnp.concatenate([rows, jnp.zeros((count - rows.shape[0], rows.shape[1]), rows.dtype)])


def split_rows(weighted):
    high = weighted.astype(BF)
    return high, (weighted - high.astype(F32)).astype(BF)


def terms_of(grads_low, weighted, outer, reduced, offset):
    rank = outer.shape[0]
    rows = set_rows(outer, offset)
    narrow = 2.0 * lax.dot_general(grads_low, rows.astype(BF), NT, preferred_element_type=F32)
    middle = lax.dot_general(weighted, rows, NT, precision=PRECISE, preferred_element_type=F32)
    own = lax.broadcasted_iota(jnp.int32, middle.shape, 0) // RANK + offset // RANK
    middle = jnp.where(
        lax.broadcasted_iota(jnp.int32, middle.shape, 1) // RANK == own, middle, 0.0
    )
    under = (((0,), (0,)), ((), ()))
    high, low = split_parts(reduced)
    both = lax.dot_general(high, grads_low, under, preferred_element_type=F32)
    both = both + lax.dot_general(low, grads_low, under, preferred_element_type=F32)
    return narrow, middle, 2.0 * both[offset : offset + rank]


def terms_kernel(
    grad_ref, z_ref, scale_ref, slope_ref, outer_ref, reduced_ref,
    rows_ref, sum_ref, product_ref, narrow_ref, middle_ref, *, offset,
):
    count = grad_ref.shape[0]
    rank = outer_ref.shape[0]
    grads = grad_ref[...]
    sums = jnp.sum(grads * z_ref[...], axis=0, keepdims=True)
    sum_ref[...] = sums
    low = (grads * scale_ref[...]).astype(BF)
    weighted = (sums * slope_ref[...]) * outer_ref[...]
    high_part, low_part = split_rows(weighted)
    rows_ref[:count, :] = low
    rows_ref[count : count + rank, :] = high_part
    rows_ref[count + rank :, :] = low_part
    narrow, middle, product = terms_of(
        low, weighted, outer_ref[...], reduced_ref[...], offset
    )
    product_ref[...] = product

    @pl.when(pl.program_id(0) == 0)
    def _():
        narrow_ref[...] = narrow
        middle_ref[...] = middle

    @pl.when(pl.program_id(0) > 0)
    def _():
        narrow_ref[...] += narrow
        middle_ref[...] += middle


def grad_terms(grads, z, scale, slope, outer, offset, reduced, tile=512):
    count, cols = grads.shape
    rank = outer.shape[0]
    tiled = lambda rows: pl.BlockSpec((rows, tile), lambda n: (0, n))
    fixed = lambda rows, width: pl.BlockSpec((rows, width), lambda n: (0, 0))
    return pl.pallas_call(
        functools.partial(terms_kernel, offset=offset),
        grid=(cols // tile,),
        in_specs=[
            tiled(count), tiled(count), tiled(1), tiled(1), tiled(rank),
            fixed(count, reduced.shape[1]),
        ],
        out_specs=[
            tiled(count + 2 * rank), tiled(1), tiled(rank), fixed(count, EXTRA), fixed(rank, EXTRA),
        ],
        out_shape=[
            jax.ShapeDtypeStruct((count + 2 * rank, cols), BF),
            jax.ShapeDtypeStruct((1, cols), F32),
            jax.ShapeDtypeStruct((rank, cols), F32),
            jax.ShapeDtypeStruct((count, EXTRA), F32),
            jax.ShapeDtypeStruct((rank, EXTRA), F32),
        ],
        compiler_params=pltpu.CompilerParams(vmem_limit_bytes=40 << 20),
        cost_estimate=pl.CostEstimate(flops=COST, bytes_accessed=COST, transcendentals=0),
    )(grads, z, scale, slope, outer, reduced)


def mlp_kernel(
    place_ref, inputs_ref, main_ref, scale_ref, slope_ref, outer_ref,
    down_grad_ref, narrow_down_ref, first_ref, down_ref, *refs, offset,
):
    slots, kept = refs[:-7], refs[-7:]
    hidden_ref, rows_ref, sum_ref, product_ref, narrow_ref, middle_ref, reduced_ref = kept
    rows = slots[0].shape[0]
    half = hidden_ref.shape[1]
    count = hidden_ref.shape[0]

    @pl.when(pl.program_id(0) == 0)
    def _():
        reduced_ref[...] = jnp.dot(inputs_ref[...], main_ref[...], preferred_element_type=F32)

    gate_lanes = lax.broadcasted_iota(jnp.int32, (RANK, 2 * half), 1) < half
    outer = jnp.concatenate(
        [
            jnp.where(gate_lanes, outer_ref[...], 0.0),
            jnp.where(gate_lanes, 0.0, outer_ref[...]),
        ],
        axis=0,
    )
    z = low_rank(reduced_ref[...], outer, offset)
    for slot, ref in enumerate(slots):
        z = z + jnp.dot(
            inputs_ref[:, pl.ds(place_of(place_ref, slot, rows), rows)],
            ref[...],
            preferred_element_type=F32,
        )
    grad_hidden = lax.dot_general(
        down_grad_ref[...], down_ref[...], NT, preferred_element_type=F32
    ) + lax.dot_general(narrow_down_ref[...], first_ref[...], NT, preferred_element_type=F32)
    scale = scale_ref[...]
    gate_z, up_z = z[:, :half], z[:, half:]
    gate = gate_z * scale[:, :half]
    up = up_z * scale[:, half:]
    sigmoid = 1.0 / (1.0 + jnp.exp(-gate))
    silu = gate * sigmoid
    hidden_ref[...] = (silu * up).astype(BF)
    grad_up = grad_hidden * silu
    grad_gate = grad_hidden * up * (sigmoid * (1.0 + gate * (1.0 - sigmoid)))
    sums = jnp.concatenate(
        [
            jnp.sum(grad_gate * gate_z, axis=0, keepdims=True),
            jnp.sum(grad_up * up_z, axis=0, keepdims=True),
        ],
        axis=1,
    )
    sum_ref[...] = sums
    low = jnp.concatenate(
        [(grad_gate * scale[:, :half]).astype(BF), (grad_up * scale[:, half:]).astype(BF)], axis=1
    )
    rank = outer.shape[0]
    weighted = (sums * slope_ref[...]) * outer
    high_part, low_part = split_rows(weighted)
    rows_ref[:count, :] = low
    rows_ref[count : count + rank, :] = high_part
    rows_ref[count + rank :, :] = low_part
    narrow, middle, product = terms_of(low, weighted, outer, reduced_ref[...], offset)
    product_ref[:, :half] = product[: rank // 2, :half]
    product_ref[:, half:] = product[rank // 2 :, half:]

    @pl.when(pl.program_id(0) == 0)
    def _():
        narrow_ref[...] = narrow
        middle_ref[...] = middle

    @pl.when(pl.program_id(0) > 0)
    def _():
        narrow_ref[...] += narrow
        middle_ref[...] += middle


def mlp_block(
    place, inputs, first, offset, scale, slope, outer, down_grad, narrow_down, down, slots
):
    rows, cols = slots[0].shape
    count = inputs.shape[0]
    rank = 2 * RANK
    tile = 256
    fixed = lambda array: pl.BlockSpec(array.shape, lambda n, s: (0, 0))
    tiled = lambda rows: pl.BlockSpec((rows, tile), lambda n, s: (0, n))
    kept = lambda rows: pl.BlockSpec((rows, EXTRA), lambda n, s: (0, 0))
    return pl.pallas_call(
        functools.partial(mlp_kernel, offset=offset),
        grid_spec=pltpu.PrefetchScalarGridSpec(
            num_scalar_prefetch=1,
            grid=(cols // tile,),
            in_specs=[
                fixed(inputs), fixed(first), tiled(1), tiled(1), tiled(RANK), fixed(down_grad),
                fixed(narrow_down),
                pl.BlockSpec((tile // 2, 128), lambda n, s: (n, D // 128)),
                pl.BlockSpec((tile // 2, D), lambda n, s: (n, 0)),
            ]
            + [tiled(rows) for _ in slots],
            out_specs=[
                pl.BlockSpec((count, tile // 2), lambda n, s: (0, n)),
                tiled(count + 2 * rank),
                tiled(1),
                tiled(RANK),
                kept(count),
                kept(rank),
            ],
            scratch_shapes=[pltpu.VMEM((count, EXTRA), F32)],
        ),
        out_shape=[
            jax.ShapeDtypeStruct((count, cols // 2), BF),
            jax.ShapeDtypeStruct((count + 2 * rank, cols), BF),
            jax.ShapeDtypeStruct((1, cols), F32),
            jax.ShapeDtypeStruct((RANK, cols), F32),
            jax.ShapeDtypeStruct((count, EXTRA), F32),
            jax.ShapeDtypeStruct((rank, EXTRA), F32),
        ],
        compiler_params=pltpu.CompilerParams(vmem_limit_bytes=48 << 20),
        cost_estimate=pl.CostEstimate(flops=COST, bytes_accessed=COST, transcendentals=0),
    )(place, inputs, first, scale, slope, outer, down_grad, narrow_down, down, down, *slots)


def spread_kernel(quarter_ref, own_ref, other_ref, gate_ref, up_ref, hold, *, part):
    width = gate_ref.shape[1]
    blocks = width // (4 * part)
    for side, ref in enumerate((gate_ref, up_ref)):
        ref[...] = jnp.zeros_like(ref)
        for which, source in enumerate((own_ref, other_ref)):
            for tile in range(blocks * part // 128):
                hold[:, tile * 128 : (tile + 1) * 128] = source[
                    :, (2 * tile + side) * 128 : (2 * tile + side + 1) * 128
                ]
            for quarter in range(4):

                @pl.when((quarter_ref[0] ^ which) == quarter)
                def _():
                    for at in range(blocks):
                        low = (at * 4 + quarter) * part
                        ref[:, low : low + part] = hold[:, at * part : (at + 1) * part]


def spread_pair(quarter, own, other, part):
    rows, cols = own.shape
    return pl.pallas_call(
        functools.partial(spread_kernel, part=part),
        grid_spec=pltpu.PrefetchScalarGridSpec(
            num_scalar_prefetch=1,
            grid=(1,),
            in_specs=[pl.BlockSpec((rows, cols), lambda n, s: (0, 0))] * 2,
            out_specs=[pl.BlockSpec((rows, 2 * cols), lambda n, s: (0, 0))] * 2,
            scratch_shapes=[pltpu.VMEM((rows, cols // 2), F32)],
        ),
        out_shape=[jax.ShapeDtypeStruct((rows, 2 * cols), F32)] * 2,
        cost_estimate=pl.CostEstimate(flops=rows, bytes_accessed=1 << 20, transcendentals=0),
    )(quarter, own, other)


def column_sums(base, first_high, first_low, outer, offset):
    outer_high, outer_low = split_parts(set_rows(outer, offset))
    product = (
        jnp.dot(first_high, outer_high, preferred_element_type=F32)
        + jnp.dot(first_high, outer_low, preferred_element_type=F32)
        + jnp.dot(first_low, outer_high, preferred_element_type=F32)
    )
    merged = base.astype(F32) + 2.0 * product
    merged_high, merged_low = split_parts(merged)
    under = (((0,), (0,)), ((), ()))
    cross = (
        lax.dot_general(first_high, merged_high, under, preferred_element_type=F32)
        + lax.dot_general(first_high, merged_low, under, preferred_element_type=F32)
        + lax.dot_general(first_low, merged_high, under, preferred_element_type=F32)
    )
    return jnp.sum(merged * merged, axis=0, keepdims=True), cross[offset : offset + RANK]


def widened(first):
    return jnp.concatenate(
        [first, jnp.zeros((first.shape[0], EXTRA - first.shape[1]), first.dtype)], axis=1
    )


def early_kernel(
    place_ref, query_ref, key_ref, value_ref, main_ref, outer_ref,
    query_out, kv_out, square_ref, cross_ref,
):
    half = query_out.shape[1]
    kv_cols = key_ref.shape[1]
    high, low = split_parts(widened(main_ref[...]))
    kv_out[:, kv_cols:] = high
    for core in range(2):

        @pl.when(place_ref[1] == core)
        def _():
            query_out[...] = query_ref[:, core * half : (core + 1) * half]
            kv = (key_ref, value_ref)[core][...]
            kv_out[:, :kv_cols] = kv
            start = 2 * half + core * kv_cols
            square, cross = column_sums(
                kv, high, low, outer_ref[:, start : start + kv_cols], (1 + core) * RANK
            )
            square_ref[:, :kv_cols] = square
            cross_ref[:, :kv_cols] = cross
            for tile in range(half // 256):
                at = core * half + tile * 256
                square, cross = column_sums(
                    query_ref[:, at : at + 256], high, low, outer_ref[:, at : at + 256], 0
                )
                to = kv_cols + tile * 256
                square_ref[:, to : to + 256] = square
                cross_ref[:, to : to + 256] = cross


def early_work(place, query, key, value, main, outer):
    rows, cols = query.shape
    kv_cols = key.shape[1]
    fixed = lambda array: pl.BlockSpec(array.shape, lambda n, s: (0, 0))
    shapes = [
        jax.ShapeDtypeStruct((rows, cols // 2), BF),
        jax.ShapeDtypeStruct((rows, kv_cols + EXTRA), BF),
        jax.ShapeDtypeStruct((1, kv_cols + cols // 2), F32),
        jax.ShapeDtypeStruct((RANK, kv_cols + cols // 2), F32),
    ]
    return pl.pallas_call(
        early_kernel,
        grid_spec=pltpu.PrefetchScalarGridSpec(
            num_scalar_prefetch=1,
            grid=(1,),
            in_specs=[fixed(query), fixed(key), fixed(value), fixed(main)]
            + [pl.BlockSpec((RANK, cols + 2 * kv_cols), lambda n, s: (0, 0))],
            out_specs=[fixed(shape) for shape in shapes],
        ),
        out_shape=shapes,
        compiler_params=pltpu.CompilerParams(vmem_limit_bytes=32 << 20),
        cost_estimate=pl.CostEstimate(flops=COST, bytes_accessed=COST, transcendentals=0),
    )(place, query, key, value, main, outer)


def later_kernel(
    place_ref, out_w_ref, gate_ref, up_ref, down_w_ref, main_ref, first_ref, outer_ref, mags_ref,
    out_out, mlp_out, down_out, square_ref, cross_ref, picked_ref, hold, *, part,
):
    half = out_out.shape[1]
    width = gate_ref.shape[1]
    blocks = width // (4 * part)
    cols = blocks * part
    starts = [STARTS[n] for n in range(7)]
    high, low = split_parts(widened(main_ref[...]))
    down_first = widened(first_ref[...])
    down_high, down_low = split_parts(down_first)
    rows = gate_ref.shape[0]
    lanes = mags_ref.shape[0]
    for quarter in range(4):

        @pl.when(place_ref[2] == quarter)
        def _():
            for side, ref in enumerate((gate_ref, up_ref)):
                for at in range(blocks):
                    start = (at * 4 + quarter) * part
                    hold[side, :rows, at * part : (at + 1) * part] = ref[
                        :, start : start + part
                    ].astype(F32)
                    begin = starts[4 + side] + start
                    hold[side, rows : rows + RANK, at * part : (at + 1) * part] = outer_ref[
                        :, begin : begin + part
                    ]
                    hold[side, rows + RANK :, at * part : (at + 1) * part] = mags_ref[
                        :, begin : begin + part
                    ]
    for tile in range(cols // 128):
        for side in range(2):
            to = slice((2 * tile + side) * 128, (2 * tile + side + 1) * 128)
            taken = hold[side, :, tile * 128 : (tile + 1) * 128]
            base = taken[:rows].astype(BF)
            mlp_out[:, to] = base
            outer = taken[rows : rows + RANK]
            picked_ref[:RANK, to] = outer
            picked_ref[RANK:, to] = taken[rows + RANK :]
            square, cross = column_sums(base, high, low, outer, (4 + side) * RANK)
            square_ref[:, half + to.start : half + to.stop] = square
            cross_ref[:, half + to.start : half + to.stop] = cross
    down_at = pl.ds(pl.multiple_of(place_ref[2] * part, 16 if part % 16 == 0 else 8), part)
    down_out[:, : 2 * half] = down_w_ref[down_at, :]
    factor = first_ref[down_at, :]
    factor = jnp.concatenate([factor, factor], axis=1)
    down_out[:, 2 * half :] = widened(factor).astype(BF)
    for core in range(2):

        @pl.when(place_ref[1] == core)
        def _():
            out_out[...] = out_w_ref[:, core * half : (core + 1) * half]
            for tile in range(half // 256):
                at = core * half + tile * 256
                square, cross = column_sums(
                    out_w_ref[:, at : at + 256],
                    high,
                    low,
                    outer_ref[:, starts[3] + at : starts[3] + at + 256],
                    3 * RANK,
                )
                to = slice(tile * 256, (tile + 1) * 256)
                square_ref[:, to] = square
                cross_ref[:, to] = cross
                square, cross = column_sums(
                    down_w_ref[:, at : at + 256],
                    down_high,
                    down_low,
                    outer_ref[:, starts[6] + at : starts[6] + at + 256],
                    0,
                )
                begin = half + 2 * cols + tile * 256
                square_ref[:, begin : begin + 256] = square
                cross_ref[:, begin : begin + 256] = cross


def later_work(place, out_w, gate, up, down_w, main, first, outer, mags, part):
    rows, cols = out_w.shape
    half = cols // 2
    mlp = 2 * (gate.shape[1] // 4)
    total = 2 * half + mlp
    fixed = lambda array: pl.BlockSpec(array.shape, lambda n, s: (0, 0))
    inputs = [out_w, gate, up, down_w, main, first, outer, mags]
    shapes = [
        jax.ShapeDtypeStruct((rows, half), BF),
        jax.ShapeDtypeStruct((rows, mlp), BF),
        jax.ShapeDtypeStruct((part, cols + EXTRA), BF),
        jax.ShapeDtypeStruct((1, total), F32),
        jax.ShapeDtypeStruct((RANK, total), F32),
        jax.ShapeDtypeStruct((RANK + 8, mlp), F32),
    ]
    return pl.pallas_call(
        functools.partial(later_kernel, part=part),
        grid_spec=pltpu.PrefetchScalarGridSpec(
            num_scalar_prefetch=1,
            grid=(1,),
            in_specs=[fixed(array) for array in inputs],
            out_specs=[fixed(shape) for shape in shapes],
            scratch_shapes=[pltpu.VMEM((2, rows + RANK + 8, mlp // 2), F32)],
        ),
        out_shape=shapes,
        compiler_params=pltpu.CompilerParams(vmem_limit_bytes=48 << 20),
        cost_estimate=pl.CostEstimate(flops=COST, bytes_accessed=COST, transcendentals=0),
    )(place, *inputs)


def shards(
    tokens,
    cotangent,
    gain_attn,
    gain_ffn,
    w_query,
    w_key,
    w_value,
    w_output,
    w_gate,
    w_up,
    w_down,
    adapt_main,
    adapt_down,
    adapt_outer,
    magnitudes,
    main_first,
    main_second,
    down_first,
    down_second,
    outer_first,
    outer_second,
    mag_first,
    mag_second,
    segments,
):
    wide_count = lax.axis_size("wide")
    tok_count = lax.axis_size("tok")
    wide = lax.axis_index("wide")
    tok = lax.axis_index("tok")
    core = tok % 2
    place = jnp.stack([wide, core, tok % 4]).astype(jnp.int32)
    quarter = (tok % 4).astype(jnp.int32)[None]
    length, share = tokens.shape
    hidden_share = w_down.shape[0]
    part = hidden_share // 4
    block = length // (wide_count * CHUNKS)
    count = CHUNKS * block
    block_cols = wide_count * part
    half = D // 2
    kv_cols = KVH * HD

    def partner(array):
        return swap(array, "tok", 2)

    def other_core(array):
        return swap(array, "tok", 1)

    def to_tokens(features):
        pieces = features.reshape(CHUNKS, wide_count, block, share)
        whole = jnp.zeros((count, D), features.dtype)
        for slot in range(wide_count):
            piece = lax.dynamic_index_in_dim(pieces, wide ^ slot, 1, keepdims=False)
            piece = piece.reshape(count, share)
            if slot:
                piece = swap(piece, "wide", slot)
            whole = lax.dynamic_update_slice(whole, piece, (0, (wide ^ slot) * share))
        return whole

    across = wide_count // 4
    deep, side = wide // across, wide % across

    def to_tokens_staged(features):
        pieces = features.reshape(CHUNKS, 4, across, block, share)
        rows = jnp.zeros((4, CHUNKS, block, across * share), features.dtype)
        for slot in range(across):
            piece = lax.dynamic_index_in_dim(pieces, side ^ slot, 2, keepdims=False)
            piece = jnp.swapaxes(piece, 0, 1)
            if slot:
                piece = swap(piece, "wide", slot)
            rows = lax.dynamic_update_slice(rows, piece, (0, 0, 0, (side ^ slot) * share))
        whole = jnp.zeros((count, D), features.dtype)
        for slot in range(4):
            piece = lax.dynamic_index_in_dim(rows, deep ^ slot, 0, keepdims=False)
            piece = piece.reshape(count, across * share)
            if slot:
                piece = swap(piece, "wide", slot * across)
            whole = lax.dynamic_update_slice(whole, piece, (0, (deep ^ slot) * across * share))
        return whole

    def from_tokens(rows):
        cols = across * share
        held = jnp.zeros((CHUNKS, 4, block, cols), rows.dtype)
        for slot in range(4):
            piece = lax.dynamic_slice(rows, (0, (deep ^ slot) * cols), (count, cols))
            if slot:
                piece = swap(piece, "wide", slot * across)
            piece = piece.reshape(CHUNKS, 1, block, cols)
            held = lax.dynamic_update_slice(held, piece, (0, deep ^ slot, 0, 0))
        whole = jnp.zeros((CHUNKS, 4, across, block, share), rows.dtype)
        for slot in range(across):
            piece = lax.dynamic_slice_in_dim(held, (side ^ slot) * share, share, 3)
            if slot:
                piece = swap(piece, "wide", slot)
            whole = lax.dynamic_update_slice(whole, piece[:, :, None], (0, 0, side ^ slot, 0, 0))
        return whole.reshape(length, share)

    def own_half(array, axis=-1):
        size = array.shape[axis] // 2
        return lax.dynamic_slice_in_dim(array, core * size, size, axis)

    def in_order(blocks):
        return jnp.where(
            core == 0, jnp.concatenate(blocks, axis=-1), jnp.concatenate(blocks[::-1], axis=-1)
        )

    def by_core(zero, one, flip=0):
        return jnp.where(core == flip, zero, one)

    def sides(array, n):
        return array[..., STARTS[n] : STARTS[n] + WIDTHS[n]]

    ends = [0, kv_cols, kv_cols + half, kv_cols + 2 * half, kv_cols + 2 * half + 2 * block_cols]
    ends.append(ends[-1] + half)

    def cut(array, n):
        return array[..., ends[n] : ends[n + 1]]

    KV, QUERY, OUT, MLP, DOWN = range(5)

    residual = to_tokens(tokens).astype(F32)
    gains = all_blocks(jnp.stack([gain_attn, gain_ffn]), "wide")
    gains = jnp.swapaxes(gains, 0, 1).reshape(2, D)

    query_shard, kv_shard, squares, soon_cross = early_work(
        place, w_query, w_key, w_value, adapt_main, adapt_outer
    )
    kv_slots = [gather_slots(kv_shard)]
    query_slots = [gather_slots(after(query_shard, *near(kv_slots[0])))]
    mags = magnitudes[None]

    def column_terms(squares, pieces):
        norms = jnp.sqrt(all_sum(squares, ["wide"]))
        rows = jnp.concatenate([piece[0] for piece in pieces], axis=1)
        rows = jnp.concatenate([rows, norms])
        out = []
        for held in (rows, other_core(rows)):
            mags_row, norm = held[:1], held[1:2]
            scale, slope = mags_row / norm, -mags_row / (norm * norm * norm)
            start = 0
            split = []
            for piece in pieces:
                stop = start + piece[0].shape[1]
                split.append((scale[:, start:stop], slope[:, start:stop], norm[:, start:stop]))
                start = stop
            out.append(split)
        return out

    soon = column_terms(
        squares, [(by_core(sides(mags, 1), sides(mags, 2)),), (own_half(sides(mags, 0)),)]
    )
    later_output, *_ = lax.optimization_barrier(
        (w_output, residual, *near(kv_slots[0]))
    )
    out_shard, mlp_shard, down_shard, squares, rest_cross, picked = later_work(
        place, later_output, w_gate, w_up, w_down, adapt_main, adapt_down, adapt_outer,
        jnp.broadcast_to(mags, (8, OUTS)), part,
    )
    rest = column_terms(
        squares,
        [(own_half(sides(mags, 3)),), (picked[RANK : RANK + 1],), (own_half(sides(mags, 6)),)],
    )
    mlp_outer = [picked[:RANK]]
    mlp_outer.append(other_core(mlp_outer[0]))
    columns = [soon[k] + rest[k] for k in range(2)]
    scale_by, slope_by, norms_by = (
        [[columns[k][n][i] for n in range(5)] for k in range(2)] for i in range(3)
    )

    def natural_of(parts, n):
        return in_order([p[n] for p in parts])

    scales, slopes, norms = (
        [natural_of(parts, n) if n != MLP else None for n in range(5)]
        for parts in (scale_by, slope_by, norms_by)
    )
    outers = [sides(adapt_outer, n) for n in range(7)]
    outer_kv = jnp.concatenate(
        [jnp.pad(outers[1], ((0, 0), (0, kv_cols))), jnp.pad(outers[2], ((0, 0), (kv_cols, 0)))]
    )

    kv_slots.append({s: other_core(held) for s, held in kv_slots[0].items()})
    query_slots.append({s: other_core(held) for s, held in query_slots[0].items()})
    low_main = put_rows(
        {s: held[:, kv_cols:] for s, held in kv_slots[0].items()}, jnp.zeros((0, EXTRA), BF)
    )

    def main_cols(n, many=1):
        return low_main[:, n * RANK : (n + many) * RANK]

    def norm_rows(values, gain_row):
        inverse = lax.rsqrt(jnp.mean(values * values, axis=1, keepdims=True) + EPS_NORM)
        return (values * inverse * gain_row[None, :]).astype(BF), inverse

    def norm_rows_back(values, gain_row, inverse, grad_normed):
        inner = jnp.sum(values * gain_row[None, :] * grad_normed, axis=1, keepdims=True)
        return (
            grad_normed * gain_row[None, :] * inverse
            - values * (inverse * inverse * inverse * inner / D)
        )

    def ordered(slots):
        return [slots[s] for s in range(wide_count)]

    own_places = (
        jnp.arange(CHUNKS, dtype=jnp.int32)[:, None] * (wide_count * block)
        + wide * block
        + jnp.arange(block, dtype=jnp.int32)[None, :]
    ).reshape(count)
    segment_row = segments[0]
    own_segment = lax.dynamic_index_in_dim(
        segment_row.reshape(CHUNKS, wide_count, block), wide, 1, keepdims=False
    ).reshape(count)
    own_starts = jnp.sum(
        (segment_row[None, :] < own_segment[:, None]).astype(jnp.int32), axis=1
    )
    frequency = ROPE_BASE ** (-2.0 * jnp.arange(HD // 2, dtype=F32) / HD)
    angles = (own_places - own_starts).astype(F32)[:, None] * frequency[None, :]
    cosine = jnp.tile(jnp.cos(angles), (1, 4))
    sine = jnp.tile(jnp.concatenate([-jnp.sin(angles), jnp.sin(angles)], axis=1), (1, 2))
    place_rows = jnp.tile(own_places.reshape(CHUNKS, 1, block), (1, 1, GROUP))
    start_rows = jnp.tile(own_starts.reshape(CHUNKS, 1, block), (1, 1, GROUP))
    first_block = own_starts.reshape(CHUNKS, block)[:, 0] // (wide_count * block)

    normed_one, inverse_one = norm_rows(residual, gains[0])
    kv_z, reduced_one = slot_mm(
        place, normed_one, low_main, outer_kv, RANK, [ordered(kv_slots[k]) for k in range(2)]
    )
    kv_scaled = kv_z * scales[KV]
    keys = turn(kv_scaled[:, :kv_cols], cosine[:, :HD], sine[:, :HD])
    kv = jnp.concatenate(
        [keys.reshape(count, KVH, HD), kv_scaled[:, kv_cols:].reshape(count, KVH, HD)], axis=2
    ).astype(BF)
    token_slots = gather_slots(kv.reshape(CHUNKS, 1, block, KVH * 2 * HD))
    kv = jnp.zeros((CHUNKS, wide_count, block, KVH * 2 * HD), BF)
    for slot, held in token_slots.items():
        kv = lax.dynamic_update_slice(kv, held, (0, wide ^ slot, 0, 0))
    kv = kv.reshape(length, KVH * 2 * HD)
    kvt = kv.T.reshape(KVH, 2 * HD, length)
    query_z, _ = slot_mm(
        place, normed_one, low_main, outers[0], 0, [ordered(query_slots[k]) for k in range(2)]
    )
    queries, attended, log_total = attend(
        first_block, query_z, scales[QUERY], cosine, sine, place_rows, start_rows, kv, kvt
    )

    out_slots = [gather_slots(after(out_shard, *near(query_slots[0])), True)]
    out_slots.append({s: other_core(held) for s, held in out_slots[0].items()})
    upstream = to_tokens_staged(after(cotangent, *near(out_slots[0]), *near(token_slots))).astype(F32)
    down_slots = gather_slots(after(down_shard, *near(out_slots[0]), *token_slots.values()))
    down_weights = [put_rows(down_slots, jnp.zeros((0, D + EXTRA), BF))]
    down_weights.append(other_core(down_weights[0]))
    mlp_slots = [gather_slots(after(mlp_shard, *near(down_slots)), True)]
    mlp_slots.append({s: other_core(held) for s, held in mlp_slots[0].items()})

    output_z, reduced_out = slot_mm(
        place, attended, low_main, outers[3], 3 * RANK, [ordered(out_slots[k]) for k in range(2)]
    )
    hidden_one = residual + output_z * scales[OUT]

    normed_own, inverse_two = norm_rows(hidden_one, gains[1])
    normed_two = jnp.concatenate([normed_own, partner(normed_own)])
    down_low = (upstream * scales[DOWN]).astype(BF)
    down_low = jnp.concatenate([down_low, partner(down_low)])
    narrow_down = 2.0 * mm_t(down_low, outers[6].astype(BF))
    narrow_down_lanes = lanes_of(narrow_down)
    blocks = [
        mlp_block(
            place,
            normed_two,
            low_main,
            4 * RANK,
            scale_by[k][MLP],
            slope_by[k][MLP],
            mlp_outer[k],
            down_low,
            narrow_down_lanes,
            down_weights[k],
            ordered(mlp_slots[k]),
        )
        for k in range(2)
    ]
    through = mm(blocks[0][0], down_weights[0]) + mm(blocks[1][0], down_weights[1])
    reduced_down = through[:, D : D + RANK]
    down_sum = through[:, :D] + mm(
        lanes_of(reduced_down), twice_low(outers[6])
    )

    def first_term(product, weight_term, middle, first_cols):
        both = jnp.concatenate(two_parts(middle))
        return product + 2.0 * (weight_term + 2.0 * fold_parts(mm_t(both, first_cols), RANK))

    backs = [slot_back_wide(place, blocks[k][1], ordered(mlp_slots[k])) for k in range(2)]
    pairs = 2 * RANK
    grad_normed, first_pairs = finish_back(
        backs, [pairs, pairs], blocks[0][4] + blocks[1][4], blocks[0][5] + blocks[1][5], low_main,
        normed_two, 4 * RANK, True,
    )
    swapped = partner(grad_normed[count:].astype(BF))
    grad_normed = grad_normed[:count] + swapped.astype(F32)
    grad_mid = upstream + norm_rows_back(hidden_one, gains[1], inverse_two, grad_normed)
    down_far = partner(after(down_sum[count:].astype(BF), swapped))
    down_z = down_sum[:count] + down_far.astype(F32)
    layer_out = from_tokens((hidden_one + down_z * scales[DOWN]).astype(BF))

    def first_grads(rows, inputs, narrow, middle, factors, many):
        size = many * RANK
        parts = jnp.concatenate(two_parts(narrow), axis=1)
        product = fold_parts(t_mm(parts, inputs), size)
        same = jnp.arange(size)[:, None] // RANK == jnp.arange(size)[None, :] // RANK
        middle = jnp.where(same, middle[:, :size], 0.0)
        term = fold_parts(mm_t(jnp.concatenate(two_parts(middle)), factors), size)
        return product + 2.0 * (fold_parts(rows, size) + 2.0 * term)

    def twice(cols):
        return jnp.concatenate([cols, cols], axis=1)

    out_rows, scale_out, outer_out, narrow_out, middle_out = grad_terms(
        grad_mid, output_z, scales[OUT], slopes[OUT], outers[3], 3 * RANK, reduced_out
    )
    back_out = slot_back(place, out_rows, [ordered(out_slots[k]) for k in range(2)])
    grad_mixed, first_out = finish_back(
        [back_out], [RANK], narrow_out, middle_out, low_main, attended, 3 * RANK
    )
    grad_mixed = grad_mixed.astype(BF)

    query_grad, kv_grad = attend_back(
        first_block, queries, cosine, sine, place_rows, start_rows, kv, kvt, log_total, attended,
        grad_mixed,
    )
    kv_grad = kv_grad.reshape(CHUNKS, wide_count, block, KVH * 2 * HD)
    kv_grad = after(jnp.swapaxes(kv_grad, 0, 1).astype(F32), layer_out)
    bits = bits_of(wide_count)
    kv_half = KVH * HD
    kv_grad = jnp.concatenate(
        [
            scatter_sum(kv_grad[..., :kv_half], "wide", BF),
            scatter_sum(kv_grad[..., kv_half:], "wide", BF, [bits[-2], *bits[:-2], bits[-1]]),
        ],
        axis=-1,
    )
    kv_grad = kv_grad.reshape(count, KVH, 2 * HD)
    key_grad = turn(kv_grad[:, :, :HD].reshape(count, -1), cosine[:, :HD], -sine[:, :HD])
    value_grad = kv_grad[:, :, HD:].reshape(count, -1)

    query_rows_low, scale_query, outer_query, narrow_query, middle_query = grad_terms(
        query_grad, query_z, scales[QUERY], slopes[QUERY], outers[0], 0, reduced_one
    )
    back_query = slot_back(place, query_rows_low, [ordered(query_slots[k]) for k in range(2)])
    kv_rows_low, scale_kv, outer_kv_grad, narrow_kv, middle_kv = grad_terms(
        jnp.concatenate([key_grad, value_grad], axis=1), kv_z, scales[KV], slopes[KV], outer_kv,
        RANK, reduced_one,
    )
    back_kv = slot_back(place, kv_rows_low, [ordered(kv_slots[k]) for k in range(2)])
    grad_normed, first_one = finish_back(
        [back_query, back_kv],
        [RANK, pairs],
        narrow_query + narrow_kv,
        jnp.concatenate([middle_query, middle_kv]),
        low_main,
        normed_one,
        0,
    )
    grad_tokens = from_tokens(
        (grad_mid + norm_rows_back(residual, gains[0], inverse_one, grad_normed)).astype(BF)
    )

    scale_down = jnp.sum(upstream * down_z, axis=0, keepdims=True)
    pair_down = scale_down + partner(scale_down)
    weighted = (pair_down * slopes[DOWN]) * outers[6]
    middle_down = gram_of(weighted, outers[6])
    weighted_parts = jnp.pad(jnp.concatenate(two_parts(weighted)), ((0, 0), (0, EXTRA)))
    first_down = [
        first_grads(
            mm_t(weighted_parts, down_weights[k]), blocks[k][0], narrow_down, middle_down,
            down_weights[k][:, D : D + RANK], 1,
        )
        for k in range(2)
    ]
    outer_down = 2.0 * fold_parts(
        t_mm(jnp.concatenate(two_parts(reduced_down), axis=1), down_low), RANK
    )
    of_keys = (jnp.arange(2 * kv_cols) < kv_cols)[None, :]
    outer_kv_grad = jnp.where(of_keys, outer_kv_grad[:RANK], outer_kv_grad[RANK:])
    crosses = [soon_cross, rest_cross]
    cross_own = all_sum(after(jnp.concatenate(crosses, axis=1), down_z), ["wide"])
    cross_by = [cross_own, other_core(cross_own)]

    def second_grads(product, sums, slope, norm, cross):
        return jnp.concatenate([product + 2.0 * (sums * slope) * cross, sums / norm])

    plain = {
        n: second_grads(
            product, sums, slopes[n], norms[n], in_order([cut(c, n) for c in cross_by])
        )
        for n, product, sums in (
            (KV, outer_kv_grad, scale_kv),
            (QUERY, outer_query, scale_query),
            (OUT, outer_out, scale_out),
            (DOWN, outer_down, scale_down),
        )
    }
    eights = [
        jnp.pad(
            second_grads(
                blocks[k][3], blocks[k][2], slope_by[k][MLP], norms_by[k][MLP], cut(cross_by[k], MLP)
            ),
            ((0, 7), (0, 0)),
        )
        for k in range(2)
    ]
    gate_grads, up_grads = spread_pair(quarter, *eights, part)
    outer_cols = jnp.concatenate(
        [
            plain[QUERY],
            plain[KV],
            plain[OUT],
            gate_grads[: RANK + 1],
            up_grads[: RANK + 1],
            plain[DOWN],
        ],
        axis=1,
    )
    main_rows = jnp.concatenate([first_one, first_out, first_pairs])
    down_rows = jnp.zeros((RANK, wide_count, 4, part), F32)
    for k in range(2):
        down_rows = lax.dynamic_update_slice(
            down_rows,
            first_down[k].reshape(RANK, wide_count, 1, part),
            (0, 0, quarter[0] ^ k, 0),
        )
    down_rows = down_rows.reshape(RANK, FF)

    main_width = 6 * RANK // tok_count
    down_width = RANK // tok_count
    outer_share = OUTS // (tok_count * wide_count)

    def to_owner(rows, tok_rows, wide_cols):
        shaped = rows.reshape(tok_count, tok_rows, wide_count, wide_cols)
        summed = scatter_sum(shaped, "tok")
        return scatter_sum(jnp.swapaxes(summed, 0, 1), "wide")

    main_part = to_owner(main_rows, main_width, share).T
    down_part = to_owner(down_rows, down_width, hidden_share).T
    outer_blocks = jnp.moveaxis(
        outer_cols.reshape(RANK + 1, tok_count, wide_count, outer_share), 0, 2
    )
    outer_sum = scatter_sum(scatter_sum(outer_blocks, "tok"), "wide")
    outer_part = outer_sum[:RANK]
    block_start = (tok * wide_count + wide) * outer_share
    mag_part = outer_sum[RANK]

    local_squares = (
        squared_sum(main_part)
        + squared_sum(down_part)
        + squared_sum(outer_part)
        + squared_sum(mag_part)
    )
    grad_total = all_sum(jnp.full((8, 128), local_squares), ["tok", "wide"])[0, 0]
    grad_norm = jnp.sqrt(grad_total)
    clip_factor = CLIP_MAX / jnp.maximum(grad_norm, CLIP_MAX)
    main_param = lax.dynamic_slice_in_dim(adapt_main, tok * main_width, main_width, 1)
    down_param = lax.dynamic_slice_in_dim(adapt_down, tok * down_width, down_width, 1)
    outer_param = lax.dynamic_slice_in_dim(adapt_outer, block_start, outer_share, 1)
    mag_param = lax.dynamic_slice_in_dim(magnitudes, block_start, outer_share, 0)
    main_new, main_first_new, main_second_new = adam(
        main_param, main_part, main_first, main_second, RATE_ADAPT, clip_factor
    )
    down_new, down_first_new, down_second_new = adam(
        down_param, down_part, down_first, down_second, RATE_ADAPT, clip_factor
    )
    outer_new, outer_first_new, outer_second_new = adam(
        outer_param, outer_part, outer_first, outer_second, RATE_OUTER, clip_factor
    )
    mag_new, mag_first_new, mag_second_new = adam(
        mag_param, mag_part, mag_first, mag_second, RATE_MAGNITUDE, clip_factor
    )
    mag_clipped = mag_part * clip_factor
    return (
        layer_out,
        grad_tokens,
        grad_norm,
        main_new,
        main_first_new,
        main_second_new,
        down_new,
        down_first_new,
        down_second_new,
        outer_new,
        outer_first_new,
        outer_second_new,
        mag_new,
        mag_clipped,
        mag_second_new,
    )


def solution(mesh):
    return jax.shard_map(
        shards,
        mesh=mesh,
        in_specs=(
            P("tok", "wide"),
            P("tok", "wide"),
            P("wide"),
            P("wide"),
            P("wide", None),
            P("wide", None),
            P("wide", None),
            P("wide", None),
            P("wide", None),
            P("wide", None),
            P("wide", None),
            P("wide", None),
            P("wide", None),
            P(),
            P(),
            P("wide", "tok"),
            P("wide", "tok"),
            P("wide", "tok"),
            P("wide", "tok"),
            P(None, ("tok", "wide")),
            P(None, ("tok", "wide")),
            P(("tok", "wide")),
            P(("tok", "wide")),
            P("tok", None),
        ),
        out_specs=(
            P("tok", "wide"),
            P("tok", "wide"),
            P(),
            P("wide", "tok"),
            P("wide", "tok"),
            P("wide", "tok"),
            P("wide", "tok"),
            P("wide", "tok"),
            P("wide", "tok"),
            P(None, ("tok", "wide")),
            P(None, ("tok", "wide")),
            P(None, ("tok", "wide")),
            P(("tok", "wide")),
            P(("tok", "wide")),
            P(("tok", "wide")),
        ),
        check_vma=False,
    )
```

```python
import functools

import jax
import jax.numpy as jnp
from jax import lax
from jax.experimental import pallas as pl
from jax.experimental.pallas import tpu as pltpu
from jax.sharding import PartitionSpec as P

D = 2048
HEADS = 32
HD = 64
KVH = 4
FF = 5632
STEP = 10
RANK = 16
CHUNKS = 8
EXTRA = 128
COST = 1 << 10

EPS_NORM = 1e-05
ROPE_BASE = 10000.0
CLIP_MAX = 1.0
BETA_FIRST = 0.9
BETA_SECOND = 0.999
ADAM_EPS = 1e-08
WEIGHT_DECAY = 0.01
RATE_ADAPT = 0.02
RATE_OUTER = 0.05
RATE_MAGNITUDE = 0.4
PRECISE = lax.Precision.HIGHEST
MASKED = -1e30
NT = (((1,), (1,)), ((), ()))
GROUP = HEADS // KVH
FWD = 4
BWD = 4
BF = jnp.bfloat16
F32 = jnp.float32
WIDTHS = [D, KVH * HD, KVH * HD, D, FF, FF, D]
STARTS = [sum(WIDTHS[:number]) for number in range(7)]
OUTS = sum(WIDTHS)


def bits_of(count):
    return [1 << place for place in range(count.bit_length() - 1)]


def swap(array, axis, distance):
    count = lax.axis_size(axis)
    return lax.ppermute(array, axis, [(i, i ^ distance) for i in range(count)])


def mm(left, right):
    return jnp.dot(left, right, preferred_element_type=F32)


def mm_t(left, right):
    return lax.dot_general(left, right, (((1,), (1,)), ((), ())), preferred_element_type=F32)


def t_mm(left, right):
    return lax.dot_general(left, right, (((0,), (0,)), ((), ())), preferred_element_type=F32)


def two_parts(values):
    high = lax.reduce_precision(values, 8, 7)
    return high.astype(BF), (values - high).astype(BF)


def fold_parts(stacked, count):
    return stacked[:count] + stacked[count : 2 * count]


def adam(param, grad, first, second, rate, clip_factor):
    clipped = grad * clip_factor
    first_new = BETA_FIRST * first + (1.0 - BETA_FIRST) * clipped
    second_new = BETA_SECOND * second + (1.0 - BETA_SECOND) * clipped * clipped
    first_hat = first_new / (1.0 - BETA_FIRST**STEP)
    second_hat = second_new / (1.0 - BETA_SECOND**STEP)
    param_new = param - rate * (
        first_hat / (jnp.sqrt(second_hat) + ADAM_EPS) + WEIGHT_DECAY * param
    )
    return (param_new, first_new, second_new)


def squared_sum(values):
    return jnp.sum(values * values)


def all_sum(values, axes):
    for axis in axes:
        for bit in bits_of(lax.axis_size(axis)):
            values = values + swap(values, axis, bit)
    return values


def all_blocks(block, axis):
    stacked = block[None]
    index = lax.axis_index(axis)
    for bit in bits_of(lax.axis_size(axis)):
        upper = (index // bit) % 2 == 1
        received = swap(stacked, axis, bit)
        stacked = jnp.concatenate(
            [jnp.where(upper, received, stacked), jnp.where(upper, stacked, received)]
        )
    return stacked


def scatter_sum(blocks, axis, wire=F32, order=None):
    index = lax.axis_index(axis)
    bits = bits_of(lax.axis_size(axis))
    shape = blocks.shape[1:]
    left = list(reversed(bits))
    blocks = blocks.reshape((2,) * len(bits) + shape)
    for bit in order or bits:
        dim = left.index(bit)
        side = (index // bit) % 2
        keep = lax.dynamic_index_in_dim(blocks, side, dim, keepdims=False)
        send = lax.dynamic_index_in_dim(blocks, 1 - side, dim, keepdims=False)
        blocks = keep + swap(send.astype(wire), axis, bit).astype(blocks.dtype)
        left.remove(bit)
    return blocks


def after(value, *others):
    return lax.optimization_barrier((value,) + others)[0]


def gather_slots(shard, turned=False, gate=None):
    slots = {0: shard}
    count = lax.axis_size("wide")
    for slot in sorted(range(1, count), key=lambda i: bin(i).count("1")):
        low = slot & -slot
        if turned and slot == count - 1:
            low = count // 4
        held = slots[slot ^ low]
        if gate is not None and slot != low:
            held = after(held, gate)
        slots[slot] = swap(held, "wide", low)
    return slots


def near(slots):
    return [held for slot, held in slots.items() if bin(slot).count("1") == 1]


def far(slots, steps):
    return [held for slot, held in slots.items() if bin(slot).count("1") == steps]


def put_rows(slots, extra):
    count = lax.axis_size("wide")
    index = lax.axis_index("wide")
    rows, cols = slots[0].shape
    whole = jnp.zeros((count * rows + extra.shape[0], cols), extra.dtype)
    whole = lax.dynamic_update_slice(whole, extra, (count * rows, 0))
    for slot, held in slots.items():
        whole = lax.dynamic_update_slice(whole, held, ((index ^ slot) * rows, 0))
    return whole


def rotate_half(values):
    half = HD // 2
    return jnp.concatenate([values[..., half:], values[..., :half]], axis=-1)


def turn(values, cosine, sine):
    shaped = values.reshape(values.shape[0], -1, HD)
    turned = shaped * cosine[:, None, :] + rotate_half(shaped) * sine[:, None, :]
    return turned.reshape(values.shape)


def pad_rows(rows, count):
    return jnp.concatenate([rows, jnp.zeros((count - rows.shape[0], rows.shape[1]), rows.dtype)])


def lanes_of(reduced):
    high, low = two_parts(reduced)
    return jnp.pad(
        jnp.concatenate([high, low], axis=1), ((0, 0), (0, EXTRA - 2 * reduced.shape[1]))
    )


def twice_low(rows):
    doubled = 2.0 * rows.astype(BF)
    return pad_rows(jnp.concatenate([doubled, doubled]), EXTRA)


def gram_of(left, right):
    return lax.dot_general(left, right, (((1,), (1,)), ((), ())), precision=PRECISE)


def turn_lanes(values, cosine, sine):
    lane = lax.broadcasted_iota(jnp.int32, values.shape, 1) % HD
    swapped = jnp.where(
        lane < HD // 2,
        pltpu.roll(values, 2 * HD - HD // 2, 1),
        pltpu.roll(values, HD // 2, 1),
    )
    return values * cosine + swapped * sine


def head_rows(pairs, low_side):
    rows = []
    for pair in pairs:
        lane = lax.broadcasted_iota(jnp.int32, pair.shape, 1)
        moved = pltpu.roll(pair, HD, 1)
        if low_side:
            rows.append(jnp.where(lane < HD, pair, 0.0))
            rows.append(jnp.where(lane < HD, moved, 0.0))
        else:
            rows.append(jnp.where(lane >= HD, moved, 0.0))
            rows.append(jnp.where(lane >= HD, pair, 0.0))
    return jnp.concatenate(rows, axis=0).astype(BF)


def pairs_of(columns, block):
    turned = jnp.concatenate([columns, columns], axis=0).T
    lane = lax.broadcasted_iota(jnp.int32, (block, 2 * HD), 1)
    out = []
    for pair in range(GROUP // 2):
        first = turned[2 * pair * block : (2 * pair + 1) * block]
        second = turned[(2 * pair + 1) * block : (2 * pair + 2) * block]
        out.append(jnp.where(lane < HD, first, second))
    return out


def forward_kernel(
    first_ref, z_ref, scale_ref, cos_ref, sin_ref, place_ref, start_ref, kv_ref, kvt_ref,
    query_ref, out_ref, log_ref, *, block, span, groups,
):
    rows = GROUP * block
    width = GROUP * HD

    def chunk_body(chunk, carry):
        at = pl.ds(pl.multiple_of(chunk * block, block), block)
        cosine = cos_ref[at, :]
        sine = sin_ref[at, :]
        query_rows = []
        for group in range(groups):
            pairs = []
            for pair in range(GROUP // 2):
                lanes = slice(group * width + pair * 2 * HD, group * width + (pair + 1) * 2 * HD)
                turned = turn_lanes(z_ref[at, lanes] * scale_ref[:, lanes], cosine, sine)
                low = turned.astype(BF)
                query_ref[at, lanes] = low
                pairs.append(low.astype(F32) * HD**-0.5)
            query_rows.append(head_rows(pairs, True))
        place = place_ref[chunk]
        start = start_ref[chunk]

        def key_body(step, state):
            key_block = chunk - step
            keys = pl.ds(pl.multiple_of(key_block * span, span), span)
            spot = key_block * span + lax.broadcasted_iota(jnp.int32, (span, rows), 0)
            allowed = (spot <= place) & (spot >= start)
            out = []
            all_scores = [
                lax.dot_general(
                    kv_ref[keys, group * 2 * HD : (group + 1) * 2 * HD], query_rows[group], NT, preferred_element_type=F32
                )
                for group in range(groups)
            ]
            for group in range(groups):
                peak, total, mixed = state[group]
                scores = jnp.where(allowed, all_scores[group], MASKED)
                peak_new = jnp.maximum(peak, jnp.max(scores, axis=0, keepdims=True))
                powers = jnp.exp(scores - peak_new)
                shrink = jnp.exp(peak - peak_new)
                total = total * shrink + jnp.sum(powers, axis=0, keepdims=True)
                mixed = mixed * shrink + jnp.dot(
                    kvt_ref[group, HD:, keys], powers.astype(BF), preferred_element_type=F32
                )
                out.append((peak_new, total, mixed))
            return tuple(out)

        start_state = tuple(
            (
                jnp.full((1, rows), MASKED, F32),
                jnp.zeros((1, rows), F32),
                jnp.zeros((HD, rows), F32),
            )
            for _ in range(groups)
        )
        state = lax.fori_loop(0, chunk + 1 - first_ref[chunk], key_body, start_state)
        for group in range(groups):
            peak, total, mixed = state[group]
            log_ref[group, chunk] = peak + jnp.log(total)
            for pair, value in enumerate(pairs_of(mixed / total, block)):
                low_lane = group * width + pair * 2 * HD
                out_ref[at, low_lane : low_lane + 2 * HD] = value.astype(BF)
        return carry

    lax.fori_loop(0, CHUNKS, chunk_body, 0)


def backward_kernel(
    first_ref, query_ref, cos_ref, sin_ref, place_ref, start_ref, kv_ref, kvt_ref, log_ref,
    out_ref, grad_ref, query_grad_ref, kv_grad_ref, sums, *, block, span, groups,
):
    rows = GROUP * block
    width = GROUP * HD
    sums[...] = jnp.zeros_like(sums)

    def chunk_body(chunk, carry):
        at = pl.ds(pl.multiple_of(chunk * block, block), block)
        tiles = []
        for group in range(groups):
            queries = []
            grads = []
            product_rows = []
            for pair in range(GROUP // 2):
                lanes = slice(group * width + pair * 2 * HD, group * width + (pair + 1) * 2 * HD)
                queries.append(query_ref[at, lanes].astype(F32) * HD**-0.5)
                grad = grad_ref[at, lanes].astype(F32)
                grads.append(grad)
                product = grad * out_ref[at, lanes].astype(F32)
                lane = lax.broadcasted_iota(jnp.int32, product.shape, 1)
                product_rows.append(jnp.where(lane < HD, product, 0.0))
                product_rows.append(jnp.where(lane >= HD, product, 0.0))
            inner = jnp.sum(jnp.concatenate(product_rows, axis=0).T, axis=0, keepdims=True)
            query_rows = head_rows(queries, True)
            grad_rows = head_rows(grads, False)
            tiles.append((query_rows, grad_rows, inner, log_ref[group, chunk]))
        place = place_ref[chunk]
        start = start_ref[chunk]

        def key_body(key_block, query_grads):
            keys = pl.ds(pl.multiple_of(key_block * span, span), span)
            spot = key_block * span + lax.broadcasted_iota(jnp.int32, (span, rows), 0)
            allowed = (spot <= place) & (spot >= start)
            out = []
            products = []
            for group in range(groups):
                query_rows, grad_rows, inner, log_total = tiles[group]
                kv = kv_ref[keys, group * 2 * HD : (group + 1) * 2 * HD]
                products.append(
                    (
                        lax.dot_general(kv, query_rows, NT, preferred_element_type=F32),
                        lax.dot_general(kv, grad_rows, NT, preferred_element_type=F32),
                    )
                )
            for group in range(groups):
                query_rows, grad_rows, inner, log_total = tiles[group]
                scores, grad_weights = products[group]
                weights = jnp.exp(jnp.where(allowed, scores - log_total, MASKED))
                grad_scores = (weights * (grad_weights - inner)).astype(BF)
                sums[group, keys, :] += jnp.dot(
                    grad_scores, query_rows, preferred_element_type=F32
                ) + jnp.dot(weights.astype(BF), grad_rows, preferred_element_type=F32)
                out.append(
                    query_grads[group]
                    + jnp.dot(kvt_ref[group, :HD, keys], grad_scores, preferred_element_type=F32)
                )
            return tuple(out)

        query_grads = lax.fori_loop(
            first_ref[chunk],
            chunk + 1,
            key_body,
            tuple(jnp.zeros((HD, rows), F32) for _ in range(groups)),
        )
        cosine = cos_ref[at, :]
        sine = sin_ref[at, :]
        for group in range(groups):
            for pair, value in enumerate(pairs_of(query_grads[group] * HD**-0.5, block)):
                low_lane = group * width + pair * 2 * HD
                query_grad_ref[at, low_lane : low_lane + 2 * HD] = turn_lanes(
                    value, cosine, -sine
                )
        return carry

    lax.fori_loop(0, CHUNKS, chunk_body, 0)
    for group in range(groups):
        kv_grad_ref[:, group * 2 * HD : (group + 1) * 2 * HD] = sums[group].astype(BF)


def attend(first_block, z, scale, cosine, sine, places, starts, kv, kvt):
    count = z.shape[0]
    block = count // CHUNKS
    length = kv.shape[0]
    span = length // CHUNKS
    rows = GROUP * block
    width = FWD * GROUP * HD
    grid_spec = pltpu.PrefetchScalarGridSpec(
        num_scalar_prefetch=1,
        grid=(KVH // FWD,),
        in_specs=[
            pl.BlockSpec((count, width), lambda g, s: (0, g)),
            pl.BlockSpec((1, width), lambda g, s: (0, g)),
            pl.BlockSpec((count, 2 * HD), lambda g, s: (0, 0)),
            pl.BlockSpec((count, 2 * HD), lambda g, s: (0, 0)),
            pl.BlockSpec((CHUNKS, 1, rows), lambda g, s: (0, 0, 0)),
            pl.BlockSpec((CHUNKS, 1, rows), lambda g, s: (0, 0, 0)),
            pl.BlockSpec((length, FWD * 2 * HD), lambda g, s: (0, g)),
            pl.BlockSpec((FWD, 2 * HD, length), lambda g, s: (g, 0, 0)),
        ],
        out_specs=[
            pl.BlockSpec((count, width), lambda g, s: (0, g)),
            pl.BlockSpec((count, width), lambda g, s: (0, g)),
            pl.BlockSpec((FWD, CHUNKS, 1, rows), lambda g, s: (g, 0, 0, 0)),
        ],
    )
    return pl.pallas_call(
        functools.partial(forward_kernel, block=block, span=span, groups=FWD),
        grid_spec=grid_spec,
        out_shape=[
            jax.ShapeDtypeStruct((count, HEADS * HD), BF),
            jax.ShapeDtypeStruct((count, HEADS * HD), BF),
            jax.ShapeDtypeStruct((KVH, CHUNKS, 1, rows), F32),
        ],
        compiler_params=pltpu.CompilerParams(vmem_limit_bytes=40 << 20),
        cost_estimate=pl.CostEstimate(flops=40 << 30, bytes_accessed=64 << 20, transcendentals=0),
    )(first_block, z, scale, cosine, sine, places, starts, kv, kvt)


def attend_back(
    first_block, queries, cosine, sine, places, starts, kv, kvt, log_total, attended, grads
):
    count = queries.shape[0]
    block = count // CHUNKS
    length = kv.shape[0]
    span = length // CHUNKS
    rows = GROUP * block
    width = BWD * GROUP * HD
    grid_spec = pltpu.PrefetchScalarGridSpec(
        num_scalar_prefetch=1,
        grid=(KVH // BWD,),
        in_specs=[
            pl.BlockSpec((count, width), lambda g, s: (0, g)),
            pl.BlockSpec((count, 2 * HD), lambda g, s: (0, 0)),
            pl.BlockSpec((count, 2 * HD), lambda g, s: (0, 0)),
            pl.BlockSpec((CHUNKS, 1, rows), lambda g, s: (0, 0, 0)),
            pl.BlockSpec((CHUNKS, 1, rows), lambda g, s: (0, 0, 0)),
            pl.BlockSpec((length, BWD * 2 * HD), lambda g, s: (0, g)),
            pl.BlockSpec((BWD, 2 * HD, length), lambda g, s: (g, 0, 0)),
            pl.BlockSpec((BWD, CHUNKS, 1, rows), lambda g, s: (g, 0, 0, 0)),
            pl.BlockSpec((count, width), lambda g, s: (0, g)),
            pl.BlockSpec((count, width), lambda g, s: (0, g)),
        ],
        out_specs=[
            pl.BlockSpec((count, width), lambda g, s: (0, g)),
            pl.BlockSpec((length, BWD * 2 * HD), lambda g, s: (0, g)),
        ],
        scratch_shapes=[pltpu.VMEM((BWD, length, 2 * HD), F32)],
    )
    return pl.pallas_call(
        functools.partial(backward_kernel, block=block, span=span, groups=BWD),
        grid_spec=grid_spec,
        out_shape=[
            jax.ShapeDtypeStruct((count, HEADS * HD), F32),
            jax.ShapeDtypeStruct((length, KVH * 2 * HD), BF),
        ],
        compiler_params=pltpu.CompilerParams(vmem_limit_bytes=40 << 20),
        cost_estimate=pl.CostEstimate(flops=40 << 30, bytes_accessed=64 << 20, transcendentals=0),
    )(first_block, queries, cosine, sine, places, starts, kv, kvt, log_total, attended, grads)


def place_of(place_ref, slot, rows):
    return pl.multiple_of((place_ref[0] ^ slot) * rows, rows)


def half_place(place_ref, half, tiles, pair_tiles):
    return (place_ref[1] ^ half) * pair_tiles + tiles


def set_rows(outer, offset):
    rank, cols = outer.shape
    parts = [outer]
    if offset:
        parts = [jnp.zeros((offset, cols), outer.dtype)] + parts
    if EXTRA - rank - offset:
        parts = parts + [jnp.zeros((EXTRA - rank - offset, cols), outer.dtype)]
    return jnp.concatenate(parts, axis=0)


def split_parts(values):
    high = values.astype(BF)
    return high, (values - high.astype(F32)).astype(BF)


def low_rank(reduced, outer, offset):
    high, low = split_parts(reduced)
    rows = set_rows(2.0 * outer.astype(BF).astype(F32), offset).astype(BF)
    return jnp.dot(high, rows, preferred_element_type=F32) + jnp.dot(
        low, rows, preferred_element_type=F32
    )


def slot_kernel(place_ref, inputs_ref, first_ref, outer_ref, *refs, offset):
    slots, out_ref, reduced_ref = refs[:-2], refs[-2], refs[-1]
    each = len(slots) // 2
    rows = slots[0].shape[0]

    @pl.when((pl.program_id(0) == 0) & (pl.program_id(1) == 0))
    def _():
        reduced_ref[...] = jnp.dot(inputs_ref[...], first_ref[...], preferred_element_type=F32)

    def total(chosen):
        result = low_rank(reduced_ref[...], outer_ref[...], offset)
        for slot, ref in enumerate(chosen):
            result = result + jnp.dot(
                inputs_ref[:, pl.ds(place_of(place_ref, slot, rows), rows)],
                ref[...],
                preferred_element_type=F32,
            )
        out_ref[...] = result

    for half in range(2):

        @pl.when(pl.program_id(0) == half)
        def _():
            total(slots[half * each : (half + 1) * each])


def slot_mm(place, inputs, first, outer, offset, slots, skip=0, tile=256):
    rows = slots[0][0].shape[0]
    cols = outer.shape[1]
    tiles = cols // 2 // tile

    def held(half):
        def spot(h, n, s):
            return (0, skip // tile + jnp.where(h == half, n, (tiles - 1) * (1 - half)))

        return pl.BlockSpec((rows, tile), spot)

    return pl.pallas_call(
        functools.partial(slot_kernel, offset=offset),
        grid_spec=pltpu.PrefetchScalarGridSpec(
            num_scalar_prefetch=1,
            grid=(2, tiles),
            in_specs=[
                pl.BlockSpec(inputs.shape, lambda h, n, s: (0, 0)),
                pl.BlockSpec(first.shape, lambda h, n, s: (0, 0)),
                pl.BlockSpec(
                    (outer.shape[0], tile), lambda h, n, s: (0, half_place(s, h, n, tiles))
                ),
            ]
            + [held(half) for half in range(2) for _ in slots[half]],
            out_specs=[
                pl.BlockSpec(
                    (inputs.shape[0], tile), lambda h, n, s: (0, half_place(s, h, n, tiles))
                ),
                pl.BlockSpec((inputs.shape[0], EXTRA), lambda h, n, s: (0, 0)),
            ],
        ),
        out_shape=[
            jax.ShapeDtypeStruct((inputs.shape[0], cols), F32),
            jax.ShapeDtypeStruct((inputs.shape[0], EXTRA), F32),
        ],
        compiler_params=pltpu.CompilerParams(vmem_limit_bytes=40 << 20),
        cost_estimate=pl.CostEstimate(flops=COST, bytes_accessed=COST, transcendentals=0),
    )(place, inputs, first, outer, *slots[0], *slots[1])


def finish_kernel(*refs, count, sizes, offset, summed):
    raws = refs[: len(sizes)]
    narrow_ref, middle_ref, first_ref, inputs_ref, grad_ref, out_ref = refs[len(sizes) :]
    first = first_ref[...]
    narrow_high, narrow_low = split_parts(narrow_ref[...])
    total = lax.dot_general(narrow_high, first, NT, preferred_element_type=F32)
    total = total + lax.dot_general(narrow_low, first, NT, preferred_element_type=F32)
    weighted = []
    for ref, size in zip(raws, sizes):
        total = total + ref[:count, :]
        weighted.append(ref[count : count + size, :] + ref[count + size :, :])
    grad_ref[...] = total
    weighted = sum(weighted) if summed else jnp.concatenate(weighted, axis=0)
    middle_high, middle_low = split_parts(middle_ref[...])
    middle = lax.dot_general(middle_high, first, NT, preferred_element_type=F32)
    middle = middle + lax.dot_general(middle_low, first, NT, preferred_element_type=F32)
    under = (((0,), (0,)), ((), ()))
    inputs = inputs_ref[...]
    product = lax.dot_general(narrow_high, inputs, under, preferred_element_type=F32)
    product = product + lax.dot_general(narrow_low, inputs, under, preferred_element_type=F32)
    out_ref[...] = (
        product[offset : offset + weighted.shape[0]] + 2.0 * (weighted + 2.0 * middle)
    )


def finish_back(raws, sizes, narrow, middle, first, inputs, offset, summed=False, tile=512):
    count = inputs.shape[0]
    rank = middle.shape[0]
    tiled = lambda rows: pl.BlockSpec((rows, tile), lambda n: (0, n))
    return pl.pallas_call(
        functools.partial(
            finish_kernel, count=count, sizes=sizes, offset=offset, summed=summed
        ),
        grid=(D // tile,),
        in_specs=[tiled(raw.shape[0]) for raw in raws]
        + [
            pl.BlockSpec(narrow.shape, lambda n: (0, 0)),
            pl.BlockSpec(middle.shape, lambda n: (0, 0)),
            pl.BlockSpec((tile, EXTRA), lambda n: (n, 0)),
            tiled(count),
        ],
        out_specs=[tiled(count), tiled(rank)],
        out_shape=[
            jax.ShapeDtypeStruct((count, D), F32),
            jax.ShapeDtypeStruct((rank, D), F32),
        ],
        compiler_params=pltpu.CompilerParams(vmem_limit_bytes=40 << 20),
        cost_estimate=pl.CostEstimate(flops=COST, bytes_accessed=COST, transcendentals=0),
    )(*raws, narrow, middle, first, inputs)


def slot_back_kernel(place_ref, grad_ref, *refs, skip):
    slots, out_ref, held, arrived = refs[:-3], refs[-3], refs[-2], refs[-1]
    each = len(slots) // 2
    rows, cols = held.shape[1:]
    copies = [
        pltpu.make_async_copy(ref.at[:, pl.ds(skip, cols)], held.at[slot], arrived.at[slot])
        for slot, ref in enumerate(slots)
    ]
    for slot in range(each):
        copies[slot].start()
        copies[each + slot].start()
    grads = [
        grad_ref[:, pl.ds(pl.multiple_of((place_ref[1] ^ half) * cols, cols), cols)]
        for half in range(2)
    ]
    for slot in range(each):
        copies[slot].wait()
        copies[each + slot].wait()
        out_ref[:, pl.ds(place_of(place_ref, slot, rows), rows)] = lax.dot_general(
            grads[0], held[slot], NT, preferred_element_type=F32
        ) + lax.dot_general(grads[1], held[each + slot], NT, preferred_element_type=F32)


def slot_back(place, grads, slots, skip=0):
    rows = slots[0][0].shape[0]
    count, cols = grads.shape
    many = 2 * len(slots[0])
    return pl.pallas_call(
        functools.partial(slot_back_kernel, skip=skip),
        grid_spec=pltpu.PrefetchScalarGridSpec(
            num_scalar_prefetch=1,
            grid=(1,),
            in_specs=[pl.BlockSpec((count, cols), lambda n, s: (0, 0))]
            + [pl.BlockSpec(memory_space=pl.ANY) for _ in range(many)],
            out_specs=pl.BlockSpec((count, D), lambda n, s: (0, 0)),
            scratch_shapes=[
                pltpu.VMEM((many, rows, cols // 2), BF),
                pltpu.SemaphoreType.DMA((many,)),
            ],
        ),
        out_shape=jax.ShapeDtypeStruct((count, D), F32),
        compiler_params=pltpu.CompilerParams(vmem_limit_bytes=40 << 20),
        cost_estimate=pl.CostEstimate(flops=COST, bytes_accessed=COST, transcendentals=0),
    )(place, grads, *slots[0], *slots[1])


def pad_to(rows, count):
    return jnp.concatenate([rows, jnp.zeros((count - rows.shape[0], rows.shape[1]), rows.dtype)])


def split_rows(weighted):
    high = weighted.astype(BF)
    return high, (weighted - high.astype(F32)).astype(BF)


def terms_of(grads_low, weighted, outer, reduced, offset):
    rank = outer.shape[0]
    rows = set_rows(outer, offset)
    narrow = 2.0 * lax.dot_general(grads_low, rows.astype(BF), NT, preferred_element_type=F32)
    middle = lax.dot_general(weighted, rows, NT, precision=PRECISE, preferred_element_type=F32)
    own = lax.broadcasted_iota(jnp.int32, middle.shape, 0) // RANK + offset // RANK
    middle = jnp.where(
        lax.broadcasted_iota(jnp.int32, middle.shape, 1) // RANK == own, middle, 0.0
    )
    under = (((0,), (0,)), ((), ()))
    high, low = split_parts(reduced)
    both = lax.dot_general(high, grads_low, under, preferred_element_type=F32)
    both = both + lax.dot_general(low, grads_low, under, preferred_element_type=F32)
    return narrow, middle, 2.0 * both[offset : offset + rank]


def terms_kernel(
    grad_ref, z_ref, scale_ref, slope_ref, outer_ref, reduced_ref,
    rows_ref, sum_ref, product_ref, narrow_ref, middle_ref, *, offset,
):
    count = grad_ref.shape[0]
    rank = outer_ref.shape[0]
    grads = grad_ref[...]
    sums = jnp.sum(grads * z_ref[...], axis=0, keepdims=True)
    sum_ref[...] = sums
    low = (grads * scale_ref[...]).astype(BF)
    weighted = (sums * slope_ref[...]) * outer_ref[...]
    high_part, low_part = split_rows(weighted)
    rows_ref[:count, :] = low
    rows_ref[count : count + rank, :] = high_part
    rows_ref[count + rank :, :] = low_part
    narrow, middle, product = terms_of(
        low, weighted, outer_ref[...], reduced_ref[...], offset
    )
    product_ref[...] = product

    @pl.when(pl.program_id(0) == 0)
    def _():
        narrow_ref[...] = narrow
        middle_ref[...] = middle

    @pl.when(pl.program_id(0) > 0)
    def _():
        narrow_ref[...] += narrow
        middle_ref[...] += middle


def grad_terms(grads, z, scale, slope, outer, offset, reduced, tile=512):
    count, cols = grads.shape
    rank = outer.shape[0]
    tiled = lambda rows: pl.BlockSpec((rows, tile), lambda n: (0, n))
    fixed = lambda rows, width: pl.BlockSpec((rows, width), lambda n: (0, 0))
    return pl.pallas_call(
        functools.partial(terms_kernel, offset=offset),
        grid=(cols // tile,),
        in_specs=[
            tiled(count), tiled(count), tiled(1), tiled(1), tiled(rank),
            fixed(count, reduced.shape[1]),
        ],
        out_specs=[
            tiled(count + 2 * rank), tiled(1), tiled(rank), fixed(count, EXTRA), fixed(rank, EXTRA),
        ],
        out_shape=[
            jax.ShapeDtypeStruct((count + 2 * rank, cols), BF),
            jax.ShapeDtypeStruct((1, cols), F32),
            jax.ShapeDtypeStruct((rank, cols), F32),
            jax.ShapeDtypeStruct((count, EXTRA), F32),
            jax.ShapeDtypeStruct((rank, EXTRA), F32),
        ],
        compiler_params=pltpu.CompilerParams(vmem_limit_bytes=40 << 20),
        cost_estimate=pl.CostEstimate(flops=COST, bytes_accessed=COST, transcendentals=0),
    )(grads, z, scale, slope, outer, reduced)


def pack_kernel(inputs_ref, first_ref, out_ref, turned_ref, *, offset, rank):
    reduced = jnp.dot(inputs_ref[...], first_ref[...], preferred_element_type=F32)
    high, low = split_parts(reduced)
    pick = lambda part: part.astype(F32)[:, offset : offset + rank]
    count = inputs_ref.shape[0]
    packed = jnp.concatenate(
        [pick(high), pick(low), jnp.zeros((count, EXTRA - 2 * rank), F32)], axis=1
    )
    out_ref[...] = packed.astype(BF)
    turned_ref[...] = packed.T.astype(BF)


def pack_reduced(inputs, first, offset, rank):
    count = inputs.shape[0]
    return pl.pallas_call(
        functools.partial(pack_kernel, offset=offset, rank=rank),
        out_shape=[
            jax.ShapeDtypeStruct((count, EXTRA), BF),
            jax.ShapeDtypeStruct((EXTRA, count), BF),
        ],
        cost_estimate=pl.CostEstimate(flops=COST, bytes_accessed=COST, transcendentals=0),
    )(inputs, first)


def mlp_kernel(
    place_ref, inputs_ref, packed_ref, turned_ref, scale_ref, slope_ref, outer_ref,
    down_grad_ref, narrow_down_ref, first_ref, down_ref, *refs, offset,
):
    slots, kept = refs[:-8], refs[-8:]
    hidden_ref, rows_ref, sum_ref, product_ref, narrow_ref, middle_ref, z_ref, back_ref = kept
    rows = slots[0].shape[0]
    half = hidden_ref.shape[1]
    count = hidden_ref.shape[0]
    gate_lanes = lax.broadcasted_iota(jnp.int32, (RANK, 2 * half), 1) < half
    outer = jnp.concatenate(
        [
            jnp.where(gate_lanes, outer_ref[...], 0.0),
            jnp.where(gate_lanes, 0.0, outer_ref[...]),
        ],
        axis=0,
    )
    rank = outer.shape[0]
    doubled = 2.0 * outer.astype(BF).astype(F32)
    pad = jnp.zeros((EXTRA - 2 * rank, 2 * half), F32)
    z = jnp.dot(
        packed_ref[...],
        jnp.concatenate([doubled, doubled, pad], axis=0).astype(BF),
        preferred_element_type=F32,
    )
    for slot, ref in enumerate(slots):
        z = z + jnp.dot(
            inputs_ref[:, pl.ds(place_of(place_ref, slot, rows), rows)],
            ref[...],
            preferred_element_type=F32,
        )
    z_ref[...] = z
    back_ref[...] = lax.dot_general(
        down_grad_ref[...], down_ref[...], NT, preferred_element_type=F32
    ) + lax.dot_general(narrow_down_ref[...], first_ref[...], NT, preferred_element_type=F32)
    scale = scale_ref[...]
    step = 64
    gate_sums = jnp.zeros((8, half), F32)
    up_sums = jnp.zeros((8, half), F32)

    def eighth(values):
        return jnp.sum(values.reshape(step // 8, 8, half), axis=0)

    for begin in range(0, count, step):
        at = slice(begin, begin + step)
        gate_z, up_z = z_ref[at, :half], z_ref[at, half:]
        grad_hidden = back_ref[at, :]
        gate = gate_z * scale[:, :half]
        up = up_z * scale[:, half:]
        sigmoid = 0.5 * jnp.tanh(0.5 * gate) + 0.5
        silu = gate * sigmoid
        hidden_ref[at, :] = (silu * up).astype(BF)
        grad_up = grad_hidden * silu
        grad_gate = grad_hidden * up * (sigmoid + silu * (1.0 - sigmoid))
        gate_sums = gate_sums + eighth(grad_gate * gate_z)
        up_sums = up_sums + eighth(grad_up * up_z)
        rows_ref[at, :half] = (grad_gate * scale[:, :half]).astype(BF)
        rows_ref[at, half:] = (grad_up * scale[:, half:]).astype(BF)
    sums = jnp.concatenate(
        [
            jnp.sum(gate_sums, axis=0, keepdims=True),
            jnp.sum(up_sums, axis=0, keepdims=True),
        ],
        axis=1,
    )
    sum_ref[...] = sums
    low = rows_ref[:count, :]
    weighted = (sums * slope_ref[...]) * outer
    high_part, low_part = split_rows(weighted)
    rows_ref[count : count + rank, :] = high_part
    rows_ref[count + rank :, :] = low_part
    placed = set_rows(outer, offset)
    narrow = 2.0 * lax.dot_general(low, placed.astype(BF), NT, preferred_element_type=F32)
    middle = lax.dot_general(weighted, placed, NT, precision=PRECISE, preferred_element_type=F32)
    both = jnp.dot(turned_ref[...], low, preferred_element_type=F32)
    product = 2.0 * (both[:rank] + both[rank : 2 * rank])
    product_ref[:, :half] = product[: rank // 2, :half]
    product_ref[:, half:] = product[rank // 2 :, half:]

    @pl.when(pl.program_id(0) == 0)
    def _():
        narrow_ref[...] = narrow
        middle_ref[...] = middle

    @pl.when(pl.program_id(0) > 0)
    def _():
        narrow_ref[...] += narrow
        middle_ref[...] += middle


def mlp_block(
    place, inputs, packs, offset, scale, slope, outer, down_grad, narrow_down, down, slots, start
):
    rows, cols = slots[0].shape
    count = inputs.shape[0]
    rank = 2 * RANK
    tile = 256
    skip = start // tile
    fixed = lambda array: pl.BlockSpec(array.shape, lambda n, s: (0, 0))
    tiled = lambda rows: pl.BlockSpec((rows, tile), lambda n, s: (0, n))
    late = lambda rows: pl.BlockSpec((rows, tile), lambda n, s: (0, n + skip))
    kept = lambda rows: pl.BlockSpec((rows, EXTRA), lambda n, s: (0, 0))
    return pl.pallas_call(
        functools.partial(mlp_kernel, offset=offset),
        grid_spec=pltpu.PrefetchScalarGridSpec(
            num_scalar_prefetch=1,
            grid=(cols // tile,),
            in_specs=[
                fixed(inputs), fixed(packs[0]), fixed(packs[1]), late(1), late(1), late(RANK),
                fixed(down_grad), fixed(narrow_down),
                pl.BlockSpec((tile // 2, 128), lambda n, s: (n + skip, D // 128)),
                pl.BlockSpec((tile // 2, D), lambda n, s: (n + skip, 0)),
            ]
            + [tiled(rows) for _ in slots],
            out_specs=[
                pl.BlockSpec((count, tile // 2), lambda n, s: (0, n)),
                tiled(count + 2 * rank),
                tiled(1),
                tiled(RANK),
                kept(count),
                kept(rank),
            ],
            scratch_shapes=[
                pltpu.VMEM((count, tile), F32),
                pltpu.VMEM((count, tile // 2), F32),
            ],
        ),
        out_shape=[
            jax.ShapeDtypeStruct((count, cols // 2), BF),
            jax.ShapeDtypeStruct((count + 2 * rank, cols), BF),
            jax.ShapeDtypeStruct((1, cols), F32),
            jax.ShapeDtypeStruct((RANK, cols), F32),
            jax.ShapeDtypeStruct((count, EXTRA), F32),
            jax.ShapeDtypeStruct((rank, EXTRA), F32),
        ],
        compiler_params=pltpu.CompilerParams(vmem_limit_bytes=48 << 20),
        cost_estimate=pl.CostEstimate(flops=COST, bytes_accessed=COST, transcendentals=0),
    )(place, inputs, *packs, scale, slope, outer, down_grad, narrow_down, down, down, *slots)


def down_kernel(*refs, bounds):
    hiddens, (weights_ref, first_ref, outer_ref) = refs[:-6], refs[-6:-3]
    keep_ref, send_ref, reduced_ref = refs[-3:]

    @pl.when(pl.program_id(0) == 0)
    def _():
        reduced_ref[...] = jnp.zeros_like(reduced_ref)
        for (start, stop), ref in zip(bounds, hiddens):
            reduced_ref[...] += jnp.dot(
                ref[...], first_ref[start:stop, :], preferred_element_type=F32
            )

    lane = lax.broadcasted_iota(jnp.int32, reduced_ref.shape, 1)
    total = low_rank(jnp.where(lane < RANK, reduced_ref[...], 0.0), outer_ref[...], 0)
    for (start, stop), ref in zip(bounds, hiddens):
        total = total + jnp.dot(
            ref[...], weights_ref[start:stop, :], preferred_element_type=F32
        )
    count = keep_ref.shape[0]
    keep_ref[...] = total[:count]
    send_ref[...] = total[count:].astype(BF)


def down_forward(hiddens, bounds, down, outer, tile=256):
    count = hiddens[0].shape[0]
    rows = down.shape[0]
    return pl.pallas_call(
        functools.partial(down_kernel, bounds=bounds),
        grid=(D // tile,),
        in_specs=[pl.BlockSpec(hidden.shape, lambda n: (0, 0)) for hidden in hiddens]
        + [
            pl.BlockSpec((rows, tile), lambda n: (0, n)),
            pl.BlockSpec((rows, EXTRA), lambda n: (0, D // EXTRA)),
            pl.BlockSpec((RANK, tile), lambda n: (0, n)),
        ],
        out_specs=[
            pl.BlockSpec((count // 2, tile), lambda n: (0, n)),
            pl.BlockSpec((count // 2, tile), lambda n: (0, n)),
            pl.BlockSpec((count, EXTRA), lambda n: (0, 0)),
        ],
        out_shape=[
            jax.ShapeDtypeStruct((count // 2, D), F32),
            jax.ShapeDtypeStruct((count // 2, D), BF),
            jax.ShapeDtypeStruct((count, EXTRA), F32),
        ],
        compiler_params=pltpu.CompilerParams(vmem_limit_bytes=40 << 20),
        cost_estimate=pl.CostEstimate(flops=COST, bytes_accessed=COST, transcendentals=0),
    )(*hiddens, down, down, outer)


def kv_form_kernel(z_ref, scale_ref, cos_ref, sin_ref, out_ref):
    lane = lax.broadcasted_iota(jnp.int32, cos_ref.shape, 1)
    half = z_ref.shape[1] // 2
    for pair in range(half // 128):
        at = slice(pair * 128, (pair + 1) * 128)
        to = slice(half + pair * 128, half + (pair + 1) * 128)
        keys = turn_lanes(z_ref[:, at] * scale_ref[:, at], cos_ref[...], sin_ref[...])
        values = z_ref[:, to] * scale_ref[:, to]
        first = jnp.where(lane < HD, keys, pltpu.roll(values, HD, 1))
        second = jnp.where(lane < HD, pltpu.roll(keys, HD, 1), values)
        out_ref[:, 2 * pair * 128 : (2 * pair + 1) * 128] = first.astype(BF)
        out_ref[:, (2 * pair + 1) * 128 : (2 * pair + 2) * 128] = second.astype(BF)


def kv_form(z, scale, cosine, sine):
    return pl.pallas_call(
        kv_form_kernel,
        out_shape=jax.ShapeDtypeStruct(z.shape, BF),
        cost_estimate=pl.CostEstimate(flops=COST, bytes_accessed=COST, transcendentals=0),
    )(z, scale, cosine, sine)


def kv_back_kernel(sum_ref, cos_ref, sin_ref, out_ref):
    lane = lax.broadcasted_iota(jnp.int32, cos_ref.shape, 1)
    half = sum_ref.shape[1] // 2
    for pair in range(half // 128):
        first = sum_ref[:, 2 * pair * 128 : (2 * pair + 1) * 128].astype(F32)
        second = sum_ref[:, (2 * pair + 1) * 128 : (2 * pair + 2) * 128].astype(F32)
        keys = jnp.where(lane < HD, first, pltpu.roll(second, HD, 1))
        values = jnp.where(lane < HD, pltpu.roll(first, HD, 1), second)
        out_ref[:, pair * 128 : (pair + 1) * 128] = turn_lanes(keys, cos_ref[...], -sin_ref[...])
        out_ref[:, half + pair * 128 : half + (pair + 1) * 128] = values


def kv_back(sums, cosine, sine):
    return pl.pallas_call(
        kv_back_kernel,
        out_shape=jax.ShapeDtypeStruct(sums.shape, F32),
        cost_estimate=pl.CostEstimate(flops=COST, bytes_accessed=COST, transcendentals=0),
    )(sums, cosine, sine)


def pack_all_kernel(
    query_ref, kv_ref, out_ref_, mlp_ref, down_ref, one_ref, first_out_ref, pairs_ref, down_first_ref,
    place_ref, packed_ref, wide_rows, hold, down_rows, *, toks, part, layout,
):
    tall, low, lanes, share, hidden_share, outer_share = layout
    many = wide_rows.shape[0]
    wides = packed_ref.shape[0] // toks
    for n, ref in ((0, query_ref), (1, kv_ref), (3, out_ref_), (6, down_ref)):
        wide_rows[: RANK + 1, STARTS[n] : STARTS[n] + ref.shape[1]] = ref[...]
    blocks = FF // (4 * part)
    down_rows[...] = jnp.zeros_like(down_rows)
    for side in range(2):
        start = STARTS[4 + side]
        wide_rows[:, start : start + FF] = jnp.zeros((many, FF), F32)
        for tile in range(blocks * part // 128):
            hold[: RANK + 1, tile * 128 : (tile + 1) * 128] = mlp_ref[
                :, (2 * tile + side) * 128 : (2 * tile + side + 1) * 128
            ]
        for quarter in range(4):

            @pl.when(place_ref[2] == quarter)
            def _():
                for at in range(blocks):
                    to = start + (at * 4 + quarter) * part
                    wide_rows[: RANK + 1, to : to + part] = hold[
                        : RANK + 1, at * part : (at + 1) * part
                    ]
    for quarter in range(4):

        @pl.when(place_ref[2] == quarter)
        def _():
            for at in range(blocks):
                to = (at * 4 + quarter) * part
                down_rows[:, to : to + part] = down_first_ref[:, at * part : (at + 1) * part]

    packed_ref[...] = jnp.zeros_like(packed_ref)
    sources = [(0, one_ref), (3 * RANK, first_out_ref), (4 * RANK, pairs_ref)]

    def main_piece(start, rows, cols):
        parts = []
        while rows:
            base, ref = [pair for pair in sources if pair[0] <= start][-1]
            here = min(rows, base + ref.shape[0] - start)
            parts.append(ref[start - base : start - base + here, cols])
            start, rows = start + here, rows - here
        return parts[0] if len(parts) == 1 else jnp.concatenate(parts, axis=0)

    fit = lanes // share
    for tok in range(toks):
        for wide in range(wides):
            at = tok * wides + wide
            cols = slice(wide * share, (wide + 1) * share)
            for piece in range(fit):
                packed_ref[at, :tall, piece * share : (piece + 1) * share] = main_piece(
                    (tok * fit + piece) * tall, tall, cols
                )
            packed_ref[at, tall : tall + low, :hidden_share] = down_rows[
                tok * low : (tok + 1) * low, wide * hidden_share : (wide + 1) * hidden_share
            ]
            packed_ref[at, tall + low : tall + low + RANK + 1, :outer_share] = wide_rows[
                : RANK + 1, at * outer_share : (at + 1) * outer_share
            ]


def pack_all(place, pieces, toks, part, layout):
    tall, low, lanes, share, hidden_share, outer_share = layout
    owners = OUTS // outer_share
    rows = -(-(tall + low + RANK + 1) // 8) * 8
    fixed = lambda array: pl.BlockSpec(array.shape, lambda *n: (0,) * array.ndim)
    shape = jax.ShapeDtypeStruct((owners, rows, lanes), F32)
    return pl.pallas_call(
        functools.partial(pack_all_kernel, toks=toks, part=part, layout=layout),
        grid=(1,),
        in_specs=[fixed(piece) for piece in pieces]
        + [pl.BlockSpec(memory_space=pltpu.SMEM)],
        out_specs=fixed(shape),
        out_shape=shape,
        scratch_shapes=[
            pltpu.VMEM((RANK + 8, OUTS), F32),
            pltpu.VMEM((RANK + 8, FF // 4), F32),
            pltpu.VMEM((RANK, FF), F32),
        ],
        compiler_params=pltpu.CompilerParams(vmem_limit_bytes=40 << 20),
        cost_estimate=pl.CostEstimate(flops=COST, bytes_accessed=COST, transcendentals=0),
    )(*pieces, place)


def mlp_back_kernel(
    place_ref, one_ref, two_ref, narrow_ref, middle_ref, first_ref, inputs_ref, *refs, offset, rank
):
    slots, (keep_ref, send_ref, out_ref, held_one, held_two, arrived) = refs[:-6], refs[-6:]
    each = len(slots) // 2
    rows = held_one.shape[1]
    count = inputs_ref.shape[0]
    copies = []
    for half, held in enumerate((held_one, held_two)):
        copies.append(
            [
                pltpu.make_async_copy(slots[half * each + i], held.at[i], arrived.at[half * each + i])
                for i in range(each)
            ]
        )
    for i in range(each):
        copies[0][i].start()
        copies[1][i].start()
    narrow_high, narrow_low = split_parts(narrow_ref[...])
    turned_high = narrow_high.astype(F32).T.astype(BF)
    turned_low = narrow_low.astype(F32).T.astype(BF)
    middle_high, middle_low = split_parts(middle_ref[...])
    for i in range(each):
        copies[0][i].wait()
        copies[1][i].wait()
        at = pl.ds(place_of(place_ref, i, rows), rows)
        first = first_ref[at, :]
        total = lax.dot_general(one_ref[...], held_one[i], NT, preferred_element_type=F32)
        total = total + lax.dot_general(two_ref[...], held_two[i], NT, preferred_element_type=F32)
        grad = (
            total[:count]
            + lax.dot_general(narrow_high, first, NT, preferred_element_type=F32)
            + lax.dot_general(narrow_low, first, NT, preferred_element_type=F32)
        )
        keep_ref[:, at] = grad[: count // 2]
        send_ref[:, at] = grad[count // 2 :].astype(BF)
        weighted = total[count : count + rank] + total[count + rank :]
        middle = lax.dot_general(middle_high, first, NT, preferred_element_type=F32)
        middle = middle + lax.dot_general(middle_low, first, NT, preferred_element_type=F32)
        inputs = inputs_ref[:, at]
        product = jnp.dot(turned_high, inputs, preferred_element_type=F32)
        product = product + jnp.dot(turned_low, inputs, preferred_element_type=F32)
        out_ref[:, at] = product[offset : offset + rank] + 2.0 * (weighted + 2.0 * middle)


def mlp_back(place, grads, narrow, middle, first, inputs, slots, offset):
    count = inputs.shape[0]
    rank = middle.shape[0]
    rows = slots[0][0].shape[0]
    many = len(slots[0])
    operands = [*grads, narrow, middle, first, inputs]
    fixed = lambda array: pl.BlockSpec(array.shape, lambda n, s: (0, 0))
    shapes = [
        jax.ShapeDtypeStruct((count // 2, D), F32),
        jax.ShapeDtypeStruct((count // 2, D), BF),
        jax.ShapeDtypeStruct((rank, D), F32),
    ]
    return pl.pallas_call(
        functools.partial(mlp_back_kernel, offset=offset, rank=rank),
        grid_spec=pltpu.PrefetchScalarGridSpec(
            num_scalar_prefetch=1,
            grid=(1,),
            in_specs=[fixed(array) for array in operands]
            + [pl.BlockSpec(memory_space=pl.ANY) for _ in range(2 * many)],
            out_specs=[fixed(shape) for shape in shapes],
            scratch_shapes=[
                pltpu.VMEM((many, rows, grads[0].shape[1]), BF),
                pltpu.VMEM((many, rows, grads[1].shape[1]), BF),
                pltpu.SemaphoreType.DMA((2 * many,)),
            ],
        ),
        out_shape=shapes,
        compiler_params=pltpu.CompilerParams(vmem_limit_bytes=60 << 20),
        cost_estimate=pl.CostEstimate(flops=COST, bytes_accessed=COST, transcendentals=0),
    )(place, *operands, *slots[0], *slots[1])


def column_sums(base, first_high, first_low, outer, offset):
    outer_high, outer_low = split_parts(set_rows(outer, offset))
    product = (
        jnp.dot(first_high, outer_high, preferred_element_type=F32)
        + jnp.dot(first_high, outer_low, preferred_element_type=F32)
        + jnp.dot(first_low, outer_high, preferred_element_type=F32)
    )
    merged = base.astype(F32) + 2.0 * product
    merged_high, merged_low = split_parts(merged)
    under = (((0,), (0,)), ((), ()))
    cross = (
        lax.dot_general(first_high, merged_high, under, preferred_element_type=F32)
        + lax.dot_general(first_high, merged_low, under, preferred_element_type=F32)
        + lax.dot_general(first_low, merged_high, under, preferred_element_type=F32)
    )
    return jnp.sum(merged * merged, axis=0, keepdims=True), cross[offset : offset + RANK]


def widened(first):
    return jnp.concatenate(
        [first, jnp.zeros((first.shape[0], EXTRA - first.shape[1]), first.dtype)], axis=1
    )


def early_kernel(
    place_ref, query_ref, key_ref, value_ref, main_ref, outer_ref, shard_out, square_ref, cross_ref,
):
    half = query_ref.shape[1] // 2
    kv_cols = key_ref.shape[1]
    high, low = split_parts(widened(main_ref[...]))
    shard_out[:, half + kv_cols :] = high
    for core in range(2):

        @pl.when(place_ref[1] == core)
        def _():
            shard_out[:, :half] = query_ref[:, core * half : (core + 1) * half]
            kv = (key_ref, value_ref)[core][...]
            shard_out[:, half : half + kv_cols] = kv
            start = 2 * half + core * kv_cols
            square, cross = column_sums(
                kv, high, low, outer_ref[:, start : start + kv_cols], (1 + core) * RANK
            )
            square_ref[:, :kv_cols] = square
            cross_ref[:, :kv_cols] = cross
            for tile in range(half // 256):
                at = core * half + tile * 256
                square, cross = column_sums(
                    query_ref[:, at : at + 256], high, low, outer_ref[:, at : at + 256], 0
                )
                to = kv_cols + tile * 256
                square_ref[:, to : to + 256] = square
                cross_ref[:, to : to + 256] = cross


def early_work(place, query, key, value, main, outer):
    rows, cols = query.shape
    kv_cols = key.shape[1]
    fixed = lambda array: pl.BlockSpec(array.shape, lambda n, s: (0, 0))
    shapes = [
        jax.ShapeDtypeStruct((rows, cols // 2 + kv_cols + EXTRA), BF),
        jax.ShapeDtypeStruct((1, kv_cols + cols // 2), F32),
        jax.ShapeDtypeStruct((RANK, kv_cols + cols // 2), F32),
    ]
    return pl.pallas_call(
        early_kernel,
        grid_spec=pltpu.PrefetchScalarGridSpec(
            num_scalar_prefetch=1,
            grid=(1,),
            in_specs=[fixed(query), fixed(key), fixed(value), fixed(main)]
            + [pl.BlockSpec((RANK, cols + 2 * kv_cols), lambda n, s: (0, 0))],
            out_specs=[fixed(shape) for shape in shapes],
        ),
        out_shape=shapes,
        compiler_params=pltpu.CompilerParams(vmem_limit_bytes=32 << 20),
        cost_estimate=pl.CostEstimate(flops=COST, bytes_accessed=COST, transcendentals=0),
    )(place, query, key, value, main, outer)


def later_kernel(
    place_ref, out_w_ref, gate_ref, up_ref, down_w_ref, main_ref, first_ref, outer_ref, mags_ref,
    out_out, mlp_out, down_out, square_ref, cross_ref, picked_ref, hold, *, part,
):
    half = out_out.shape[1]
    width = gate_ref.shape[1]
    blocks = width // (4 * part)
    cols = blocks * part
    starts = [STARTS[n] for n in range(7)]
    high, low = split_parts(widened(main_ref[...]))
    down_first = widened(first_ref[...])
    down_high, down_low = split_parts(down_first)
    rows = gate_ref.shape[0]
    lanes = mags_ref.shape[0]
    for quarter in range(4):

        @pl.when(place_ref[2] == quarter)
        def _():
            for side, ref in enumerate((gate_ref, up_ref)):
                for at in range(blocks):
                    start = (at * 4 + quarter) * part
                    hold[side, :rows, at * part : (at + 1) * part] = ref[
                        :, start : start + part
                    ].astype(F32)
                    begin = starts[4 + side] + start
                    hold[side, rows : rows + RANK, at * part : (at + 1) * part] = outer_ref[
                        :, begin : begin + part
                    ]
                    hold[side, rows + RANK :, at * part : (at + 1) * part] = mags_ref[
                        :, begin : begin + part
                    ]
    for tile in range(cols // 128):
        for side in range(2):
            to = slice((2 * tile + side) * 128, (2 * tile + side + 1) * 128)
            taken = hold[side, :, tile * 128 : (tile + 1) * 128]
            base = taken[:rows].astype(BF)
            mlp_out[:, to] = base
            outer = taken[rows : rows + RANK]
            picked_ref[:RANK, to] = outer
            picked_ref[RANK:, to] = taken[rows + RANK :]
            square, cross = column_sums(base, high, low, outer, (4 + side) * RANK)
            square_ref[:, half + to.start : half + to.stop] = square
            cross_ref[:, half + to.start : half + to.stop] = cross
    down_at = pl.ds(pl.multiple_of(place_ref[2] * part, 16 if part % 16 == 0 else 8), part)
    down_out[:, : 2 * half] = down_w_ref[down_at, :]
    factor = first_ref[down_at, :]
    factor = jnp.concatenate([factor, factor], axis=1)
    down_out[:, 2 * half :] = widened(factor).astype(BF)
    for core in range(2):

        @pl.when(place_ref[1] == core)
        def _():
            out_out[...] = out_w_ref[:, core * half : (core + 1) * half]
            for tile in range(half // 256):
                at = core * half + tile * 256
                square, cross = column_sums(
                    out_w_ref[:, at : at + 256],
                    high,
                    low,
                    outer_ref[:, starts[3] + at : starts[3] + at + 256],
                    3 * RANK,
                )
                to = slice(tile * 256, (tile + 1) * 256)
                square_ref[:, to] = square
                cross_ref[:, to] = cross
                square, cross = column_sums(
                    down_w_ref[:, at : at + 256],
                    down_high,
                    down_low,
                    outer_ref[:, starts[6] + at : starts[6] + at + 256],
                    0,
                )
                begin = half + 2 * cols + tile * 256
                square_ref[:, begin : begin + 256] = square
                cross_ref[:, begin : begin + 256] = cross


def later_work(place, out_w, gate, up, down_w, main, first, outer, mags, part):
    rows, cols = out_w.shape
    half = cols // 2
    mlp = 2 * (gate.shape[1] // 4)
    total = 2 * half + mlp
    fixed = lambda array: pl.BlockSpec(array.shape, lambda n, s: (0, 0))
    inputs = [out_w, gate, up, down_w, main, first, outer, mags]
    shapes = [
        jax.ShapeDtypeStruct((rows, half), BF),
        jax.ShapeDtypeStruct((rows, mlp), BF),
        jax.ShapeDtypeStruct((part, cols + EXTRA), BF),
        jax.ShapeDtypeStruct((1, total), F32),
        jax.ShapeDtypeStruct((RANK, total), F32),
        jax.ShapeDtypeStruct((RANK + 8, mlp), F32),
    ]
    return pl.pallas_call(
        functools.partial(later_kernel, part=part),
        grid_spec=pltpu.PrefetchScalarGridSpec(
            num_scalar_prefetch=1,
            grid=(1,),
            in_specs=[fixed(array) for array in inputs],
            out_specs=[fixed(shape) for shape in shapes],
            scratch_shapes=[pltpu.VMEM((2, rows + RANK + 8, mlp // 2), F32)],
        ),
        out_shape=shapes,
        compiler_params=pltpu.CompilerParams(vmem_limit_bytes=48 << 20),
        cost_estimate=pl.CostEstimate(flops=COST, bytes_accessed=COST, transcendentals=0),
    )(place, *inputs)


def shards(
    tokens,
    cotangent,
    gain_attn,
    gain_ffn,
    w_query,
    w_key,
    w_value,
    w_output,
    w_gate,
    w_up,
    w_down,
    adapt_main,
    adapt_down,
    adapt_outer,
    magnitudes,
    main_first,
    main_second,
    down_first,
    down_second,
    outer_first,
    outer_second,
    mag_first,
    mag_second,
    segments,
):
    wide_count = lax.axis_size("wide")
    tok_count = lax.axis_size("tok")
    wide = lax.axis_index("wide")
    tok = lax.axis_index("tok")
    core = tok % 2
    place = jnp.stack([wide, core, tok % 4]).astype(jnp.int32)
    quarter = (tok % 4).astype(jnp.int32)[None]
    length, share = tokens.shape
    hidden_share = w_down.shape[0]
    part = hidden_share // 4
    block = length // (wide_count * CHUNKS)
    count = CHUNKS * block
    block_cols = wide_count * part
    half = D // 2
    kv_cols = KVH * HD

    def partner(array):
        return swap(array, "tok", 2)

    def other_core(array):
        return swap(array, "tok", 1)

    across = wide_count // 4
    deep, side = wide // across, wide % across

    def to_tokens(features, gate=()):
        pieces = features.reshape(CHUNKS, 4, across, block, share)
        rows = jnp.zeros((4, CHUNKS, block, across * share), features.dtype)
        for slot in range(across):
            piece = lax.dynamic_index_in_dim(pieces, side ^ slot, 2, keepdims=False)
            piece = jnp.swapaxes(piece, 0, 1)
            if slot:
                piece = swap(piece, "wide", slot)
            rows = lax.dynamic_update_slice(rows, piece, (0, 0, 0, (side ^ slot) * share))
        whole = jnp.zeros((count, D), features.dtype)
        for slot in range(4):
            piece = lax.dynamic_index_in_dim(rows, deep ^ slot, 0, keepdims=False)
            piece = piece.reshape(count, across * share)
            if slot:
                piece = swap(piece, "wide", slot * across)
            if gate:
                piece = after(piece, *gate)
            whole = lax.dynamic_update_slice(whole, piece, (0, (deep ^ slot) * across * share))
        return whole

    def from_tokens(rows):
        cols = across * share
        held = jnp.zeros((CHUNKS, 4, block, cols), rows.dtype)
        for slot in range(4):
            piece = lax.dynamic_slice(rows, (0, (deep ^ slot) * cols), (count, cols))
            if slot:
                piece = swap(piece, "wide", slot * across)
            piece = piece.reshape(CHUNKS, 1, block, cols)
            held = lax.dynamic_update_slice(held, piece, (0, deep ^ slot, 0, 0))
        whole = jnp.zeros((CHUNKS, 4, across, block, share), rows.dtype)
        for slot in range(across):
            piece = lax.dynamic_slice_in_dim(held, (side ^ slot) * share, share, 3)
            if slot:
                piece = swap(piece, "wide", slot)
            whole = lax.dynamic_update_slice(whole, piece[:, :, None], (0, 0, side ^ slot, 0, 0))
        return whole.reshape(length, share)

    def own_half(array, axis=-1):
        size = array.shape[axis] // 2
        return lax.dynamic_slice_in_dim(array, core * size, size, axis)

    def in_order(blocks):
        return jnp.where(
            core == 0, jnp.concatenate(blocks, axis=-1), jnp.concatenate(blocks[::-1], axis=-1)
        )

    def by_core(zero, one, flip=0):
        return jnp.where(core == flip, zero, one)

    def sides(array, n):
        return array[..., STARTS[n] : STARTS[n] + WIDTHS[n]]

    ends = [0, kv_cols, kv_cols + half, kv_cols + 2 * half, kv_cols + 2 * half + 2 * block_cols]
    ends.append(ends[-1] + half)

    def cut(array, n):
        return array[..., ends[n] : ends[n + 1]]

    KV, QUERY, OUT, MLP, DOWN = range(5)

    residual = to_tokens(tokens).astype(F32)
    gain_parts = jnp.stack([gain_attn, gain_ffn], axis=1)
    split = [lax.reduce_precision(gain_parts, 8, 7)]
    split.append(lax.reduce_precision(gain_parts - split[0], 8, 7))
    split.append(gain_parts - split[0] - split[1])
    qkv_shard, squares, soon_cross = early_work(
        place, w_query, w_key, w_value, jnp.concatenate([adapt_main, *split], axis=1), adapt_outer
    )
    qkv_slots = [gather_slots(qkv_shard)]
    mags = after(magnitudes, residual)[None]

    def column_terms(squares, pieces):
        norms = jnp.sqrt(all_sum(squares, ["wide"]))
        rows = jnp.concatenate([piece[0] for piece in pieces], axis=1)
        rows = jnp.concatenate([rows, norms])
        out = []
        for held in (rows, other_core(rows)):
            mags_row, norm = held[:1], held[1:2]
            scale, slope = mags_row / norm, -mags_row / (norm * norm * norm)
            start = 0
            split = []
            for piece in pieces:
                stop = start + piece[0].shape[1]
                split.append((scale[:, start:stop], slope[:, start:stop], norm[:, start:stop]))
                start = stop
            out.append(split)
        return out

    soon = column_terms(
        squares, [(by_core(sides(mags, 1), sides(mags, 2)),), (own_half(sides(mags, 0)),)]
    )
    scale_by, slope_by, norms_by = ([list(soon[k][n][i] for n in range(2)) for k in range(2)] for i in range(3))

    def natural_of(parts, n):
        return in_order([p[n] for p in parts])

    scales, slopes, norms = (
        [natural_of(parts, n) for n in range(2)] for parts in (scale_by, slope_by, norms_by)
    )
    outers = [sides(adapt_outer, n) for n in range(7)]
    outer_kv = jnp.concatenate(
        [jnp.pad(outers[1], ((0, 0), (0, kv_cols))), jnp.pad(outers[2], ((0, 0), (kv_cols, 0)))]
    )

    qkv_slots.append({s: other_core(held) for s, held in qkv_slots[0].items()})
    low_main = put_rows(
        {s: held[:, half + kv_cols :] for s, held in qkv_slots[0].items()},
        jnp.zeros((0, EXTRA), BF),
    )
    gains = low_main[:, 6 * RANK : 6 * RANK + 6].astype(F32).T
    gains = (gains[4:6] + gains[2:4]) + gains[:2]

    def main_cols(n, many=1):
        return low_main[:, n * RANK : (n + many) * RANK]

    def norm_rows(values, gain_row):
        inverse = lax.rsqrt(jnp.mean(values * values, axis=1, keepdims=True) + EPS_NORM)
        return (values * inverse * gain_row[None, :]).astype(BF), inverse

    def norm_rows_back(values, gain_row, inverse, grad_normed):
        inner = jnp.sum(values * gain_row[None, :] * grad_normed, axis=1, keepdims=True)
        return (
            grad_normed * gain_row[None, :] * inverse
            - values * (inverse * inverse * inverse * inner / D)
        )

    def ordered(slots):
        return [slots[s] for s in range(wide_count)]

    own_places = (
        jnp.arange(CHUNKS, dtype=jnp.int32)[:, None] * (wide_count * block)
        + wide * block
        + jnp.arange(block, dtype=jnp.int32)[None, :]
    ).reshape(count)
    segment_row = after(segments, residual)[0]
    own_segment = lax.dynamic_index_in_dim(
        segment_row.reshape(CHUNKS, wide_count, block), wide, 1, keepdims=False
    ).reshape(count)
    own_starts = jnp.sum(
        (segment_row[None, :] < own_segment[:, None]).astype(jnp.int32), axis=1
    )
    frequency = ROPE_BASE ** (-2.0 * jnp.arange(HD // 2, dtype=F32) / HD)
    angles = (own_places - own_starts).astype(F32)[:, None] * frequency[None, :]
    cosine = jnp.tile(jnp.cos(angles), (1, 4))
    sine = jnp.tile(jnp.concatenate([-jnp.sin(angles), jnp.sin(angles)], axis=1), (1, 2))
    place_rows = jnp.tile(own_places.reshape(CHUNKS, 1, block), (1, 1, GROUP))
    start_rows = jnp.tile(own_starts.reshape(CHUNKS, 1, block), (1, 1, GROUP))
    first_block = own_starts.reshape(CHUNKS, block)[:, 0] // (wide_count * block)

    ready = residual
    normed_one, inverse_one = norm_rows(ready, gains[0])
    kv_z, reduced_one = slot_mm(
        place, normed_one, low_main, outer_kv, RANK, [ordered(qkv_slots[k]) for k in range(2)], half
    )
    kv = kv_form(kv_z, scales[KV], cosine, sine)
    token_slots = gather_slots(kv.reshape(CHUNKS, 1, block, KVH * 2 * HD))

    out_shard, mlp_shard, down_shard, squares, rest_cross, picked = later_work(
        place, after(w_output, *near(qkv_slots[0])), w_gate, w_up, w_down, adapt_main, adapt_down, adapt_outer,
        jnp.broadcast_to(mags, (8, OUTS)), part,
    )
    kv = jnp.zeros((CHUNKS, wide_count, block, KVH * 2 * HD), BF)
    for slot, held in token_slots.items():
        kv = lax.dynamic_update_slice(kv, held, (0, wide ^ slot, 0, 0))
    kv = kv.reshape(length, KVH * 2 * HD)
    kvt = kv.T.reshape(KVH, 2 * HD, length)
    query_z, _ = slot_mm(
        place, normed_one, low_main, outers[0], 0, [ordered(qkv_slots[k]) for k in range(2)]
    )
    queries, attended, log_total = attend(
        first_block, query_z, scales[QUERY], cosine, sine, place_rows, start_rows, kv, kvt
    )

    rest = column_terms(
        after(squares, attended),
        [(own_half(sides(mags, 3)),), (picked[RANK : RANK + 1],), (own_half(sides(mags, 6)),)],
    )
    mlp_outer = [picked[:RANK]]
    for found, index in ((scale_by, 0), (slope_by, 1), (norms_by, 2)):
        for k in range(2):
            found[k].extend(rest[k][n][index] for n in range(3))
    for found, parts in ((scales, scale_by), (slopes, slope_by), (norms, norms_by)):
        found.extend(natural_of(parts, n) if n != MLP else None for n in range(2, 5))

    down_slots = gather_slots(after(down_shard, *near(qkv_slots[0])))
    out_slots = [gather_slots(after(out_shard, *near(down_slots)), True)]
    out_slots.append({s: other_core(held) for s, held in out_slots[0].items()})
    down_weights = put_rows(down_slots, jnp.zeros((0, D + EXTRA), BF))
    tiles = 2 * block_cols // 256
    cuts = [0, (tiles + 1) // 2 * 256, 2 * block_cols]
    spans = [slice(cuts[i], cuts[i + 1]) for i in range(2)]
    mlp_slots = []
    before = near(out_slots[0])
    for i, span in enumerate(spans):
        mlp_slots.append(gather_slots(after(mlp_shard[:, span], *before), i == 0))
        before = near(mlp_slots[-1])

    upstream = to_tokens(
        after(cotangent, kv, *near(out_slots[0])), far(mlp_slots[0], 2)
    ).astype(F32)
    output_z, reduced_out = slot_mm(
        place, attended, low_main, outers[3], 3 * RANK, [ordered(out_slots[k]) for k in range(2)]
    )
    hidden_one = residual + output_z * scales[OUT]

    normed_own, inverse_two = norm_rows(hidden_one, gains[1])
    def of_four(rows):
        pair = jnp.concatenate([rows, partner(rows)])
        return jnp.concatenate([pair, other_core(pair)])

    def to_owner_of_four(keep, sent, *behind):
        pair = keep + other_core(after(sent, *behind) if behind else sent).astype(F32)
        swapped = partner(pair[count:].astype(BF))
        return pair[:count] + swapped.astype(F32), swapped

    normed_two = of_four(normed_own)
    down_low = (upstream * scales[DOWN]).astype(BF)
    down_low = of_four(down_low)
    narrow_down = 2.0 * mm_t(down_low, outers[6].astype(BF))
    narrow_down_lanes = lanes_of(narrow_down)
    crosses = after(jnp.concatenate([soon_cross, rest_cross], axis=1), normed_own)
    for bit in bits_of(wide_count):
        crosses = crosses + swap(crosses.astype(BF), "wide", bit).astype(F32)
    cross_by = [crosses, other_core(crosses)]
    normed_two = after(normed_two, *cross_by)
    packs = pack_reduced(normed_two, low_main, 4 * RANK, 2 * RANK)
    blocks = [
        mlp_block(
            place,
            normed_two,
            packs,
            4 * RANK,
            scale_by[0][MLP],
            slope_by[0][MLP],
            mlp_outer[0],
            down_low,
            narrow_down_lanes,
            down_weights,
            ordered(mlp_slots[i]),
            span.start,
        )
        for i, span in enumerate(spans)
    ]
    bounds = [(span.start // 2, span.stop // 2) for span in spans]
    down_keep, down_sent, reduced_down = down_forward([b[0] for b in blocks], bounds, down_weights, outers[6])
    reduced_down = reduced_down[:, :RANK]

    pairs = 2 * RANK
    keep, sent, first_pairs = mlp_back(
        place,
        [b[1] for b in blocks],
        sum(b[4] for b in blocks),
        sum(b[5] for b in blocks),
        low_main,
        normed_two,
        [ordered(slots) for slots in mlp_slots],
        4 * RANK,
    )
    grad_normed, swapped = to_owner_of_four(keep, sent)
    grad_mid = upstream + norm_rows_back(hidden_one, gains[1], inverse_two, grad_normed)
    down_z, _ = to_owner_of_four(down_keep, down_sent, swapped)
    layer_rows = (hidden_one + down_z * scales[DOWN]).astype(BF)

    def first_grads(rows, inputs, narrow, middle, factors, many):
        size = many * RANK
        parts = jnp.concatenate(two_parts(narrow), axis=1)
        product = fold_parts(t_mm(parts, inputs), size)
        same = jnp.arange(size)[:, None] // RANK == jnp.arange(size)[None, :] // RANK
        middle = jnp.where(same, middle[:, :size], 0.0)
        term = fold_parts(mm_t(jnp.concatenate(two_parts(middle)), factors), size)
        return product + 2.0 * (fold_parts(rows, size) + 2.0 * term)

    def twice(cols):
        return jnp.concatenate([cols, cols], axis=1)

    out_rows, scale_out, outer_out, narrow_out, middle_out = grad_terms(
        grad_mid, output_z, scales[OUT], slopes[OUT], outers[3], 3 * RANK, reduced_out
    )
    back_out = slot_back(place, out_rows, [ordered(out_slots[k]) for k in range(2)])
    grad_mixed, first_out = finish_back(
        [back_out], [RANK], narrow_out, middle_out, low_main, attended, 3 * RANK
    )
    grad_mixed = grad_mixed.astype(BF)

    query_grad, kv_grad = attend_back(
        first_block, queries, cosine, sine, place_rows, start_rows, kv, kvt, log_total, attended,
        grad_mixed,
    )
    kv_grad = kv_grad.reshape(CHUNKS, wide_count, block, KVH * 2 * HD)
    kv_grad = jnp.swapaxes(kv_grad, 0, 1).astype(F32)
    kv_grad = scatter_sum(kv_grad, "wide", BF)
    kv_grad = kv_back(kv_grad.reshape(count, KVH * 2 * HD), cosine, sine)
    layer_out = from_tokens(after(layer_rows, kv_grad))

    query_rows_low, scale_query, outer_query, narrow_query, middle_query = grad_terms(
        query_grad, query_z, scales[QUERY], slopes[QUERY], outers[0], 0, reduced_one
    )
    back_query = slot_back(place, query_rows_low, [ordered(qkv_slots[k]) for k in range(2)])
    kv_rows_low, scale_kv, outer_kv_grad, narrow_kv, middle_kv = grad_terms(
        kv_grad, kv_z, scales[KV], slopes[KV], outer_kv,
        RANK, reduced_one,
    )
    back_kv = slot_back(place, kv_rows_low, [ordered(qkv_slots[k]) for k in range(2)], half)
    grad_normed, first_one = finish_back(
        [back_query, back_kv],
        [RANK, pairs],
        narrow_query + narrow_kv,
        jnp.concatenate([middle_query, middle_kv]),
        low_main,
        normed_one,
        0,
    )
    grad_tokens = from_tokens(
        (grad_mid + norm_rows_back(residual, gains[0], inverse_one, grad_normed)).astype(BF)
    )

    scale_down = jnp.sum(upstream * down_z, axis=0, keepdims=True)
    pair_down = scale_down + partner(scale_down)
    pair_down = pair_down + other_core(pair_down)
    weighted = (pair_down * slopes[DOWN]) * outers[6]
    middle_down = gram_of(weighted, outers[6])
    weighted_parts = jnp.pad(jnp.concatenate(two_parts(weighted)), ((0, 0), (0, EXTRA)))
    first_down = first_grads(
        mm_t(weighted_parts, down_weights),
        jnp.concatenate([b[0] for b in blocks], axis=1),
        narrow_down,
        middle_down,
        down_weights[:, D : D + RANK],
        1,
    )
    outer_down = 2.0 * fold_parts(
        t_mm(jnp.concatenate(two_parts(reduced_down), axis=1), down_low), RANK
    )
    of_keys = (jnp.arange(2 * kv_cols) < kv_cols)[None, :]
    outer_kv_grad = jnp.where(of_keys, outer_kv_grad[:RANK], outer_kv_grad[RANK:])
    def second_grads(product, sums, slope, norm, cross):
        return jnp.concatenate([product + 2.0 * (sums * slope) * cross, sums / norm])

    plain = {
        n: second_grads(
            product, sums, slopes[n], norms[n], in_order([cut(c, n) for c in cross_by])
        )
        for n, product, sums in (
            (KV, outer_kv_grad, scale_kv),
            (QUERY, outer_query, scale_query),
            (OUT, outer_out, scale_out),
            (DOWN, outer_down, scale_down),
        )
    }
    mlp_grads = second_grads(
        jnp.concatenate([b[3] for b in blocks], axis=1),
        jnp.concatenate([b[2] for b in blocks], axis=1),
        slope_by[0][MLP],
        norms_by[0][MLP],
        cut(cross_by[0], MLP),
    )
    main_width = 6 * RANK // tok_count
    down_width = RANK // tok_count
    outer_share = OUTS // (tok_count * wide_count)

    lanes = 768
    fit = lanes // share
    tall = main_width // fit
    packed = pack_all(
        place,
        [
            plain[QUERY], plain[KV], plain[OUT], mlp_grads, plain[DOWN], first_one, first_out,
            first_pairs, first_down,
        ],
        tok_count,
        part,
        (tall, down_width, lanes, share, hidden_share, outer_share),
    )
    packed = packed.reshape((tok_count, wide_count) + packed.shape[1:])
    packed = scatter_sum(scatter_sum(packed, "tok"), "wide")
    main_part = jnp.swapaxes(packed[:tall].reshape(tall, fit, share), 0, 1)
    main_part = main_part.reshape(main_width, share).T
    down_part = packed[tall : tall + down_width, :hidden_share].T
    outer_sum = packed[tall + down_width : tall + down_width + RANK + 1, :outer_share]
    outer_part = outer_sum[:RANK]
    block_start = (tok * wide_count + wide) * outer_share
    mag_part = outer_sum[RANK]

    local_squares = (
        squared_sum(main_part)
        + squared_sum(down_part)
        + squared_sum(outer_part)
        + squared_sum(mag_part)
    )
    grad_total = all_sum(jnp.full((8, 128), local_squares), ["tok", "wide"])[0, 0]
    grad_norm = jnp.sqrt(grad_total)
    clip_factor = CLIP_MAX / jnp.maximum(grad_norm, CLIP_MAX)
    main_param = lax.dynamic_slice_in_dim(adapt_main, tok * main_width, main_width, 1)
    down_param = lax.dynamic_slice_in_dim(adapt_down, tok * down_width, down_width, 1)
    outer_param = lax.dynamic_slice_in_dim(adapt_outer, block_start, outer_share, 1)
    mag_param = lax.dynamic_slice_in_dim(magnitudes, block_start, outer_share, 0)
    main_new, main_first_new, main_second_new = adam(
        main_param, main_part, main_first, main_second, RATE_ADAPT, clip_factor
    )
    down_new, down_first_new, down_second_new = adam(
        down_param, down_part, down_first, down_second, RATE_ADAPT, clip_factor
    )
    outer_new, outer_first_new, outer_second_new = adam(
        outer_param, outer_part, outer_first, outer_second, RATE_OUTER, clip_factor
    )
    mag_new, mag_first_new, mag_second_new = adam(
        mag_param, mag_part, mag_first, mag_second, RATE_MAGNITUDE, clip_factor
    )
    mag_clipped = mag_part * clip_factor
    return (
        layer_out,
        grad_tokens,
        grad_norm,
        main_new,
        main_first_new,
        main_second_new,
        down_new,
        down_first_new,
        down_second_new,
        outer_new,
        outer_first_new,
        outer_second_new,
        mag_new,
        mag_clipped,
        mag_second_new,
    )


def solution(mesh):
    return jax.shard_map(
        shards,
        mesh=mesh,
        in_specs=(
            P("tok", "wide"),
            P("tok", "wide"),
            P("wide"),
            P("wide"),
            P("wide", None),
            P("wide", None),
            P("wide", None),
            P("wide", None),
            P("wide", None),
            P("wide", None),
            P("wide", None),
            P("wide", None),
            P("wide", None),
            P(),
            P(),
            P("wide", "tok"),
            P("wide", "tok"),
            P("wide", "tok"),
            P("wide", "tok"),
            P(None, ("tok", "wide")),
            P(None, ("tok", "wide")),
            P(("tok", "wide")),
            P(("tok", "wide")),
            P("tok", None),
        ),
        out_specs=(
            P("tok", "wide"),
            P("tok", "wide"),
            P(),
            P("wide", "tok"),
            P("wide", "tok"),
            P("wide", "tok"),
            P("wide", "tok"),
            P("wide", "tok"),
            P("wide", "tok"),
            P(None, ("tok", "wide")),
            P(None, ("tok", "wide")),
            P(None, ("tok", "wide")),
            P(("tok", "wide")),
            P(("tok", "wide")),
            P(("tok", "wide")),
        ),
        check_vma=False,
    )
```

```python
import functools

import jax
import jax.numpy as jnp
from jax import lax
from jax.experimental import pallas as pl
from jax.experimental.pallas import tpu as pltpu
from jax.sharding import PartitionSpec as P

D = 2048
HEADS = 32
HD = 64
KVH = 4
FF = 5632
STEP = 10
RANK = 16
CHUNKS = 8
EXTRA = 128
COST = 1 << 10

EPS_NORM = 1e-05
ROPE_BASE = 10000.0
CLIP_MAX = 1.0
BETA_FIRST = 0.9
BETA_SECOND = 0.999
ADAM_EPS = 1e-08
WEIGHT_DECAY = 0.01
RATE_ADAPT = 0.02
RATE_OUTER = 0.05
RATE_MAGNITUDE = 0.4
PRECISE = lax.Precision.HIGHEST
MASKED = -1e30
NT = (((1,), (1,)), ((), ()))
GROUP = HEADS // KVH
FWD = 4
BWD = 4
BF = jnp.bfloat16
F32 = jnp.float32
WIDTHS = [D, KVH * HD, KVH * HD, D, FF, FF, D]
STARTS = [sum(WIDTHS[:number]) for number in range(7)]
OUTS = sum(WIDTHS)


def bits_of(count):
    return [1 << place for place in range(count.bit_length() - 1)]


def swap(array, axis, distance):
    count = lax.axis_size(axis)
    return lax.ppermute(array, axis, [(i, i ^ distance) for i in range(count)])


def mm(left, right):
    return jnp.dot(left, right, preferred_element_type=F32)


def mm_t(left, right):
    return lax.dot_general(left, right, (((1,), (1,)), ((), ())), preferred_element_type=F32)


def t_mm(left, right):
    return lax.dot_general(left, right, (((0,), (0,)), ((), ())), preferred_element_type=F32)


def two_parts(values):
    high = lax.reduce_precision(values, 8, 7)
    return high.astype(BF), (values - high).astype(BF)


def fold_parts(stacked, count):
    return stacked[:count] + stacked[count : 2 * count]


def adam(param, grad, first, second, rate, clip_factor):
    clipped = grad * clip_factor
    first_new = BETA_FIRST * first + (1.0 - BETA_FIRST) * clipped
    second_new = BETA_SECOND * second + (1.0 - BETA_SECOND) * clipped * clipped
    first_hat = first_new / (1.0 - BETA_FIRST**STEP)
    second_hat = second_new / (1.0 - BETA_SECOND**STEP)
    param_new = param - rate * (
        first_hat / (jnp.sqrt(second_hat) + ADAM_EPS) + WEIGHT_DECAY * param
    )
    return (param_new, first_new, second_new)


def squared_sum(values):
    return jnp.sum(values * values)


def all_sum(values, axes):
    for axis in axes:
        for bit in bits_of(lax.axis_size(axis)):
            values = values + swap(values, axis, bit)
    return values


def all_blocks(block, axis):
    stacked = block[None]
    index = lax.axis_index(axis)
    for bit in bits_of(lax.axis_size(axis)):
        upper = (index // bit) % 2 == 1
        received = swap(stacked, axis, bit)
        stacked = jnp.concatenate(
            [jnp.where(upper, received, stacked), jnp.where(upper, stacked, received)]
        )
    return stacked


def scatter_sum(blocks, axis, wire=F32, order=None):
    index = lax.axis_index(axis)
    bits = bits_of(lax.axis_size(axis))
    shape = blocks.shape[1:]
    left = list(reversed(bits))
    blocks = blocks.reshape((2,) * len(bits) + shape)
    for bit in order or bits:
        dim = left.index(bit)
        side = (index // bit) % 2
        keep = lax.dynamic_index_in_dim(blocks, side, dim, keepdims=False)
        send = lax.dynamic_index_in_dim(blocks, 1 - side, dim, keepdims=False)
        blocks = keep + swap(send.astype(wire), axis, bit).astype(blocks.dtype)
        left.remove(bit)
    return blocks


def after(value, *others):
    return lax.optimization_barrier((value,) + others)[0]


def gather_slots(shard, turned=False, gate=None):
    slots = {0: shard}
    count = lax.axis_size("wide")
    for slot in sorted(range(1, count), key=lambda i: bin(i).count("1")):
        low = slot & -slot
        if turned and slot == count - 1:
            low = count // 4
        held = slots[slot ^ low]
        if gate is not None and slot != low:
            held = after(held, gate)
        slots[slot] = swap(held, "wide", low)
    return slots


def near(slots):
    return [held for slot, held in slots.items() if bin(slot).count("1") == 1]


def far(slots, steps):
    return [held for slot, held in slots.items() if bin(slot).count("1") == steps]


def put_rows(slots, extra):
    count = lax.axis_size("wide")
    index = lax.axis_index("wide")
    rows, cols = slots[0].shape
    whole = jnp.zeros((count * rows + extra.shape[0], cols), extra.dtype)
    whole = lax.dynamic_update_slice(whole, extra, (count * rows, 0))
    for slot, held in slots.items():
        whole = lax.dynamic_update_slice(whole, held, ((index ^ slot) * rows, 0))
    return whole


def rotate_half(values):
    half = HD // 2
    return jnp.concatenate([values[..., half:], values[..., :half]], axis=-1)


def turn(values, cosine, sine):
    shaped = values.reshape(values.shape[0], -1, HD)
    turned = shaped * cosine[:, None, :] + rotate_half(shaped) * sine[:, None, :]
    return turned.reshape(values.shape)


def pad_rows(rows, count):
    return jnp.concatenate([rows, jnp.zeros((count - rows.shape[0], rows.shape[1]), rows.dtype)])


def lanes_of(reduced):
    high, low = two_parts(reduced)
    return jnp.pad(
        jnp.concatenate([high, low], axis=1), ((0, 0), (0, EXTRA - 2 * reduced.shape[1]))
    )


def twice_low(rows):
    doubled = 2.0 * rows.astype(BF)
    return pad_rows(jnp.concatenate([doubled, doubled]), EXTRA)


def gram_of(left, right):
    return lax.dot_general(left, right, (((1,), (1,)), ((), ())), precision=PRECISE)


def turn_lanes(values, cosine, sine):
    lane = lax.broadcasted_iota(jnp.int32, values.shape, 1) % HD
    swapped = jnp.where(
        lane < HD // 2,
        pltpu.roll(values, 2 * HD - HD // 2, 1),
        pltpu.roll(values, HD // 2, 1),
    )
    return values * cosine + swapped * sine


def head_rows(pairs, low_side):
    rows = []
    for pair in pairs:
        lane = lax.broadcasted_iota(jnp.int32, pair.shape, 1)
        moved = pltpu.roll(pair, HD, 1)
        if low_side:
            rows.append(jnp.where(lane < HD, pair, 0.0))
            rows.append(jnp.where(lane < HD, moved, 0.0))
        else:
            rows.append(jnp.where(lane >= HD, moved, 0.0))
            rows.append(jnp.where(lane >= HD, pair, 0.0))
    return jnp.concatenate(rows, axis=0).astype(BF)


def pairs_of(columns, block):
    turned = jnp.concatenate([columns, columns], axis=0).T
    lane = lax.broadcasted_iota(jnp.int32, (block, 2 * HD), 1)
    out = []
    for pair in range(GROUP // 2):
        first = turned[2 * pair * block : (2 * pair + 1) * block]
        second = turned[(2 * pair + 1) * block : (2 * pair + 2) * block]
        out.append(jnp.where(lane < HD, first, second))
    return out


def forward_kernel(
    first_ref, z_ref, scale_ref, cos_ref, sin_ref, place_ref, start_ref, kv_ref, kvt_ref,
    query_ref, out_ref, log_ref, *, block, span, groups,
):
    rows = GROUP * block
    width = GROUP * HD

    def chunk_body(chunk, carry):
        at = pl.ds(pl.multiple_of(chunk * block, block), block)
        cosine = cos_ref[at, :]
        sine = sin_ref[at, :]
        query_rows = []
        for group in range(groups):
            pairs = []
            for pair in range(GROUP // 2):
                lanes = slice(group * width + pair * 2 * HD, group * width + (pair + 1) * 2 * HD)
                turned = turn_lanes(z_ref[at, lanes] * scale_ref[:, lanes], cosine, sine)
                low = turned.astype(BF)
                query_ref[at, lanes] = low
                pairs.append(low.astype(F32) * HD**-0.5)
            query_rows.append(head_rows(pairs, True))
        place = place_ref[chunk]
        start = start_ref[chunk]

        def key_body(step, state):
            key_block = chunk - step
            keys = pl.ds(pl.multiple_of(key_block * span, span), span)
            spot = key_block * span + lax.broadcasted_iota(jnp.int32, (span, rows), 0)
            allowed = (spot <= place) & (spot >= start)
            out = []
            all_scores = [
                lax.dot_general(
                    kv_ref[keys, group * 2 * HD : (group + 1) * 2 * HD], query_rows[group], NT, preferred_element_type=F32
                )
                for group in range(groups)
            ]
            for group in range(groups):
                peak, total, mixed = state[group]
                scores = jnp.where(allowed, all_scores[group], MASKED)
                peak_new = jnp.maximum(peak, jnp.max(scores, axis=0, keepdims=True))
                powers = jnp.exp(scores - peak_new)
                shrink = jnp.exp(peak - peak_new)
                total = total * shrink + jnp.sum(powers, axis=0, keepdims=True)
                mixed = mixed * shrink + jnp.dot(
                    kvt_ref[group, HD:, keys], powers.astype(BF), preferred_element_type=F32
                )
                out.append((peak_new, total, mixed))
            return tuple(out)

        start_state = tuple(
            (
                jnp.full((1, rows), MASKED, F32),
                jnp.zeros((1, rows), F32),
                jnp.zeros((HD, rows), F32),
            )
            for _ in range(groups)
        )
        state = lax.fori_loop(0, chunk + 1 - first_ref[chunk], key_body, start_state)
        for group in range(groups):
            peak, total, mixed = state[group]
            log_ref[group, chunk] = peak + jnp.log(total)
            for pair, value in enumerate(pairs_of(mixed / total, block)):
                low_lane = group * width + pair * 2 * HD
                out_ref[at, low_lane : low_lane + 2 * HD] = value.astype(BF)
        return carry

    lax.fori_loop(0, CHUNKS, chunk_body, 0)


def backward_kernel(
    first_ref, query_ref, cos_ref, sin_ref, place_ref, start_ref, kv_ref, kvt_ref, log_ref,
    out_ref, grad_ref, query_grad_ref, kv_grad_ref, sums, *, block, span, groups,
):
    rows = GROUP * block
    width = GROUP * HD
    sums[...] = jnp.zeros_like(sums)

    def chunk_body(chunk, carry):
        at = pl.ds(pl.multiple_of(chunk * block, block), block)
        tiles = []
        for group in range(groups):
            queries = []
            grads = []
            product_rows = []
            for pair in range(GROUP // 2):
                lanes = slice(group * width + pair * 2 * HD, group * width + (pair + 1) * 2 * HD)
                queries.append(query_ref[at, lanes].astype(F32) * HD**-0.5)
                grad = grad_ref[at, lanes].astype(F32)
                grads.append(grad)
                product = grad * out_ref[at, lanes].astype(F32)
                lane = lax.broadcasted_iota(jnp.int32, product.shape, 1)
                product_rows.append(jnp.where(lane < HD, product, 0.0))
                product_rows.append(jnp.where(lane >= HD, product, 0.0))
            inner = jnp.sum(jnp.concatenate(product_rows, axis=0).T, axis=0, keepdims=True)
            query_rows = head_rows(queries, True)
            grad_rows = head_rows(grads, False)
            tiles.append((query_rows, grad_rows, inner, log_ref[group, chunk]))
        place = place_ref[chunk]
        start = start_ref[chunk]

        def key_body(key_block, query_grads):
            keys = pl.ds(pl.multiple_of(key_block * span, span), span)
            spot = key_block * span + lax.broadcasted_iota(jnp.int32, (span, rows), 0)
            allowed = (spot <= place) & (spot >= start)
            out = []
            products = []
            for group in range(groups):
                query_rows, grad_rows, inner, log_total = tiles[group]
                kv = kv_ref[keys, group * 2 * HD : (group + 1) * 2 * HD]
                products.append(
                    (
                        lax.dot_general(kv, query_rows, NT, preferred_element_type=F32),
                        lax.dot_general(kv, grad_rows, NT, preferred_element_type=F32),
                    )
                )
            for group in range(groups):
                query_rows, grad_rows, inner, log_total = tiles[group]
                scores, grad_weights = products[group]
                weights = jnp.exp(jnp.where(allowed, scores - log_total, MASKED))
                grad_scores = (weights * (grad_weights - inner)).astype(BF)
                sums[group, keys, :] += jnp.dot(
                    grad_scores, query_rows, preferred_element_type=F32
                ) + jnp.dot(weights.astype(BF), grad_rows, preferred_element_type=F32)
                out.append(
                    query_grads[group]
                    + jnp.dot(kvt_ref[group, :HD, keys], grad_scores, preferred_element_type=F32)
                )
            return tuple(out)

        query_grads = lax.fori_loop(
            first_ref[chunk],
            chunk + 1,
            key_body,
            tuple(jnp.zeros((HD, rows), F32) for _ in range(groups)),
        )
        cosine = cos_ref[at, :]
        sine = sin_ref[at, :]
        for group in range(groups):
            for pair, value in enumerate(pairs_of(query_grads[group] * HD**-0.5, block)):
                low_lane = group * width + pair * 2 * HD
                query_grad_ref[at, low_lane : low_lane + 2 * HD] = turn_lanes(
                    value, cosine, -sine
                )
        return carry

    lax.fori_loop(0, CHUNKS, chunk_body, 0)
    for group in range(groups):
        kv_grad_ref[:, group * 2 * HD : (group + 1) * 2 * HD] = sums[group].astype(BF)


def attend(first_block, z, scale, cosine, sine, places, starts, kv, kvt):
    count = z.shape[0]
    block = count // CHUNKS
    length = kv.shape[0]
    span = length // CHUNKS
    rows = GROUP * block
    width = FWD * GROUP * HD
    grid_spec = pltpu.PrefetchScalarGridSpec(
        num_scalar_prefetch=1,
        grid=(KVH // FWD,),
        in_specs=[
            pl.BlockSpec((count, width), lambda g, s: (0, g)),
            pl.BlockSpec((1, width), lambda g, s: (0, g)),
            pl.BlockSpec((count, 2 * HD), lambda g, s: (0, 0)),
            pl.BlockSpec((count, 2 * HD), lambda g, s: (0, 0)),
            pl.BlockSpec((CHUNKS, 1, rows), lambda g, s: (0, 0, 0)),
            pl.BlockSpec((CHUNKS, 1, rows), lambda g, s: (0, 0, 0)),
            pl.BlockSpec((length, FWD * 2 * HD), lambda g, s: (0, g)),
            pl.BlockSpec((FWD, 2 * HD, length), lambda g, s: (g, 0, 0)),
        ],
        out_specs=[
            pl.BlockSpec((count, width), lambda g, s: (0, g)),
            pl.BlockSpec((count, width), lambda g, s: (0, g)),
            pl.BlockSpec((FWD, CHUNKS, 1, rows), lambda g, s: (g, 0, 0, 0)),
        ],
    )
    return pl.pallas_call(
        functools.partial(forward_kernel, block=block, span=span, groups=FWD),
        grid_spec=grid_spec,
        out_shape=[
            jax.ShapeDtypeStruct((count, HEADS * HD), BF),
            jax.ShapeDtypeStruct((count, HEADS * HD), BF),
            jax.ShapeDtypeStruct((KVH, CHUNKS, 1, rows), F32),
        ],
        compiler_params=pltpu.CompilerParams(vmem_limit_bytes=40 << 20),
        cost_estimate=pl.CostEstimate(flops=COST, bytes_accessed=COST, transcendentals=0),
    )(first_block, z, scale, cosine, sine, places, starts, kv, kvt)


def attend_back(
    first_block, queries, cosine, sine, places, starts, kv, kvt, log_total, attended, grads
):
    count = queries.shape[0]
    block = count // CHUNKS
    length = kv.shape[0]
    span = length // CHUNKS
    rows = GROUP * block
    width = BWD * GROUP * HD
    grid_spec = pltpu.PrefetchScalarGridSpec(
        num_scalar_prefetch=1,
        grid=(KVH // BWD,),
        in_specs=[
            pl.BlockSpec((count, width), lambda g, s: (0, g)),
            pl.BlockSpec((count, 2 * HD), lambda g, s: (0, 0)),
            pl.BlockSpec((count, 2 * HD), lambda g, s: (0, 0)),
            pl.BlockSpec((CHUNKS, 1, rows), lambda g, s: (0, 0, 0)),
            pl.BlockSpec((CHUNKS, 1, rows), lambda g, s: (0, 0, 0)),
            pl.BlockSpec((length, BWD * 2 * HD), lambda g, s: (0, g)),
            pl.BlockSpec((BWD, 2 * HD, length), lambda g, s: (g, 0, 0)),
            pl.BlockSpec((BWD, CHUNKS, 1, rows), lambda g, s: (g, 0, 0, 0)),
            pl.BlockSpec((count, width), lambda g, s: (0, g)),
            pl.BlockSpec((count, width), lambda g, s: (0, g)),
        ],
        out_specs=[
            pl.BlockSpec((count, width), lambda g, s: (0, g)),
            pl.BlockSpec((length, BWD * 2 * HD), lambda g, s: (0, g)),
        ],
        scratch_shapes=[pltpu.VMEM((BWD, length, 2 * HD), F32)],
    )
    return pl.pallas_call(
        functools.partial(backward_kernel, block=block, span=span, groups=BWD),
        grid_spec=grid_spec,
        out_shape=[
            jax.ShapeDtypeStruct((count, HEADS * HD), F32),
            jax.ShapeDtypeStruct((length, KVH * 2 * HD), BF),
        ],
        compiler_params=pltpu.CompilerParams(vmem_limit_bytes=40 << 20),
        cost_estimate=pl.CostEstimate(flops=40 << 30, bytes_accessed=64 << 20, transcendentals=0),
    )(first_block, queries, cosine, sine, places, starts, kv, kvt, log_total, attended, grads)


def place_of(place_ref, slot, rows):
    return pl.multiple_of((place_ref[0] ^ slot) * rows, rows)


def half_place(place_ref, half, tiles, pair_tiles):
    return (place_ref[1] ^ half) * pair_tiles + tiles


def set_rows(outer, offset):
    rank, cols = outer.shape
    parts = [outer]
    if offset:
        parts = [jnp.zeros((offset, cols), outer.dtype)] + parts
    if EXTRA - rank - offset:
        parts = parts + [jnp.zeros((EXTRA - rank - offset, cols), outer.dtype)]
    return jnp.concatenate(parts, axis=0)


def split_parts(values):
    high = values.astype(BF)
    return high, (values - high.astype(F32)).astype(BF)


def low_rank(reduced, outer, offset):
    high, low = split_parts(reduced)
    rows = set_rows(2.0 * outer.astype(BF).astype(F32), offset).astype(BF)
    return jnp.dot(high, rows, preferred_element_type=F32) + jnp.dot(
        low, rows, preferred_element_type=F32
    )


def slot_kernel(place_ref, inputs_ref, first_ref, outer_ref, *refs, offset):
    slots, out_ref, reduced_ref = refs[:-2], refs[-2], refs[-1]
    each = len(slots) // 2
    rows = slots[0].shape[0]

    @pl.when((pl.program_id(0) == 0) & (pl.program_id(1) == 0))
    def _():
        reduced_ref[...] = jnp.dot(inputs_ref[...], first_ref[...], preferred_element_type=F32)

    def total(chosen):
        result = low_rank(reduced_ref[...], outer_ref[...], offset)
        for slot, ref in enumerate(chosen):
            result = result + jnp.dot(
                inputs_ref[:, pl.ds(place_of(place_ref, slot, rows), rows)],
                ref[...],
                preferred_element_type=F32,
            )
        out_ref[...] = result

    for half in range(2):

        @pl.when(pl.program_id(0) == half)
        def _():
            total(slots[half * each : (half + 1) * each])


def slot_mm(place, inputs, first, outer, offset, slots, skip=0, tile=256):
    rows = slots[0][0].shape[0]
    cols = outer.shape[1]
    tiles = cols // 2 // tile

    def held(half):
        def spot(h, n, s):
            return (0, skip // tile + jnp.where(h == half, n, (tiles - 1) * (1 - half)))

        return pl.BlockSpec((rows, tile), spot)

    return pl.pallas_call(
        functools.partial(slot_kernel, offset=offset),
        grid_spec=pltpu.PrefetchScalarGridSpec(
            num_scalar_prefetch=1,
            grid=(2, tiles),
            in_specs=[
                pl.BlockSpec(inputs.shape, lambda h, n, s: (0, 0)),
                pl.BlockSpec(first.shape, lambda h, n, s: (0, 0)),
                pl.BlockSpec(
                    (outer.shape[0], tile), lambda h, n, s: (0, half_place(s, h, n, tiles))
                ),
            ]
            + [held(half) for half in range(2) for _ in slots[half]],
            out_specs=[
                pl.BlockSpec(
                    (inputs.shape[0], tile), lambda h, n, s: (0, half_place(s, h, n, tiles))
                ),
                pl.BlockSpec((inputs.shape[0], EXTRA), lambda h, n, s: (0, 0)),
            ],
        ),
        out_shape=[
            jax.ShapeDtypeStruct((inputs.shape[0], cols), F32),
            jax.ShapeDtypeStruct((inputs.shape[0], EXTRA), F32),
        ],
        compiler_params=pltpu.CompilerParams(vmem_limit_bytes=40 << 20),
        cost_estimate=pl.CostEstimate(flops=COST, bytes_accessed=COST, transcendentals=0),
    )(place, inputs, first, outer, *slots[0], *slots[1])


def finish_kernel(*refs, count, sizes, offset, summed):
    raws = refs[: len(sizes)]
    narrow_ref, middle_ref, first_ref, inputs_ref, grad_ref, out_ref = refs[len(sizes) :]
    first = first_ref[...]
    narrow_high, narrow_low = split_parts(narrow_ref[...])
    total = lax.dot_general(narrow_high, first, NT, preferred_element_type=F32)
    total = total + lax.dot_general(narrow_low, first, NT, preferred_element_type=F32)
    weighted = []
    for ref, size in zip(raws, sizes):
        total = total + ref[:count, :]
        weighted.append(ref[count : count + size, :] + ref[count + size :, :])
    grad_ref[...] = total
    weighted = sum(weighted) if summed else jnp.concatenate(weighted, axis=0)
    middle_high, middle_low = split_parts(middle_ref[...])
    middle = lax.dot_general(middle_high, first, NT, preferred_element_type=F32)
    middle = middle + lax.dot_general(middle_low, first, NT, preferred_element_type=F32)
    under = (((0,), (0,)), ((), ()))
    inputs = inputs_ref[...]
    product = lax.dot_general(narrow_high, inputs, under, preferred_element_type=F32)
    product = product + lax.dot_general(narrow_low, inputs, under, preferred_element_type=F32)
    out_ref[...] = (
        product[offset : offset + weighted.shape[0]] + 2.0 * (weighted + 2.0 * middle)
    )


def finish_back(raws, sizes, narrow, middle, first, inputs, offset, summed=False, tile=512):
    count = inputs.shape[0]
    rank = middle.shape[0]
    tiled = lambda rows: pl.BlockSpec((rows, tile), lambda n: (0, n))
    return pl.pallas_call(
        functools.partial(
            finish_kernel, count=count, sizes=sizes, offset=offset, summed=summed
        ),
        grid=(D // tile,),
        in_specs=[tiled(raw.shape[0]) for raw in raws]
        + [
            pl.BlockSpec(narrow.shape, lambda n: (0, 0)),
            pl.BlockSpec(middle.shape, lambda n: (0, 0)),
            pl.BlockSpec((tile, EXTRA), lambda n: (n, 0)),
            tiled(count),
        ],
        out_specs=[tiled(count), tiled(rank)],
        out_shape=[
            jax.ShapeDtypeStruct((count, D), F32),
            jax.ShapeDtypeStruct((rank, D), F32),
        ],
        compiler_params=pltpu.CompilerParams(vmem_limit_bytes=40 << 20),
        cost_estimate=pl.CostEstimate(flops=COST, bytes_accessed=COST, transcendentals=0),
    )(*raws, narrow, middle, first, inputs)


def slot_back_kernel(place_ref, grad_ref, *refs, skip):
    slots, out_ref, held, arrived = refs[:-3], refs[-3], refs[-2], refs[-1]
    each = len(slots) // 2
    rows, cols = held.shape[1:]
    copies = [
        pltpu.make_async_copy(ref.at[:, pl.ds(skip, cols)], held.at[slot], arrived.at[slot])
        for slot, ref in enumerate(slots)
    ]
    for slot in range(each):
        copies[slot].start()
        copies[each + slot].start()
    grads = [
        grad_ref[:, pl.ds(pl.multiple_of((place_ref[1] ^ half) * cols, cols), cols)]
        for half in range(2)
    ]
    for slot in range(each):
        copies[slot].wait()
        copies[each + slot].wait()
        out_ref[:, pl.ds(place_of(place_ref, slot, rows), rows)] = lax.dot_general(
            grads[0], held[slot], NT, preferred_element_type=F32
        ) + lax.dot_general(grads[1], held[each + slot], NT, preferred_element_type=F32)


def slot_back(place, grads, slots, skip=0):
    rows = slots[0][0].shape[0]
    count, cols = grads.shape
    many = 2 * len(slots[0])
    return pl.pallas_call(
        functools.partial(slot_back_kernel, skip=skip),
        grid_spec=pltpu.PrefetchScalarGridSpec(
            num_scalar_prefetch=1,
            grid=(1,),
            in_specs=[pl.BlockSpec((count, cols), lambda n, s: (0, 0))]
            + [pl.BlockSpec(memory_space=pl.ANY) for _ in range(many)],
            out_specs=pl.BlockSpec((count, D), lambda n, s: (0, 0)),
            scratch_shapes=[
                pltpu.VMEM((many, rows, cols // 2), BF),
                pltpu.SemaphoreType.DMA((many,)),
            ],
        ),
        out_shape=jax.ShapeDtypeStruct((count, D), F32),
        compiler_params=pltpu.CompilerParams(vmem_limit_bytes=40 << 20),
        cost_estimate=pl.CostEstimate(flops=COST, bytes_accessed=COST, transcendentals=0),
    )(place, grads, *slots[0], *slots[1])


def pad_to(rows, count):
    return jnp.concatenate([rows, jnp.zeros((count - rows.shape[0], rows.shape[1]), rows.dtype)])


def split_rows(weighted):
    high = weighted.astype(BF)
    return high, (weighted - high.astype(F32)).astype(BF)


def terms_of(grads_low, weighted, outer, reduced, offset):
    rank = outer.shape[0]
    rows = set_rows(outer, offset)
    narrow = 2.0 * lax.dot_general(grads_low, rows.astype(BF), NT, preferred_element_type=F32)
    middle = lax.dot_general(weighted, rows, NT, precision=PRECISE, preferred_element_type=F32)
    own = lax.broadcasted_iota(jnp.int32, middle.shape, 0) // RANK + offset // RANK
    middle = jnp.where(
        lax.broadcasted_iota(jnp.int32, middle.shape, 1) // RANK == own, middle, 0.0
    )
    under = (((0,), (0,)), ((), ()))
    high, low = split_parts(reduced)
    both = lax.dot_general(high, grads_low, under, preferred_element_type=F32)
    both = both + lax.dot_general(low, grads_low, under, preferred_element_type=F32)
    return narrow, middle, 2.0 * both[offset : offset + rank]


def terms_kernel(
    grad_ref, z_ref, scale_ref, slope_ref, outer_ref, reduced_ref,
    rows_ref, sum_ref, product_ref, narrow_ref, middle_ref, *, offset,
):
    count = grad_ref.shape[0]
    rank = outer_ref.shape[0]
    grads = grad_ref[...]
    sums = jnp.sum(grads * z_ref[...], axis=0, keepdims=True)
    sum_ref[...] = sums
    low = (grads * scale_ref[...]).astype(BF)
    weighted = (sums * slope_ref[...]) * outer_ref[...]
    high_part, low_part = split_rows(weighted)
    rows_ref[:count, :] = low
    rows_ref[count : count + rank, :] = high_part
    rows_ref[count + rank :, :] = low_part
    narrow, middle, product = terms_of(
        low, weighted, outer_ref[...], reduced_ref[...], offset
    )
    product_ref[...] = product

    @pl.when(pl.program_id(0) == 0)
    def _():
        narrow_ref[...] = narrow
        middle_ref[...] = middle

    @pl.when(pl.program_id(0) > 0)
    def _():
        narrow_ref[...] += narrow
        middle_ref[...] += middle


def grad_terms(grads, z, scale, slope, outer, offset, reduced, tile=512):
    count, cols = grads.shape
    rank = outer.shape[0]
    tiled = lambda rows: pl.BlockSpec((rows, tile), lambda n: (0, n))
    fixed = lambda rows, width: pl.BlockSpec((rows, width), lambda n: (0, 0))
    return pl.pallas_call(
        functools.partial(terms_kernel, offset=offset),
        grid=(cols // tile,),
        in_specs=[
            tiled(count), tiled(count), tiled(1), tiled(1), tiled(rank),
            fixed(count, reduced.shape[1]),
        ],
        out_specs=[
            tiled(count + 2 * rank), tiled(1), tiled(rank), fixed(count, EXTRA), fixed(rank, EXTRA),
        ],
        out_shape=[
            jax.ShapeDtypeStruct((count + 2 * rank, cols), BF),
            jax.ShapeDtypeStruct((1, cols), F32),
            jax.ShapeDtypeStruct((rank, cols), F32),
            jax.ShapeDtypeStruct((count, EXTRA), F32),
            jax.ShapeDtypeStruct((rank, EXTRA), F32),
        ],
        compiler_params=pltpu.CompilerParams(vmem_limit_bytes=40 << 20),
        cost_estimate=pl.CostEstimate(flops=COST, bytes_accessed=COST, transcendentals=0),
    )(grads, z, scale, slope, outer, reduced)


def pack_kernel(inputs_ref, first_ref, out_ref, turned_ref, *, offset, rank):
    reduced = jnp.dot(inputs_ref[...], first_ref[...], preferred_element_type=F32)
    high, low = split_parts(reduced)
    pick = lambda part: part.astype(F32)[:, offset : offset + rank]
    count = inputs_ref.shape[0]
    packed = jnp.concatenate(
        [pick(high), pick(low), jnp.zeros((count, EXTRA - 2 * rank), F32)], axis=1
    )
    out_ref[...] = packed.astype(BF)
    turned_ref[...] = packed.T.astype(BF)


def pack_reduced(inputs, first, offset, rank):
    count = inputs.shape[0]
    return pl.pallas_call(
        functools.partial(pack_kernel, offset=offset, rank=rank),
        out_shape=[
            jax.ShapeDtypeStruct((count, EXTRA), BF),
            jax.ShapeDtypeStruct((EXTRA, count), BF),
        ],
        cost_estimate=pl.CostEstimate(flops=COST, bytes_accessed=COST, transcendentals=0),
    )(inputs, first)


def mlp_kernel(
    place_ref, inputs_ref, packed_ref, turned_ref, scale_ref, slope_ref, outer_ref,
    down_grad_ref, narrow_down_ref, first_ref, down_ref, *refs, offset,
):
    slots, kept = refs[:-8], refs[-8:]
    hidden_ref, rows_ref, sum_ref, product_ref, narrow_ref, middle_ref, z_ref, back_ref = kept
    rows = slots[0].shape[0]
    half = hidden_ref.shape[1]
    count = hidden_ref.shape[0]
    gate_lanes = lax.broadcasted_iota(jnp.int32, (RANK, 2 * half), 1) < half
    outer = jnp.concatenate(
        [
            jnp.where(gate_lanes, outer_ref[...], 0.0),
            jnp.where(gate_lanes, 0.0, outer_ref[...]),
        ],
        axis=0,
    )
    rank = outer.shape[0]
    doubled = 2.0 * outer.astype(BF).astype(F32)
    pad = jnp.zeros((EXTRA - 2 * rank, 2 * half), F32)
    z = jnp.dot(
        packed_ref[...],
        jnp.concatenate([doubled, doubled, pad], axis=0).astype(BF),
        preferred_element_type=F32,
    )
    for slot, ref in enumerate(slots):
        z = z + jnp.dot(
            inputs_ref[:, pl.ds(place_of(place_ref, slot, rows), rows)],
            ref[...],
            preferred_element_type=F32,
        )
    z_ref[...] = z
    back_ref[...] = lax.dot_general(
        down_grad_ref[...], down_ref[...], NT, preferred_element_type=F32
    ) + lax.dot_general(narrow_down_ref[...], first_ref[...], NT, preferred_element_type=F32)
    scale = scale_ref[...]
    step = 64
    gate_sums = jnp.zeros((8, half), F32)
    up_sums = jnp.zeros((8, half), F32)

    def eighth(values):
        return jnp.sum(values.reshape(step // 8, 8, half), axis=0)

    for begin in range(0, count, step):
        at = slice(begin, begin + step)
        gate_z, up_z = z_ref[at, :half], z_ref[at, half:]
        grad_hidden = back_ref[at, :]
        gate = gate_z * scale[:, :half]
        up = up_z * scale[:, half:]
        sigmoid = 0.5 * jnp.tanh(0.5 * gate) + 0.5
        silu = gate * sigmoid
        hidden_ref[at, :] = (silu * up).astype(BF)
        grad_up = grad_hidden * silu
        grad_gate = grad_hidden * up * (sigmoid + silu * (1.0 - sigmoid))
        gate_sums = gate_sums + eighth(grad_gate * gate_z)
        up_sums = up_sums + eighth(grad_up * up_z)
        rows_ref[at, :half] = (grad_gate * scale[:, :half]).astype(BF)
        rows_ref[at, half:] = (grad_up * scale[:, half:]).astype(BF)
    sums = jnp.concatenate(
        [
            jnp.sum(gate_sums, axis=0, keepdims=True),
            jnp.sum(up_sums, axis=0, keepdims=True),
        ],
        axis=1,
    )
    sum_ref[...] = sums
    low = rows_ref[:count, :]
    weighted = (sums * slope_ref[...]) * outer
    high_part, low_part = split_rows(weighted)
    rows_ref[count : count + rank, :] = high_part
    rows_ref[count + rank :, :] = low_part
    placed = set_rows(outer, offset)
    narrow = 2.0 * lax.dot_general(low, placed.astype(BF), NT, preferred_element_type=F32)
    middle = lax.dot_general(weighted, placed, NT, precision=PRECISE, preferred_element_type=F32)
    both = jnp.dot(turned_ref[...], low, preferred_element_type=F32)
    product = 2.0 * (both[:rank] + both[rank : 2 * rank])
    product_ref[:, :half] = product[: rank // 2, :half]
    product_ref[:, half:] = product[rank // 2 :, half:]

    @pl.when(pl.program_id(0) == 0)
    def _():
        narrow_ref[...] = narrow
        middle_ref[...] = middle

    @pl.when(pl.program_id(0) > 0)
    def _():
        narrow_ref[...] += narrow
        middle_ref[...] += middle


def mlp_block(
    place, inputs, packs, offset, scale, slope, outer, down_grad, narrow_down, down, slots, start
):
    rows, cols = slots[0].shape
    count = inputs.shape[0]
    rank = 2 * RANK
    tile = 256
    skip = start // tile
    fixed = lambda array: pl.BlockSpec(array.shape, lambda n, s: (0, 0))
    tiled = lambda rows: pl.BlockSpec((rows, tile), lambda n, s: (0, n))
    late = lambda rows: pl.BlockSpec((rows, tile), lambda n, s: (0, n + skip))
    kept = lambda rows: pl.BlockSpec((rows, EXTRA), lambda n, s: (0, 0))
    return pl.pallas_call(
        functools.partial(mlp_kernel, offset=offset),
        grid_spec=pltpu.PrefetchScalarGridSpec(
            num_scalar_prefetch=1,
            grid=(cols // tile,),
            in_specs=[
                fixed(inputs), fixed(packs[0]), fixed(packs[1]), late(1), late(1), late(RANK),
                fixed(down_grad), fixed(narrow_down),
                pl.BlockSpec((tile // 2, 128), lambda n, s: (n + skip, D // 128)),
                pl.BlockSpec((tile // 2, D), lambda n, s: (n + skip, 0)),
            ]
            + [tiled(rows) for _ in slots],
            out_specs=[
                pl.BlockSpec((count, tile // 2), lambda n, s: (0, n)),
                tiled(count + 2 * rank),
                tiled(1),
                tiled(RANK),
                kept(count),
                kept(rank),
            ],
            scratch_shapes=[
                pltpu.VMEM((count, tile), F32),
                pltpu.VMEM((count, tile // 2), F32),
            ],
        ),
        out_shape=[
            jax.ShapeDtypeStruct((count, cols // 2), BF),
            jax.ShapeDtypeStruct((count + 2 * rank, cols), BF),
            jax.ShapeDtypeStruct((1, cols), F32),
            jax.ShapeDtypeStruct((RANK, cols), F32),
            jax.ShapeDtypeStruct((count, EXTRA), F32),
            jax.ShapeDtypeStruct((rank, EXTRA), F32),
        ],
        compiler_params=pltpu.CompilerParams(vmem_limit_bytes=48 << 20),
        cost_estimate=pl.CostEstimate(flops=COST, bytes_accessed=COST, transcendentals=0),
    )(place, inputs, *packs, scale, slope, outer, down_grad, narrow_down, down, down, *slots)


def down_kernel(*refs, bounds):
    hiddens, (weights_ref, first_ref, outer_ref) = refs[:-6], refs[-6:-3]
    keep_ref, send_ref, reduced_ref = refs[-3:]

    @pl.when(pl.program_id(0) == 0)
    def _():
        reduced_ref[...] = jnp.zeros_like(reduced_ref)
        for (start, stop), ref in zip(bounds, hiddens):
            reduced_ref[...] += jnp.dot(
                ref[...], first_ref[start:stop, :], preferred_element_type=F32
            )

    lane = lax.broadcasted_iota(jnp.int32, reduced_ref.shape, 1)
    total = low_rank(jnp.where(lane < RANK, reduced_ref[...], 0.0), outer_ref[...], 0)
    for (start, stop), ref in zip(bounds, hiddens):
        total = total + jnp.dot(
            ref[...], weights_ref[start:stop, :], preferred_element_type=F32
        )
    count = keep_ref.shape[0]
    keep_ref[...] = total[:count]
    send_ref[...] = total[count:].astype(BF)


def down_forward(hiddens, bounds, down, outer, tile=256):
    count = hiddens[0].shape[0]
    rows = down.shape[0]
    return pl.pallas_call(
        functools.partial(down_kernel, bounds=bounds),
        grid=(D // tile,),
        in_specs=[pl.BlockSpec(hidden.shape, lambda n: (0, 0)) for hidden in hiddens]
        + [
            pl.BlockSpec((rows, tile), lambda n: (0, n)),
            pl.BlockSpec((rows, EXTRA), lambda n: (0, D // EXTRA)),
            pl.BlockSpec((RANK, tile), lambda n: (0, n)),
        ],
        out_specs=[
            pl.BlockSpec((count // 2, tile), lambda n: (0, n)),
            pl.BlockSpec((count // 2, tile), lambda n: (0, n)),
            pl.BlockSpec((count, EXTRA), lambda n: (0, 0)),
        ],
        out_shape=[
            jax.ShapeDtypeStruct((count // 2, D), F32),
            jax.ShapeDtypeStruct((count // 2, D), BF),
            jax.ShapeDtypeStruct((count, EXTRA), F32),
        ],
        compiler_params=pltpu.CompilerParams(vmem_limit_bytes=40 << 20),
        cost_estimate=pl.CostEstimate(flops=COST, bytes_accessed=COST, transcendentals=0),
    )(*hiddens, down, down, outer)


def kv_form_kernel(z_ref, scale_ref, cos_ref, sin_ref, out_ref):
    lane = lax.broadcasted_iota(jnp.int32, cos_ref.shape, 1)
    half = z_ref.shape[1] // 2
    for pair in range(half // 128):
        at = slice(pair * 128, (pair + 1) * 128)
        to = slice(half + pair * 128, half + (pair + 1) * 128)
        keys = turn_lanes(z_ref[:, at] * scale_ref[:, at], cos_ref[...], sin_ref[...])
        values = z_ref[:, to] * scale_ref[:, to]
        first = jnp.where(lane < HD, keys, pltpu.roll(values, HD, 1))
        second = jnp.where(lane < HD, pltpu.roll(keys, HD, 1), values)
        out_ref[:, 2 * pair * 128 : (2 * pair + 1) * 128] = first.astype(BF)
        out_ref[:, (2 * pair + 1) * 128 : (2 * pair + 2) * 128] = second.astype(BF)


def kv_form(z, scale, cosine, sine):
    return pl.pallas_call(
        kv_form_kernel,
        out_shape=jax.ShapeDtypeStruct(z.shape, BF),
        cost_estimate=pl.CostEstimate(flops=COST, bytes_accessed=COST, transcendentals=0),
    )(z, scale, cosine, sine)


def kv_back_kernel(sum_ref, cos_ref, sin_ref, out_ref):
    lane = lax.broadcasted_iota(jnp.int32, cos_ref.shape, 1)
    half = sum_ref.shape[1] // 2
    for pair in range(half // 128):
        first = sum_ref[:, 2 * pair * 128 : (2 * pair + 1) * 128].astype(F32)
        second = sum_ref[:, (2 * pair + 1) * 128 : (2 * pair + 2) * 128].astype(F32)
        keys = jnp.where(lane < HD, first, pltpu.roll(second, HD, 1))
        values = jnp.where(lane < HD, pltpu.roll(first, HD, 1), second)
        out_ref[:, pair * 128 : (pair + 1) * 128] = turn_lanes(keys, cos_ref[...], -sin_ref[...])
        out_ref[:, half + pair * 128 : half + (pair + 1) * 128] = values


def kv_back(sums, cosine, sine):
    return pl.pallas_call(
        kv_back_kernel,
        out_shape=jax.ShapeDtypeStruct(sums.shape, F32),
        cost_estimate=pl.CostEstimate(flops=COST, bytes_accessed=COST, transcendentals=0),
    )(sums, cosine, sine)


def pack_all_kernel(
    query_ref, kv_ref, out_ref_, mlp_ref, down_ref, one_ref, first_out_ref, pairs_ref, down_first_ref,
    place_ref, packed_ref, wide_rows, hold, down_rows, *, toks, part, layout,
):
    tall, low, lanes, share, hidden_share, outer_share = layout
    many = wide_rows.shape[0]
    wides = packed_ref.shape[0] // toks
    for n, ref in ((0, query_ref), (1, kv_ref), (3, out_ref_), (6, down_ref)):
        wide_rows[: RANK + 1, STARTS[n] : STARTS[n] + ref.shape[1]] = ref[...]
    blocks = FF // (4 * part)
    down_rows[...] = jnp.zeros_like(down_rows)
    for side in range(2):
        start = STARTS[4 + side]
        wide_rows[:, start : start + FF] = jnp.zeros((many, FF), F32)
        for tile in range(blocks * part // 128):
            hold[: RANK + 1, tile * 128 : (tile + 1) * 128] = mlp_ref[
                :, (2 * tile + side) * 128 : (2 * tile + side + 1) * 128
            ]
        for quarter in range(4):

            @pl.when(place_ref[2] == quarter)
            def _():
                for at in range(blocks):
                    to = start + (at * 4 + quarter) * part
                    wide_rows[: RANK + 1, to : to + part] = hold[
                        : RANK + 1, at * part : (at + 1) * part
                    ]
    for quarter in range(4):

        @pl.when(place_ref[2] == quarter)
        def _():
            for at in range(blocks):
                to = (at * 4 + quarter) * part
                down_rows[:, to : to + part] = down_first_ref[:, at * part : (at + 1) * part]

    packed_ref[...] = jnp.zeros_like(packed_ref)
    sources = [(0, one_ref), (3 * RANK, first_out_ref), (4 * RANK, pairs_ref)]

    def main_piece(start, rows, cols):
        parts = []
        while rows:
            base, ref = [pair for pair in sources if pair[0] <= start][-1]
            here = min(rows, base + ref.shape[0] - start)
            parts.append(ref[start - base : start - base + here, cols])
            start, rows = start + here, rows - here
        return parts[0] if len(parts) == 1 else jnp.concatenate(parts, axis=0)

    fit = lanes // share
    for tok in range(toks):
        for wide in range(wides):
            at = tok * wides + wide
            cols = slice(wide * share, (wide + 1) * share)
            for piece in range(fit):
                packed_ref[at, :tall, piece * share : (piece + 1) * share] = main_piece(
                    (tok * fit + piece) * tall, tall, cols
                )
            packed_ref[at, tall : tall + low, :hidden_share] = down_rows[
                tok * low : (tok + 1) * low, wide * hidden_share : (wide + 1) * hidden_share
            ]
            packed_ref[at, tall + low : tall + low + RANK + 1, :outer_share] = wide_rows[
                : RANK + 1, at * outer_share : (at + 1) * outer_share
            ]


def pack_all(place, pieces, toks, part, layout):
    tall, low, lanes, share, hidden_share, outer_share = layout
    owners = OUTS // outer_share
    rows = -(-(tall + low + RANK + 1) // 8) * 8
    fixed = lambda array: pl.BlockSpec(array.shape, lambda *n: (0,) * array.ndim)
    shape = jax.ShapeDtypeStruct((owners, rows, lanes), F32)
    return pl.pallas_call(
        functools.partial(pack_all_kernel, toks=toks, part=part, layout=layout),
        grid=(1,),
        in_specs=[fixed(piece) for piece in pieces]
        + [pl.BlockSpec(memory_space=pltpu.SMEM)],
        out_specs=fixed(shape),
        out_shape=shape,
        scratch_shapes=[
            pltpu.VMEM((RANK + 8, OUTS), F32),
            pltpu.VMEM((RANK + 8, FF // 4), F32),
            pltpu.VMEM((RANK, FF), F32),
        ],
        compiler_params=pltpu.CompilerParams(vmem_limit_bytes=40 << 20),
        cost_estimate=pl.CostEstimate(flops=COST, bytes_accessed=COST, transcendentals=0),
    )(*pieces, place)


def mlp_back_kernel(
    place_ref, one_ref, two_ref, narrow_ref, middle_ref, first_ref, inputs_ref, *refs, offset, rank
):
    slots, (keep_ref, send_ref, out_ref, held_one, held_two, arrived) = refs[:-6], refs[-6:]
    each = len(slots) // 2
    rows = held_one.shape[1]
    count = inputs_ref.shape[0]
    copies = []
    for half, held in enumerate((held_one, held_two)):
        copies.append(
            [
                pltpu.make_async_copy(slots[half * each + i], held.at[i], arrived.at[half * each + i])
                for i in range(each)
            ]
        )
    for i in range(each):
        copies[0][i].start()
        copies[1][i].start()
    narrow_high, narrow_low = split_parts(narrow_ref[...])
    turned_high = narrow_high.astype(F32).T.astype(BF)
    turned_low = narrow_low.astype(F32).T.astype(BF)
    middle_high, middle_low = split_parts(middle_ref[...])
    for i in range(each):
        copies[0][i].wait()
        copies[1][i].wait()
        at = pl.ds(place_of(place_ref, i, rows), rows)
        first = first_ref[at, :]
        total = lax.dot_general(one_ref[...], held_one[i], NT, preferred_element_type=F32)
        total = total + lax.dot_general(two_ref[...], held_two[i], NT, preferred_element_type=F32)
        grad = (
            total[:count]
            + lax.dot_general(narrow_high, first, NT, preferred_element_type=F32)
            + lax.dot_general(narrow_low, first, NT, preferred_element_type=F32)
        )
        keep_ref[:, at] = grad[: count // 2]
        send_ref[:, at] = grad[count // 2 :].astype(BF)
        weighted = total[count : count + rank] + total[count + rank :]
        middle = lax.dot_general(middle_high, first, NT, preferred_element_type=F32)
        middle = middle + lax.dot_general(middle_low, first, NT, preferred_element_type=F32)
        inputs = inputs_ref[:, at]
        product = jnp.dot(turned_high, inputs, preferred_element_type=F32)
        product = product + jnp.dot(turned_low, inputs, preferred_element_type=F32)
        out_ref[:, at] = product[offset : offset + rank] + 2.0 * (weighted + 2.0 * middle)


def mlp_back(place, grads, narrow, middle, first, inputs, slots, offset):
    count = inputs.shape[0]
    rank = middle.shape[0]
    rows = slots[0][0].shape[0]
    many = len(slots[0])
    operands = [*grads, narrow, middle, first, inputs]
    fixed = lambda array: pl.BlockSpec(array.shape, lambda n, s: (0, 0))
    shapes = [
        jax.ShapeDtypeStruct((count // 2, D), F32),
        jax.ShapeDtypeStruct((count // 2, D), BF),
        jax.ShapeDtypeStruct((rank, D), F32),
    ]
    return pl.pallas_call(
        functools.partial(mlp_back_kernel, offset=offset, rank=rank),
        grid_spec=pltpu.PrefetchScalarGridSpec(
            num_scalar_prefetch=1,
            grid=(1,),
            in_specs=[fixed(array) for array in operands]
            + [pl.BlockSpec(memory_space=pl.ANY) for _ in range(2 * many)],
            out_specs=[fixed(shape) for shape in shapes],
            scratch_shapes=[
                pltpu.VMEM((many, rows, grads[0].shape[1]), BF),
                pltpu.VMEM((many, rows, grads[1].shape[1]), BF),
                pltpu.SemaphoreType.DMA((2 * many,)),
            ],
        ),
        out_shape=shapes,
        compiler_params=pltpu.CompilerParams(vmem_limit_bytes=60 << 20),
        cost_estimate=pl.CostEstimate(flops=COST, bytes_accessed=COST, transcendentals=0),
    )(place, *operands, *slots[0], *slots[1])


def column_sums(base, first_high, first_low, outer, offset):
    outer_high, outer_low = split_parts(set_rows(outer, offset))
    product = (
        jnp.dot(first_high, outer_high, preferred_element_type=F32)
        + jnp.dot(first_high, outer_low, preferred_element_type=F32)
        + jnp.dot(first_low, outer_high, preferred_element_type=F32)
    )
    merged = base.astype(F32) + 2.0 * product
    merged_high, merged_low = split_parts(merged)
    under = (((0,), (0,)), ((), ()))
    cross = (
        lax.dot_general(first_high, merged_high, under, preferred_element_type=F32)
        + lax.dot_general(first_high, merged_low, under, preferred_element_type=F32)
        + lax.dot_general(first_low, merged_high, under, preferred_element_type=F32)
    )
    return jnp.sum(merged * merged, axis=0, keepdims=True), cross[offset : offset + RANK]


def widened(first):
    return jnp.concatenate(
        [first, jnp.zeros((first.shape[0], EXTRA - first.shape[1]), first.dtype)], axis=1
    )


def early_kernel(
    place_ref, query_ref, key_ref, value_ref, main_ref, outer_ref, shard_out, square_ref, cross_ref,
):
    half = query_ref.shape[1] // 2
    kv_cols = key_ref.shape[1]
    high, low = split_parts(widened(main_ref[...]))
    shard_out[:, half + kv_cols :] = high
    for core in range(2):

        @pl.when(place_ref[1] == core)
        def _():
            shard_out[:, :half] = query_ref[:, core * half : (core + 1) * half]
            kv = (key_ref, value_ref)[core][...]
            shard_out[:, half : half + kv_cols] = kv
            start = 2 * half + core * kv_cols
            square, cross = column_sums(
                kv, high, low, outer_ref[:, start : start + kv_cols], (1 + core) * RANK
            )
            square_ref[:, :kv_cols] = square
            cross_ref[:, :kv_cols] = cross
            for tile in range(half // 256):
                at = core * half + tile * 256
                square, cross = column_sums(
                    query_ref[:, at : at + 256], high, low, outer_ref[:, at : at + 256], 0
                )
                to = kv_cols + tile * 256
                square_ref[:, to : to + 256] = square
                cross_ref[:, to : to + 256] = cross


def early_work(place, query, key, value, main, outer):
    rows, cols = query.shape
    kv_cols = key.shape[1]
    fixed = lambda array: pl.BlockSpec(array.shape, lambda n, s: (0, 0))
    shapes = [
        jax.ShapeDtypeStruct((rows, cols // 2 + kv_cols + EXTRA), BF),
        jax.ShapeDtypeStruct((1, kv_cols + cols // 2), F32),
        jax.ShapeDtypeStruct((RANK, kv_cols + cols // 2), F32),
    ]
    return pl.pallas_call(
        early_kernel,
        grid_spec=pltpu.PrefetchScalarGridSpec(
            num_scalar_prefetch=1,
            grid=(1,),
            in_specs=[fixed(query), fixed(key), fixed(value), fixed(main)]
            + [pl.BlockSpec((RANK, cols + 2 * kv_cols), lambda n, s: (0, 0))],
            out_specs=[fixed(shape) for shape in shapes],
        ),
        out_shape=shapes,
        compiler_params=pltpu.CompilerParams(vmem_limit_bytes=32 << 20),
        cost_estimate=pl.CostEstimate(flops=COST, bytes_accessed=COST, transcendentals=0),
    )(place, query, key, value, main, outer)


def later_kernel(
    place_ref, out_w_ref, gate_ref, up_ref, down_w_ref, main_ref, first_ref, outer_ref, mags_ref,
    out_out, mlp_out, down_out, square_ref, cross_ref, picked_ref, hold, *, part,
):
    half = out_out.shape[1]
    width = gate_ref.shape[1]
    blocks = width // (4 * part)
    cols = blocks * part
    starts = [STARTS[n] for n in range(7)]
    high, low = split_parts(widened(main_ref[...]))
    down_first = widened(first_ref[...])
    down_high, down_low = split_parts(down_first)
    rows = gate_ref.shape[0]
    lanes = mags_ref.shape[0]
    for quarter in range(4):

        @pl.when(place_ref[2] == quarter)
        def _():
            for side, ref in enumerate((gate_ref, up_ref)):
                for at in range(blocks):
                    start = (at * 4 + quarter) * part
                    hold[side, :rows, at * part : (at + 1) * part] = ref[
                        :, start : start + part
                    ].astype(F32)
                    begin = starts[4 + side] + start
                    hold[side, rows : rows + RANK, at * part : (at + 1) * part] = outer_ref[
                        :, begin : begin + part
                    ]
                    hold[side, rows + RANK :, at * part : (at + 1) * part] = mags_ref[
                        :, begin : begin + part
                    ]
    for tile in range(cols // 128):
        for side in range(2):
            to = slice((2 * tile + side) * 128, (2 * tile + side + 1) * 128)
            taken = hold[side, :, tile * 128 : (tile + 1) * 128]
            base = taken[:rows].astype(BF)
            mlp_out[:, to] = base
            outer = taken[rows : rows + RANK]
            picked_ref[:RANK, to] = outer
            picked_ref[RANK:, to] = taken[rows + RANK :]
            square, cross = column_sums(base, high, low, outer, (4 + side) * RANK)
            square_ref[:, half + to.start : half + to.stop] = square
            cross_ref[:, half + to.start : half + to.stop] = cross
    down_at = pl.ds(pl.multiple_of(place_ref[2] * part, 16 if part % 16 == 0 else 8), part)
    down_out[:, : 2 * half] = down_w_ref[down_at, :]
    factor = first_ref[down_at, :]
    factor = jnp.concatenate([factor, factor], axis=1)
    down_out[:, 2 * half :] = widened(factor).astype(BF)
    for core in range(2):

        @pl.when(place_ref[1] == core)
        def _():
            out_out[...] = out_w_ref[:, core * half : (core + 1) * half]
            for tile in range(half // 256):
                at = core * half + tile * 256
                square, cross = column_sums(
                    out_w_ref[:, at : at + 256],
                    high,
                    low,
                    outer_ref[:, starts[3] + at : starts[3] + at + 256],
                    3 * RANK,
                )
                to = slice(tile * 256, (tile + 1) * 256)
                square_ref[:, to] = square
                cross_ref[:, to] = cross
                square, cross = column_sums(
                    down_w_ref[:, at : at + 256],
                    down_high,
                    down_low,
                    outer_ref[:, starts[6] + at : starts[6] + at + 256],
                    0,
                )
                begin = half + 2 * cols + tile * 256
                square_ref[:, begin : begin + 256] = square
                cross_ref[:, begin : begin + 256] = cross


def later_work(place, out_w, gate, up, down_w, main, first, outer, mags, part):
    rows, cols = out_w.shape
    half = cols // 2
    mlp = 2 * (gate.shape[1] // 4)
    total = 2 * half + mlp
    fixed = lambda array: pl.BlockSpec(array.shape, lambda n, s: (0, 0))
    inputs = [out_w, gate, up, down_w, main, first, outer, mags]
    shapes = [
        jax.ShapeDtypeStruct((rows, half), BF),
        jax.ShapeDtypeStruct((rows, mlp), BF),
        jax.ShapeDtypeStruct((part, cols + EXTRA), BF),
        jax.ShapeDtypeStruct((1, total), F32),
        jax.ShapeDtypeStruct((RANK, total), F32),
        jax.ShapeDtypeStruct((RANK + 8, mlp), F32),
    ]
    return pl.pallas_call(
        functools.partial(later_kernel, part=part),
        grid_spec=pltpu.PrefetchScalarGridSpec(
            num_scalar_prefetch=1,
            grid=(1,),
            in_specs=[fixed(array) for array in inputs],
            out_specs=[fixed(shape) for shape in shapes],
            scratch_shapes=[pltpu.VMEM((2, rows + RANK + 8, mlp // 2), F32)],
        ),
        out_shape=shapes,
        compiler_params=pltpu.CompilerParams(vmem_limit_bytes=48 << 20),
        cost_estimate=pl.CostEstimate(flops=COST, bytes_accessed=COST, transcendentals=0),
    )(place, *inputs)


def shards(
    tokens,
    cotangent,
    gain_attn,
    gain_ffn,
    w_query,
    w_key,
    w_value,
    w_output,
    w_gate,
    w_up,
    w_down,
    adapt_main,
    adapt_down,
    adapt_outer,
    magnitudes,
    main_first,
    main_second,
    down_first,
    down_second,
    outer_first,
    outer_second,
    mag_first,
    mag_second,
    segments,
):
    wide_count = lax.axis_size("wide")
    tok_count = lax.axis_size("tok")
    wide = lax.axis_index("wide")
    tok = lax.axis_index("tok")
    core = tok % 2
    place = jnp.stack([wide, core, tok % 4]).astype(jnp.int32)
    quarter = (tok % 4).astype(jnp.int32)[None]
    length, share = tokens.shape
    hidden_share = w_down.shape[0]
    part = hidden_share // 4
    block = length // (wide_count * CHUNKS)
    count = CHUNKS * block
    block_cols = wide_count * part
    half = D // 2
    kv_cols = KVH * HD

    def partner(array):
        return swap(array, "tok", 2)

    def other_core(array):
        return swap(array, "tok", 1)

    across = wide_count // 4
    deep, side = wide // across, wide % across

    def to_tokens(features):
        many = features.shape[0]
        pieces = features.reshape(many, CHUNKS, 4, across, block, share)
        rows = jnp.zeros((4, many, CHUNKS, block, across * share), features.dtype)
        for slot in range(across):
            piece = lax.dynamic_index_in_dim(pieces, side ^ slot, 3, keepdims=False)
            piece = jnp.moveaxis(piece, 2, 0)
            if slot:
                piece = swap(piece, "wide", slot)
            rows = lax.dynamic_update_slice(rows, piece, (0, 0, 0, 0, (side ^ slot) * share))
        whole = jnp.zeros((many, count, D), features.dtype)
        for slot in range(4):
            piece = lax.dynamic_index_in_dim(rows, deep ^ slot, 0, keepdims=False)
            piece = piece.reshape(many, count, across * share)
            if slot:
                piece = swap(piece, "wide", slot * across)
            whole = lax.dynamic_update_slice(
                whole, piece, (0, 0, (deep ^ slot) * across * share)
            )
        return whole

    def from_tokens_deep(rows):
        cols = across * share
        held = jnp.zeros((CHUNKS, 4, block, cols), rows.dtype)
        for slot in range(4):
            piece = lax.dynamic_slice(rows, (0, (deep ^ slot) * cols), (count, cols))
            if slot:
                piece = swap(piece, "wide", slot * across)
            piece = piece.reshape(CHUNKS, 1, block, cols)
            held = lax.dynamic_update_slice(held, piece, (0, deep ^ slot, 0, 0))
        return held

    def from_tokens(rows):
        return from_tokens_side(from_tokens_deep(rows))

    def from_tokens_side(held):
        whole = jnp.zeros((CHUNKS, 4, across, block, share), held.dtype)
        for slot in range(across):
            piece = lax.dynamic_slice_in_dim(held, (side ^ slot) * share, share, 3)
            if slot:
                piece = swap(piece, "wide", slot)
            whole = lax.dynamic_update_slice(whole, piece[:, :, None], (0, 0, side ^ slot, 0, 0))
        return whole.reshape(length, share)

    def own_half(array, axis=-1):
        size = array.shape[axis] // 2
        return lax.dynamic_slice_in_dim(array, core * size, size, axis)

    def in_order(blocks):
        return jnp.where(
            core == 0, jnp.concatenate(blocks, axis=-1), jnp.concatenate(blocks[::-1], axis=-1)
        )

    def by_core(zero, one, flip=0):
        return jnp.where(core == flip, zero, one)

    def sides(array, n):
        return array[..., STARTS[n] : STARTS[n] + WIDTHS[n]]

    ends = [0, kv_cols, kv_cols + half, kv_cols + 2 * half, kv_cols + 2 * half + 2 * block_cols]
    ends.append(ends[-1] + half)

    def cut(array, n):
        return array[..., ends[n] : ends[n + 1]]

    KV, QUERY, OUT, MLP, DOWN = range(5)

    both_rows = to_tokens(jnp.stack([tokens, cotangent]))
    residual, upstream = both_rows[0].astype(F32), both_rows[1].astype(F32)
    gain_parts = jnp.stack([gain_attn, gain_ffn], axis=1)
    split = [lax.reduce_precision(gain_parts, 8, 7)]
    split.append(lax.reduce_precision(gain_parts - split[0], 8, 7))
    split.append(gain_parts - split[0] - split[1])
    qkv_shard, squares, soon_cross = early_work(
        place, w_query, w_key, w_value, jnp.concatenate([adapt_main, *split], axis=1), adapt_outer
    )
    qkv_slots = [gather_slots(qkv_shard)]
    mags = magnitudes[None]
    out_shard, mlp_shard, down_shard, rest_squares, rest_cross, picked = later_work(
        place, after(w_output, *near(qkv_slots[0])), w_gate, w_up, w_down, adapt_main, adapt_down,
        adapt_outer, jnp.broadcast_to(mags, (8, OUTS)), part,
    )
    squares = jnp.concatenate([squares, rest_squares], axis=1)
    crosses = jnp.concatenate([soon_cross, rest_cross], axis=1)
    for bit in bits_of(wide_count):
        sent = jnp.concatenate([crosses.astype(BF), *two_parts(squares)])
        sent = swap(sent, "wide", bit).astype(F32)
        crosses = crosses + sent[:RANK]
        squares = squares + (sent[RANK : RANK + 1] + sent[RANK + 1 :])
    norms_own = jnp.sqrt(squares)
    mags_own = jnp.concatenate(
        [
            by_core(sides(mags, 1), sides(mags, 2)),
            own_half(sides(mags, 0)),
            own_half(sides(mags, 3)),
            picked[RANK : RANK + 1],
            own_half(sides(mags, 6)),
        ],
        axis=1,
    )
    own_rows = jnp.concatenate([crosses, mags_own, norms_own])
    rows_by = [own_rows, other_core(own_rows)]
    cross_by = [rows[:RANK] for rows in rows_by]
    scale_by, slope_by, norms_by = [], [], []
    for rows in rows_by:
        mags_row, norm = rows[RANK : RANK + 1], rows[RANK + 1 :]
        scale, slope = mags_row / norm, -mags_row / (norm * norm * norm)
        for found, row in ((scale_by, scale), (slope_by, slope), (norms_by, norm)):
            found.append([cut(row, n) for n in range(5)])
    mlp_outer = [picked[:RANK]]

    def natural_of(parts, n):
        return in_order([p[n] for p in parts])

    scales, slopes, norms = (
        [natural_of(parts, n) if n != MLP else None for n in range(5)]
        for parts in (scale_by, slope_by, norms_by)
    )
    outers = [sides(adapt_outer, n) for n in range(7)]
    outer_kv = jnp.concatenate(
        [jnp.pad(outers[1], ((0, 0), (0, kv_cols))), jnp.pad(outers[2], ((0, 0), (kv_cols, 0)))]
    )

    qkv_slots.append({s: other_core(held) for s, held in qkv_slots[0].items()})
    low_main = put_rows(
        {s: held[:, half + kv_cols :] for s, held in qkv_slots[0].items()},
        jnp.zeros((0, EXTRA), BF),
    )
    gains = low_main[:, 6 * RANK : 6 * RANK + 6].astype(F32).T
    gains = (gains[4:6] + gains[2:4]) + gains[:2]

    def main_cols(n, many=1):
        return low_main[:, n * RANK : (n + many) * RANK]

    def norm_rows(values, gain_row):
        inverse = lax.rsqrt(jnp.mean(values * values, axis=1, keepdims=True) + EPS_NORM)
        return (values * inverse * gain_row[None, :]).astype(BF), inverse

    def norm_rows_back(values, gain_row, inverse, grad_normed):
        inner = jnp.sum(values * gain_row[None, :] * grad_normed, axis=1, keepdims=True)
        return (
            grad_normed * gain_row[None, :] * inverse
            - values * (inverse * inverse * inverse * inner / D)
        )

    def ordered(slots):
        return [slots[s] for s in range(wide_count)]

    own_places = (
        jnp.arange(CHUNKS, dtype=jnp.int32)[:, None] * (wide_count * block)
        + wide * block
        + jnp.arange(block, dtype=jnp.int32)[None, :]
    ).reshape(count)
    segment_row = after(segments, residual)[0]
    own_segment = lax.dynamic_index_in_dim(
        segment_row.reshape(CHUNKS, wide_count, block), wide, 1, keepdims=False
    ).reshape(count)
    own_starts = jnp.sum(
        (segment_row[None, :] < own_segment[:, None]).astype(jnp.int32), axis=1
    )
    frequency = ROPE_BASE ** (-2.0 * jnp.arange(HD // 2, dtype=F32) / HD)
    angles = (own_places - own_starts).astype(F32)[:, None] * frequency[None, :]
    cosine = jnp.tile(jnp.cos(angles), (1, 4))
    sine = jnp.tile(jnp.concatenate([-jnp.sin(angles), jnp.sin(angles)], axis=1), (1, 2))
    place_rows = jnp.tile(own_places.reshape(CHUNKS, 1, block), (1, 1, GROUP))
    start_rows = jnp.tile(own_starts.reshape(CHUNKS, 1, block), (1, 1, GROUP))
    first_block = own_starts.reshape(CHUNKS, block)[:, 0] // (wide_count * block)

    ready = residual
    normed_one, inverse_one = norm_rows(ready, gains[0])
    kv_z, reduced_one = slot_mm(
        place, normed_one, low_main, outer_kv, RANK, [ordered(qkv_slots[k]) for k in range(2)], half
    )
    kv = kv_form(kv_z, scales[KV], cosine, sine)
    token_slots = gather_slots(kv.reshape(CHUNKS, 1, block, KVH * 2 * HD))

    kv = jnp.zeros((CHUNKS, wide_count, block, KVH * 2 * HD), BF)
    for slot, held in token_slots.items():
        kv = lax.dynamic_update_slice(kv, held, (0, wide ^ slot, 0, 0))
    kv = kv.reshape(length, KVH * 2 * HD)
    kvt = kv.T.reshape(KVH, 2 * HD, length)
    query_z, _ = slot_mm(
        place, normed_one, low_main, outers[0], 0, [ordered(qkv_slots[k]) for k in range(2)]
    )
    queries, attended, log_total = attend(
        first_block, query_z, scales[QUERY], cosine, sine, place_rows, start_rows, kv, kvt
    )

    down_slots = gather_slots(after(down_shard, *near(token_slots)))
    out_slots = [gather_slots(after(out_shard, qkv_slots[0][wide_count - 1]), True)]
    out_slots.append({s: other_core(held) for s, held in out_slots[0].items()})
    down_weights = put_rows(down_slots, jnp.zeros((0, D + EXTRA), BF))
    tiles = 2 * block_cols // 256
    cuts = [0, (tiles + 1) // 2 * 256, 2 * block_cols]
    spans = [slice(cuts[i], cuts[i + 1]) for i in range(2)]
    mlp_slots = []
    before = near(down_slots)
    for i, span in enumerate(spans):
        mlp_slots.append(gather_slots(after(mlp_shard[:, span], *before), i == 0))
        before = near(mlp_slots[-1])

    output_z, reduced_out = slot_mm(
        place, attended, low_main, outers[3], 3 * RANK, [ordered(out_slots[k]) for k in range(2)]
    )
    hidden_one = residual + output_z * scales[OUT]

    normed_own, inverse_two = norm_rows(hidden_one, gains[1])
    def of_four(rows):
        pair = jnp.concatenate([rows, partner(rows)])
        return jnp.concatenate([pair, other_core(pair)])

    def to_owner_of_four(keep, sent):
        pair = keep + other_core(sent).astype(F32)
        swapped = partner(pair[count:].astype(BF))
        return pair[:count] + swapped.astype(F32), swapped

    normed_two = of_four(normed_own)
    down_low = (upstream * scales[DOWN]).astype(BF)
    down_low = of_four(down_low)
    narrow_down = 2.0 * mm_t(down_low, outers[6].astype(BF))
    narrow_down_lanes = lanes_of(narrow_down)
    packs = pack_reduced(normed_two, low_main, 4 * RANK, 2 * RANK)
    blocks = [
        mlp_block(
            place,
            normed_two,
            packs,
            4 * RANK,
            scale_by[0][MLP],
            slope_by[0][MLP],
            mlp_outer[0],
            down_low,
            narrow_down_lanes,
            down_weights,
            ordered(mlp_slots[i]),
            span.start,
        )
        for i, span in enumerate(spans)
    ]
    bounds = [(span.start // 2, span.stop // 2) for span in spans]
    down_keep, down_sent, reduced_down = down_forward([b[0] for b in blocks], bounds, down_weights, outers[6])
    reduced_down = reduced_down[:, :RANK]

    pairs = 2 * RANK
    keep, sent, first_pairs = mlp_back(
        place,
        [b[1] for b in blocks],
        sum(b[4] for b in blocks),
        sum(b[5] for b in blocks),
        low_main,
        normed_two,
        [ordered(slots) for slots in mlp_slots],
        4 * RANK,
    )
    grad_normed, swapped = to_owner_of_four(keep, sent)
    grad_mid = upstream + norm_rows_back(hidden_one, gains[1], inverse_two, grad_normed)
    down_pair = down_keep + other_core(after(down_sent, swapped)).astype(F32)

    def first_grads(rows, inputs, narrow, middle, factors, many):
        size = many * RANK
        parts = jnp.concatenate(two_parts(narrow), axis=1)
        product = fold_parts(t_mm(parts, inputs), size)
        same = jnp.arange(size)[:, None] // RANK == jnp.arange(size)[None, :] // RANK
        middle = jnp.where(same, middle[:, :size], 0.0)
        term = fold_parts(mm_t(jnp.concatenate(two_parts(middle)), factors), size)
        return product + 2.0 * (fold_parts(rows, size) + 2.0 * term)

    def twice(cols):
        return jnp.concatenate([cols, cols], axis=1)

    out_rows, scale_out, outer_out, narrow_out, middle_out = grad_terms(
        grad_mid, output_z, scales[OUT], slopes[OUT], outers[3], 3 * RANK, reduced_out
    )
    back_out = slot_back(place, out_rows, [ordered(out_slots[k]) for k in range(2)])
    grad_mixed, first_out = finish_back(
        [back_out], [RANK], narrow_out, middle_out, low_main, attended, 3 * RANK
    )
    grad_mixed = after(grad_mixed.astype(BF), down_pair)
    down_far = partner(down_pair[count:].astype(BF))
    down_z = down_pair[:count] + down_far.astype(F32)
    layer_rows = (hidden_one + down_z * scales[DOWN]).astype(BF)

    query_grad, kv_grad = attend_back(
        first_block, queries, cosine, sine, place_rows, start_rows, kv, kvt, log_total, attended,
        grad_mixed,
    )
    kv_grad = kv_grad.reshape(CHUNKS, wide_count, block, KVH * 2 * HD)
    kv_grad = jnp.swapaxes(after(kv_grad, down_far), 0, 1).astype(F32)
    bits = bits_of(wide_count)
    kv_half = KVH * HD
    kv_grad = jnp.concatenate(
        [
            scatter_sum(kv_grad[..., :kv_half], "wide", BF),
            scatter_sum(kv_grad[..., kv_half:], "wide", BF, [bits[-2], *bits[:-2], bits[-1]]),
        ],
        axis=-1,
    )
    layer_deep = from_tokens_deep(after(layer_rows, kv_grad))
    scale_down = jnp.sum(upstream * down_z, axis=0, keepdims=True)
    pair_down = scale_down + partner(scale_down)
    pair_down = pair_down + other_core(pair_down)
    weighted = (pair_down * slopes[DOWN]) * outers[6]
    middle_down = gram_of(weighted, outers[6])
    weighted_parts = jnp.pad(jnp.concatenate(two_parts(weighted)), ((0, 0), (0, EXTRA)))
    first_down = first_grads(
        mm_t(weighted_parts, down_weights),
        jnp.concatenate([b[0] for b in blocks], axis=1),
        narrow_down,
        middle_down,
        down_weights[:, D : D + RANK],
        1,
    )
    kv_grad = kv_back(
        after(kv_grad, first_down).reshape(count, KVH * 2 * HD), cosine, sine
    )
    layer_out = from_tokens_side(after(layer_deep, kv_grad))

    query_rows_low, scale_query, outer_query, narrow_query, middle_query = grad_terms(
        query_grad, query_z, scales[QUERY], slopes[QUERY], outers[0], 0, reduced_one
    )
    back_query = slot_back(place, query_rows_low, [ordered(qkv_slots[k]) for k in range(2)])
    kv_rows_low, scale_kv, outer_kv_grad, narrow_kv, middle_kv = grad_terms(
        kv_grad, kv_z, scales[KV], slopes[KV], outer_kv,
        RANK, reduced_one,
    )
    back_kv = slot_back(place, kv_rows_low, [ordered(qkv_slots[k]) for k in range(2)], half)
    grad_normed, first_one = finish_back(
        [back_query, after(back_kv, layer_deep)],
        [RANK, pairs],
        narrow_query + narrow_kv,
        jnp.concatenate([middle_query, middle_kv]),
        low_main,
        normed_one,
        0,
    )
    grad_tokens = from_tokens(
        (grad_mid + norm_rows_back(residual, gains[0], inverse_one, grad_normed)).astype(BF)
    )

    outer_down = 2.0 * fold_parts(
        t_mm(jnp.concatenate(two_parts(reduced_down), axis=1), down_low), RANK
    )
    of_keys = (jnp.arange(2 * kv_cols) < kv_cols)[None, :]
    outer_kv_grad = jnp.where(of_keys, outer_kv_grad[:RANK], outer_kv_grad[RANK:])
    def second_grads(product, sums, slope, norm, cross):
        return jnp.concatenate([product + 2.0 * (sums * slope) * cross, sums / norm])

    plain = {
        n: second_grads(
            product, sums, slopes[n], norms[n], in_order([cut(c, n) for c in cross_by])
        )
        for n, product, sums in (
            (KV, outer_kv_grad, scale_kv),
            (QUERY, outer_query, scale_query),
            (OUT, outer_out, scale_out),
            (DOWN, outer_down, scale_down),
        )
    }
    mlp_grads = second_grads(
        jnp.concatenate([b[3] for b in blocks], axis=1),
        jnp.concatenate([b[2] for b in blocks], axis=1),
        slope_by[0][MLP],
        norms_by[0][MLP],
        cut(cross_by[0], MLP),
    )
    main_width = 6 * RANK // tok_count
    down_width = RANK // tok_count
    outer_share = OUTS // (tok_count * wide_count)

    lanes = 768
    fit = lanes // share
    tall = main_width // fit
    packed = pack_all(
        place,
        [
            plain[QUERY], plain[KV], plain[OUT], mlp_grads, plain[DOWN], first_one, first_out,
            first_pairs, first_down,
        ],
        tok_count,
        part,
        (tall, down_width, lanes, share, hidden_share, outer_share),
    )
    packed = packed.reshape((tok_count, wide_count) + packed.shape[1:])
    packed = scatter_sum(scatter_sum(packed, "tok", BF), "wide", BF)
    main_part = jnp.swapaxes(packed[:tall].reshape(tall, fit, share), 0, 1)
    main_part = main_part.reshape(main_width, share).T
    down_part = packed[tall : tall + down_width, :hidden_share].T
    outer_sum = packed[tall + down_width : tall + down_width + RANK + 1, :outer_share]
    outer_part = outer_sum[:RANK]
    block_start = (tok * wide_count + wide) * outer_share
    mag_part = outer_sum[RANK]

    local_squares = (
        squared_sum(main_part)
        + squared_sum(down_part)
        + squared_sum(outer_part)
        + squared_sum(mag_part)
    )
    grad_total = all_sum(jnp.full((8, 128), local_squares), ["tok", "wide"])[0, 0]
    grad_norm = jnp.sqrt(grad_total)
    clip_factor = CLIP_MAX / jnp.maximum(grad_norm, CLIP_MAX)
    main_param = lax.dynamic_slice_in_dim(adapt_main, tok * main_width, main_width, 1)
    down_param = lax.dynamic_slice_in_dim(adapt_down, tok * down_width, down_width, 1)
    outer_param = lax.dynamic_slice_in_dim(adapt_outer, block_start, outer_share, 1)
    mag_param = lax.dynamic_slice_in_dim(magnitudes, block_start, outer_share, 0)
    main_new, main_first_new, main_second_new = adam(
        main_param, main_part, main_first, main_second, RATE_ADAPT, clip_factor
    )
    down_new, down_first_new, down_second_new = adam(
        down_param, down_part, down_first, down_second, RATE_ADAPT, clip_factor
    )
    outer_new, outer_first_new, outer_second_new = adam(
        outer_param, outer_part, outer_first, outer_second, RATE_OUTER, clip_factor
    )
    mag_new, mag_first_new, mag_second_new = adam(
        mag_param, mag_part, mag_first, mag_second, RATE_MAGNITUDE, clip_factor
    )
    mag_clipped = mag_part * clip_factor
    return (
        layer_out,
        grad_tokens,
        grad_norm,
        main_new,
        main_first_new,
        main_second_new,
        down_new,
        down_first_new,
        down_second_new,
        outer_new,
        outer_first_new,
        outer_second_new,
        mag_new,
        mag_clipped,
        mag_second_new,
    )


def solution(mesh):
    return jax.shard_map(
        shards,
        mesh=mesh,
        in_specs=(
            P("tok", "wide"),
            P("tok", "wide"),
            P("wide"),
            P("wide"),
            P("wide", None),
            P("wide", None),
            P("wide", None),
            P("wide", None),
            P("wide", None),
            P("wide", None),
            P("wide", None),
            P("wide", None),
            P("wide", None),
            P(),
            P(),
            P("wide", "tok"),
            P("wide", "tok"),
            P("wide", "tok"),
            P("wide", "tok"),
            P(None, ("tok", "wide")),
            P(None, ("tok", "wide")),
            P(("tok", "wide")),
            P(("tok", "wide")),
            P("tok", None),
        ),
        out_specs=(
            P("tok", "wide"),
            P("tok", "wide"),
            P(),
            P("wide", "tok"),
            P("wide", "tok"),
            P("wide", "tok"),
            P("wide", "tok"),
            P("wide", "tok"),
            P("wide", "tok"),
            P(None, ("tok", "wide")),
            P(None, ("tok", "wide")),
            P(None, ("tok", "wide")),
            P(("tok", "wide")),
            P(("tok", "wide")),
            P(("tok", "wide")),
        ),
        check_vma=False,
    )
```

```python
import functools

import jax
import jax.numpy as jnp
from jax import lax
from jax.experimental import pallas as pl
from jax.experimental.pallas import tpu as pltpu
from jax.sharding import PartitionSpec as P

D = 2048
HEADS = 32
HD = 64
KVH = 4
FF = 5632
STEP = 10
RANK = 16
CHUNKS = 8
EXTRA = 128
COST = 1 << 10

EPS_NORM = 1e-05
ROPE_BASE = 10000.0
CLIP_MAX = 1.0
BETA_FIRST = 0.9
BETA_SECOND = 0.999
ADAM_EPS = 1e-08
WEIGHT_DECAY = 0.01
RATE_ADAPT = 0.02
RATE_OUTER = 0.05
RATE_MAGNITUDE = 0.4
PRECISE = lax.Precision.HIGHEST
MASKED = -1e30
NT = (((1,), (1,)), ((), ()))
GROUP = HEADS // KVH
FWD = 4
BWD = 4
BF = jnp.bfloat16
F32 = jnp.float32
WIDTHS = [D, KVH * HD, KVH * HD, D, FF, FF, D]
STARTS = [sum(WIDTHS[:number]) for number in range(7)]
OUTS = sum(WIDTHS)


def bits_of(count):
    return [1 << place for place in range(count.bit_length() - 1)]


def swap(array, axis, distance):
    count = lax.axis_size(axis)
    return lax.ppermute(array, axis, [(i, i ^ distance) for i in range(count)])


def mm(left, right):
    return jnp.dot(left, right, preferred_element_type=F32)


def mm_t(left, right):
    return lax.dot_general(left, right, (((1,), (1,)), ((), ())), preferred_element_type=F32)


def t_mm(left, right):
    return lax.dot_general(left, right, (((0,), (0,)), ((), ())), preferred_element_type=F32)


def two_parts(values):
    high = lax.reduce_precision(values, 8, 7)
    return high.astype(BF), (values - high).astype(BF)


def fold_parts(stacked, count):
    return stacked[:count] + stacked[count : 2 * count]


def adam(param, grad, first, second, rate, clip_factor):
    clipped = grad * clip_factor
    first_new = BETA_FIRST * first + (1.0 - BETA_FIRST) * clipped
    second_new = BETA_SECOND * second + (1.0 - BETA_SECOND) * clipped * clipped
    first_hat = first_new / (1.0 - BETA_FIRST**STEP)
    second_hat = second_new / (1.0 - BETA_SECOND**STEP)
    param_new = param - rate * (
        first_hat / (jnp.sqrt(second_hat) + ADAM_EPS) + WEIGHT_DECAY * param
    )
    return (param_new, first_new, second_new)


def squared_sum(values):
    return jnp.sum(values * values)


def all_sum(values, axes):
    for axis in axes:
        for bit in bits_of(lax.axis_size(axis)):
            values = values + swap(values, axis, bit)
    return values


def all_blocks(block, axis):
    stacked = block[None]
    index = lax.axis_index(axis)
    for bit in bits_of(lax.axis_size(axis)):
        upper = (index // bit) % 2 == 1
        received = swap(stacked, axis, bit)
        stacked = jnp.concatenate(
            [jnp.where(upper, received, stacked), jnp.where(upper, stacked, received)]
        )
    return stacked


def scatter_sum(blocks, axis, wire=F32, order=None):
    index = lax.axis_index(axis)
    bits = bits_of(lax.axis_size(axis))
    shape = blocks.shape[1:]
    left = list(reversed(bits))
    blocks = blocks.reshape((2,) * len(bits) + shape)
    for bit in order or bits:
        dim = left.index(bit)
        side = (index // bit) % 2
        keep = lax.dynamic_index_in_dim(blocks, side, dim, keepdims=False)
        send = lax.dynamic_index_in_dim(blocks, 1 - side, dim, keepdims=False)
        blocks = keep + swap(send.astype(wire), axis, bit).astype(blocks.dtype)
        left.remove(bit)
    return blocks


def after(value, *others):
    return lax.optimization_barrier((value,) + others)[0]


def gather_slots(shard, turned=False, gate=None):
    slots = {0: shard}
    count = lax.axis_size("wide")
    for slot in sorted(range(1, count), key=lambda i: bin(i).count("1")):
        low = slot & -slot
        if turned and slot == count - 1:
            low = count // 4
        held = slots[slot ^ low]
        if gate is not None and slot != low:
            held = after(held, gate)
        slots[slot] = swap(held, "wide", low)
    return slots


def near(slots):
    return [held for slot, held in slots.items() if bin(slot).count("1") == 1]


def far(slots, steps):
    return [held for slot, held in slots.items() if bin(slot).count("1") == steps]


def put_rows(slots, extra):
    count = lax.axis_size("wide")
    index = lax.axis_index("wide")
    rows, cols = slots[0].shape
    whole = jnp.zeros((count * rows + extra.shape[0], cols), extra.dtype)
    whole = lax.dynamic_update_slice(whole, extra, (count * rows, 0))
    for slot, held in slots.items():
        whole = lax.dynamic_update_slice(whole, held, ((index ^ slot) * rows, 0))
    return whole


def rotate_half(values):
    half = HD // 2
    return jnp.concatenate([values[..., half:], values[..., :half]], axis=-1)


def turn(values, cosine, sine):
    shaped = values.reshape(values.shape[0], -1, HD)
    turned = shaped * cosine[:, None, :] + rotate_half(shaped) * sine[:, None, :]
    return turned.reshape(values.shape)


def pad_rows(rows, count):
    return jnp.concatenate([rows, jnp.zeros((count - rows.shape[0], rows.shape[1]), rows.dtype)])


def lanes_of(reduced):
    high, low = two_parts(reduced)
    return jnp.pad(
        jnp.concatenate([high, low], axis=1), ((0, 0), (0, EXTRA - 2 * reduced.shape[1]))
    )


def twice_low(rows):
    doubled = 2.0 * rows.astype(BF)
    return pad_rows(jnp.concatenate([doubled, doubled]), EXTRA)


def gram_of(left, right):
    return lax.dot_general(left, right, (((1,), (1,)), ((), ())), precision=PRECISE)


def turn_lanes(values, cosine, sine):
    lane = lax.broadcasted_iota(jnp.int32, values.shape, 1) % HD
    swapped = jnp.where(
        lane < HD // 2,
        pltpu.roll(values, 2 * HD - HD // 2, 1),
        pltpu.roll(values, HD // 2, 1),
    )
    return values * cosine + swapped * sine


def head_rows(pairs, low_side):
    rows = []
    for pair in pairs:
        lane = lax.broadcasted_iota(jnp.int32, pair.shape, 1)
        moved = pltpu.roll(pair, HD, 1)
        if low_side:
            rows.append(jnp.where(lane < HD, pair, 0.0))
            rows.append(jnp.where(lane < HD, moved, 0.0))
        else:
            rows.append(jnp.where(lane >= HD, moved, 0.0))
            rows.append(jnp.where(lane >= HD, pair, 0.0))
    return jnp.concatenate(rows, axis=0).astype(BF)


def pairs_of(columns, block):
    turned = jnp.concatenate([columns, columns], axis=0).T
    lane = lax.broadcasted_iota(jnp.int32, (block, 2 * HD), 1)
    out = []
    for pair in range(GROUP // 2):
        first = turned[2 * pair * block : (2 * pair + 1) * block]
        second = turned[(2 * pair + 1) * block : (2 * pair + 2) * block]
        out.append(jnp.where(lane < HD, first, second))
    return out


def forward_kernel(
    first_ref, z_ref, scale_ref, cos_ref, sin_ref, place_ref, start_ref, kv_ref, kvt_ref,
    query_ref, out_ref, log_ref, *, block, span, groups,
):
    rows = GROUP * block
    width = GROUP * HD

    def chunk_body(chunk, carry):
        at = pl.ds(pl.multiple_of(chunk * block, block), block)
        cosine = cos_ref[at, :]
        sine = sin_ref[at, :]
        query_rows = []
        for group in range(groups):
            pairs = []
            for pair in range(GROUP // 2):
                lanes = slice(group * width + pair * 2 * HD, group * width + (pair + 1) * 2 * HD)
                turned = turn_lanes(z_ref[at, lanes] * scale_ref[:, lanes], cosine, sine)
                low = turned.astype(BF)
                query_ref[at, lanes] = low
                pairs.append(low.astype(F32) * HD**-0.5)
            query_rows.append(head_rows(pairs, True))
        place = place_ref[chunk]
        start = start_ref[chunk]

        def key_body(step, state):
            key_block = chunk - step
            keys = pl.ds(pl.multiple_of(key_block * span, span), span)
            spot = key_block * span + lax.broadcasted_iota(jnp.int32, (span, rows), 0)
            allowed = (spot <= place) & (spot >= start)
            out = []
            all_scores = [
                lax.dot_general(
                    kv_ref[keys, group * 2 * HD : (group + 1) * 2 * HD], query_rows[group], NT, preferred_element_type=F32
                )
                for group in range(groups)
            ]
            for group in range(groups):
                peak, total, mixed = state[group]
                scores = jnp.where(allowed, all_scores[group], MASKED)
                peak_new = jnp.maximum(peak, jnp.max(scores, axis=0, keepdims=True))
                powers = jnp.exp(scores - peak_new)
                shrink = jnp.exp(peak - peak_new)
                total = total * shrink + jnp.sum(powers, axis=0, keepdims=True)
                mixed = mixed * shrink + jnp.dot(
                    kvt_ref[group, HD:, keys], powers.astype(BF), preferred_element_type=F32
                )
                out.append((peak_new, total, mixed))
            return tuple(out)

        start_state = tuple(
            (
                jnp.full((1, rows), MASKED, F32),
                jnp.zeros((1, rows), F32),
                jnp.zeros((HD, rows), F32),
            )
            for _ in range(groups)
        )
        state = lax.fori_loop(0, chunk + 1 - first_ref[chunk], key_body, start_state)
        for group in range(groups):
            peak, total, mixed = state[group]
            log_ref[group, chunk] = peak + jnp.log(total)
            for pair, value in enumerate(pairs_of(mixed / total, block)):
                low_lane = group * width + pair * 2 * HD
                out_ref[at, low_lane : low_lane + 2 * HD] = value.astype(BF)
        return carry

    lax.fori_loop(0, CHUNKS, chunk_body, 0)


def backward_kernel(
    first_ref, query_ref, cos_ref, sin_ref, place_ref, start_ref, kv_ref, kvt_ref, log_ref,
    out_ref, grad_ref, query_grad_ref, kv_grad_ref, sums, *, block, span, groups,
):
    rows = GROUP * block
    width = GROUP * HD
    sums[...] = jnp.zeros_like(sums)

    def chunk_body(chunk, carry):
        at = pl.ds(pl.multiple_of(chunk * block, block), block)
        tiles = []
        for group in range(groups):
            queries = []
            grads = []
            product_rows = []
            for pair in range(GROUP // 2):
                lanes = slice(group * width + pair * 2 * HD, group * width + (pair + 1) * 2 * HD)
                queries.append(query_ref[at, lanes].astype(F32) * HD**-0.5)
                grad = grad_ref[at, lanes].astype(F32)
                grads.append(grad)
                product = grad * out_ref[at, lanes].astype(F32)
                lane = lax.broadcasted_iota(jnp.int32, product.shape, 1)
                product_rows.append(jnp.where(lane < HD, product, 0.0))
                product_rows.append(jnp.where(lane >= HD, product, 0.0))
            inner = jnp.sum(jnp.concatenate(product_rows, axis=0).T, axis=0, keepdims=True)
            query_rows = head_rows(queries, True)
            grad_rows = head_rows(grads, False)
            tiles.append((query_rows, grad_rows, inner, log_ref[group, chunk]))
        place = place_ref[chunk]
        start = start_ref[chunk]

        def key_body(key_block, query_grads):
            keys = pl.ds(pl.multiple_of(key_block * span, span), span)
            spot = key_block * span + lax.broadcasted_iota(jnp.int32, (span, rows), 0)
            allowed = (spot <= place) & (spot >= start)
            out = []
            products = []
            for group in range(groups):
                query_rows, grad_rows, inner, log_total = tiles[group]
                kv = kv_ref[keys, group * 2 * HD : (group + 1) * 2 * HD]
                products.append(
                    (
                        lax.dot_general(kv, query_rows, NT, preferred_element_type=F32),
                        lax.dot_general(kv, grad_rows, NT, preferred_element_type=F32),
                    )
                )
            for group in range(groups):
                query_rows, grad_rows, inner, log_total = tiles[group]
                scores, grad_weights = products[group]
                weights = jnp.exp(jnp.where(allowed, scores - log_total, MASKED))
                grad_scores = (weights * (grad_weights - inner)).astype(BF)
                sums[group, keys, :] += jnp.dot(
                    grad_scores, query_rows, preferred_element_type=F32
                ) + jnp.dot(weights.astype(BF), grad_rows, preferred_element_type=F32)
                out.append(
                    query_grads[group]
                    + jnp.dot(kvt_ref[group, :HD, keys], grad_scores, preferred_element_type=F32)
                )
            return tuple(out)

        query_grads = lax.fori_loop(
            first_ref[chunk],
            chunk + 1,
            key_body,
            tuple(jnp.zeros((HD, rows), F32) for _ in range(groups)),
        )
        cosine = cos_ref[at, :]
        sine = sin_ref[at, :]
        for group in range(groups):
            for pair, value in enumerate(pairs_of(query_grads[group] * HD**-0.5, block)):
                low_lane = group * width + pair * 2 * HD
                query_grad_ref[at, low_lane : low_lane + 2 * HD] = turn_lanes(
                    value, cosine, -sine
                )
        return carry

    lax.fori_loop(0, CHUNKS, chunk_body, 0)
    for group in range(groups):
        kv_grad_ref[:, group * 2 * HD : (group + 1) * 2 * HD] = sums[group].astype(BF)


def attend(first_block, z, scale, cosine, sine, places, starts, kv, kvt):
    count = z.shape[0]
    block = count // CHUNKS
    length = kv.shape[0]
    span = length // CHUNKS
    rows = GROUP * block
    width = FWD * GROUP * HD
    grid_spec = pltpu.PrefetchScalarGridSpec(
        num_scalar_prefetch=1,
        grid=(KVH // FWD,),
        in_specs=[
            pl.BlockSpec((count, width), lambda g, s: (0, g)),
            pl.BlockSpec((1, width), lambda g, s: (0, g)),
            pl.BlockSpec((count, 2 * HD), lambda g, s: (0, 0)),
            pl.BlockSpec((count, 2 * HD), lambda g, s: (0, 0)),
            pl.BlockSpec((CHUNKS, 1, rows), lambda g, s: (0, 0, 0)),
            pl.BlockSpec((CHUNKS, 1, rows), lambda g, s: (0, 0, 0)),
            pl.BlockSpec((length, FWD * 2 * HD), lambda g, s: (0, g)),
            pl.BlockSpec((FWD, 2 * HD, length), lambda g, s: (g, 0, 0)),
        ],
        out_specs=[
            pl.BlockSpec((count, width), lambda g, s: (0, g)),
            pl.BlockSpec((count, width), lambda g, s: (0, g)),
            pl.BlockSpec((FWD, CHUNKS, 1, rows), lambda g, s: (g, 0, 0, 0)),
        ],
    )
    return pl.pallas_call(
        functools.partial(forward_kernel, block=block, span=span, groups=FWD),
        grid_spec=grid_spec,
        out_shape=[
            jax.ShapeDtypeStruct((count, HEADS * HD), BF),
            jax.ShapeDtypeStruct((count, HEADS * HD), BF),
            jax.ShapeDtypeStruct((KVH, CHUNKS, 1, rows), F32),
        ],
        compiler_params=pltpu.CompilerParams(vmem_limit_bytes=40 << 20),
        cost_estimate=pl.CostEstimate(flops=COST, bytes_accessed=COST, transcendentals=0),
    )(first_block, z, scale, cosine, sine, places, starts, kv, kvt)


def attend_back(
    first_block, queries, cosine, sine, places, starts, kv, kvt, log_total, attended, grads
):
    count = queries.shape[0]
    block = count // CHUNKS
    length = kv.shape[0]
    span = length // CHUNKS
    rows = GROUP * block
    width = BWD * GROUP * HD
    grid_spec = pltpu.PrefetchScalarGridSpec(
        num_scalar_prefetch=1,
        grid=(KVH // BWD,),
        in_specs=[
            pl.BlockSpec((count, width), lambda g, s: (0, g)),
            pl.BlockSpec((count, 2 * HD), lambda g, s: (0, 0)),
            pl.BlockSpec((count, 2 * HD), lambda g, s: (0, 0)),
            pl.BlockSpec((CHUNKS, 1, rows), lambda g, s: (0, 0, 0)),
            pl.BlockSpec((CHUNKS, 1, rows), lambda g, s: (0, 0, 0)),
            pl.BlockSpec((length, BWD * 2 * HD), lambda g, s: (0, g)),
            pl.BlockSpec((BWD, 2 * HD, length), lambda g, s: (g, 0, 0)),
            pl.BlockSpec((BWD, CHUNKS, 1, rows), lambda g, s: (g, 0, 0, 0)),
            pl.BlockSpec((count, width), lambda g, s: (0, g)),
            pl.BlockSpec((count, width), lambda g, s: (0, g)),
        ],
        out_specs=[
            pl.BlockSpec((count, width), lambda g, s: (0, g)),
            pl.BlockSpec((length, BWD * 2 * HD), lambda g, s: (0, g)),
        ],
        scratch_shapes=[pltpu.VMEM((BWD, length, 2 * HD), F32)],
    )
    return pl.pallas_call(
        functools.partial(backward_kernel, block=block, span=span, groups=BWD),
        grid_spec=grid_spec,
        out_shape=[
            jax.ShapeDtypeStruct((count, HEADS * HD), F32),
            jax.ShapeDtypeStruct((length, KVH * 2 * HD), BF),
        ],
        compiler_params=pltpu.CompilerParams(vmem_limit_bytes=40 << 20),
        cost_estimate=pl.CostEstimate(flops=40 << 30, bytes_accessed=64 << 20, transcendentals=0),
    )(first_block, queries, cosine, sine, places, starts, kv, kvt, log_total, attended, grads)


def place_of(place_ref, slot, rows):
    return pl.multiple_of((place_ref[0] ^ slot) * rows, rows)


def half_place(place_ref, half, tiles, pair_tiles):
    return (place_ref[1] ^ half) * pair_tiles + tiles


def set_rows(outer, offset):
    rank, cols = outer.shape
    parts = [outer]
    if offset:
        parts = [jnp.zeros((offset, cols), outer.dtype)] + parts
    if EXTRA - rank - offset:
        parts = parts + [jnp.zeros((EXTRA - rank - offset, cols), outer.dtype)]
    return jnp.concatenate(parts, axis=0)


def split_parts(values):
    high = values.astype(BF)
    return high, (values - high.astype(F32)).astype(BF)


def low_rank(reduced, outer, offset):
    high, low = split_parts(reduced)
    rows = set_rows(2.0 * outer.astype(BF).astype(F32), offset).astype(BF)
    return jnp.dot(high, rows, preferred_element_type=F32) + jnp.dot(
        low, rows, preferred_element_type=F32
    )


def slot_kernel(place_ref, inputs_ref, first_ref, outer_ref, *refs, offset):
    slots, out_ref, reduced_ref = refs[:-2], refs[-2], refs[-1]
    each = len(slots) // 2
    rows = slots[0].shape[0]

    @pl.when((pl.program_id(0) == 0) & (pl.program_id(1) == 0))
    def _():
        reduced_ref[...] = jnp.dot(inputs_ref[...], first_ref[...], preferred_element_type=F32)

    def total(chosen):
        result = low_rank(reduced_ref[...], outer_ref[...], offset)
        for slot, ref in enumerate(chosen):
            result = result + jnp.dot(
                inputs_ref[:, pl.ds(place_of(place_ref, slot, rows), rows)],
                ref[...],
                preferred_element_type=F32,
            )
        out_ref[...] = result

    for half in range(2):

        @pl.when(pl.program_id(0) == half)
        def _():
            total(slots[half * each : (half + 1) * each])


def slot_mm(place, inputs, first, outer, offset, slots, skip=0, tile=256):
    rows = slots[0][0].shape[0]
    cols = outer.shape[1]
    tiles = cols // 2 // tile

    def held(half):
        def spot(h, n, s):
            return (0, skip // tile + jnp.where(h == half, n, (tiles - 1) * (1 - half)))

        return pl.BlockSpec((rows, tile), spot)

    return pl.pallas_call(
        functools.partial(slot_kernel, offset=offset),
        grid_spec=pltpu.PrefetchScalarGridSpec(
            num_scalar_prefetch=1,
            grid=(2, tiles),
            in_specs=[
                pl.BlockSpec(inputs.shape, lambda h, n, s: (0, 0)),
                pl.BlockSpec(first.shape, lambda h, n, s: (0, 0)),
                pl.BlockSpec(
                    (outer.shape[0], tile), lambda h, n, s: (0, half_place(s, h, n, tiles))
                ),
            ]
            + [held(half) for half in range(2) for _ in slots[half]],
            out_specs=[
                pl.BlockSpec(
                    (inputs.shape[0], tile), lambda h, n, s: (0, half_place(s, h, n, tiles))
                ),
                pl.BlockSpec((inputs.shape[0], EXTRA), lambda h, n, s: (0, 0)),
            ],
        ),
        out_shape=[
            jax.ShapeDtypeStruct((inputs.shape[0], cols), F32),
            jax.ShapeDtypeStruct((inputs.shape[0], EXTRA), F32),
        ],
        compiler_params=pltpu.CompilerParams(vmem_limit_bytes=40 << 20),
        cost_estimate=pl.CostEstimate(flops=COST, bytes_accessed=COST, transcendentals=0),
    )(place, inputs, first, outer, *slots[0], *slots[1])


def finish_kernel(*refs, count, sizes, offset, summed):
    raws = refs[: len(sizes)]
    narrow_ref, middle_ref, first_ref, inputs_ref, grad_ref, out_ref = refs[len(sizes) :]
    first = first_ref[...]
    narrow_high, narrow_low = split_parts(narrow_ref[...])
    total = lax.dot_general(narrow_high, first, NT, preferred_element_type=F32)
    total = total + lax.dot_general(narrow_low, first, NT, preferred_element_type=F32)
    weighted = []
    for ref, size in zip(raws, sizes):
        total = total + ref[:count, :]
        weighted.append(ref[count : count + size, :] + ref[count + size :, :])
    grad_ref[...] = total
    weighted = sum(weighted) if summed else jnp.concatenate(weighted, axis=0)
    middle_high, middle_low = split_parts(middle_ref[...])
    middle = lax.dot_general(middle_high, first, NT, preferred_element_type=F32)
    middle = middle + lax.dot_general(middle_low, first, NT, preferred_element_type=F32)
    under = (((0,), (0,)), ((), ()))
    inputs = inputs_ref[...]
    product = lax.dot_general(narrow_high, inputs, under, preferred_element_type=F32)
    product = product + lax.dot_general(narrow_low, inputs, under, preferred_element_type=F32)
    out_ref[...] = (
        product[offset : offset + weighted.shape[0]] + 2.0 * (weighted + 2.0 * middle)
    )


def finish_back(raws, sizes, narrow, middle, first, inputs, offset, summed=False, tile=512):
    count = inputs.shape[0]
    rank = middle.shape[0]
    tiled = lambda rows: pl.BlockSpec((rows, tile), lambda n: (0, n))
    return pl.pallas_call(
        functools.partial(
            finish_kernel, count=count, sizes=sizes, offset=offset, summed=summed
        ),
        grid=(D // tile,),
        in_specs=[tiled(raw.shape[0]) for raw in raws]
        + [
            pl.BlockSpec(narrow.shape, lambda n: (0, 0)),
            pl.BlockSpec(middle.shape, lambda n: (0, 0)),
            pl.BlockSpec((tile, EXTRA), lambda n: (n, 0)),
            tiled(count),
        ],
        out_specs=[tiled(count), tiled(rank)],
        out_shape=[
            jax.ShapeDtypeStruct((count, D), F32),
            jax.ShapeDtypeStruct((rank, D), F32),
        ],
        compiler_params=pltpu.CompilerParams(vmem_limit_bytes=40 << 20),
        cost_estimate=pl.CostEstimate(flops=COST, bytes_accessed=COST, transcendentals=0),
    )(*raws, narrow, middle, first, inputs)


def slot_back_kernel(place_ref, grad_ref, *refs, skip):
    slots, out_ref, held, arrived = refs[:-3], refs[-3], refs[-2], refs[-1]
    each = len(slots) // 2
    rows, cols = held.shape[1:]
    copies = [
        pltpu.make_async_copy(ref.at[:, pl.ds(skip, cols)], held.at[slot], arrived.at[slot])
        for slot, ref in enumerate(slots)
    ]
    for slot in range(each):
        copies[slot].start()
        copies[each + slot].start()
    grads = [
        grad_ref[:, pl.ds(pl.multiple_of((place_ref[1] ^ half) * cols, cols), cols)]
        for half in range(2)
    ]
    for slot in range(each):
        copies[slot].wait()
        copies[each + slot].wait()
        out_ref[:, pl.ds(place_of(place_ref, slot, rows), rows)] = lax.dot_general(
            grads[0], held[slot], NT, preferred_element_type=F32
        ) + lax.dot_general(grads[1], held[each + slot], NT, preferred_element_type=F32)


def slot_back(place, grads, slots, skip=0):
    rows = slots[0][0].shape[0]
    count, cols = grads.shape
    many = 2 * len(slots[0])
    return pl.pallas_call(
        functools.partial(slot_back_kernel, skip=skip),
        grid_spec=pltpu.PrefetchScalarGridSpec(
            num_scalar_prefetch=1,
            grid=(1,),
            in_specs=[pl.BlockSpec((count, cols), lambda n, s: (0, 0))]
            + [pl.BlockSpec(memory_space=pl.ANY) for _ in range(many)],
            out_specs=pl.BlockSpec((count, D), lambda n, s: (0, 0)),
            scratch_shapes=[
                pltpu.VMEM((many, rows, cols // 2), BF),
                pltpu.SemaphoreType.DMA((many,)),
            ],
        ),
        out_shape=jax.ShapeDtypeStruct((count, D), F32),
        compiler_params=pltpu.CompilerParams(vmem_limit_bytes=40 << 20),
        cost_estimate=pl.CostEstimate(flops=COST, bytes_accessed=COST, transcendentals=0),
    )(place, grads, *slots[0], *slots[1])


def pad_to(rows, count):
    return jnp.concatenate([rows, jnp.zeros((count - rows.shape[0], rows.shape[1]), rows.dtype)])


def split_rows(weighted):
    high = weighted.astype(BF)
    return high, (weighted - high.astype(F32)).astype(BF)


def terms_of(grads_low, weighted, outer, reduced, offset):
    rank = outer.shape[0]
    rows = set_rows(outer, offset)
    narrow = 2.0 * lax.dot_general(grads_low, rows.astype(BF), NT, preferred_element_type=F32)
    middle = lax.dot_general(weighted, rows, NT, precision=PRECISE, preferred_element_type=F32)
    own = lax.broadcasted_iota(jnp.int32, middle.shape, 0) // RANK + offset // RANK
    middle = jnp.where(
        lax.broadcasted_iota(jnp.int32, middle.shape, 1) // RANK == own, middle, 0.0
    )
    under = (((0,), (0,)), ((), ()))
    high, low = split_parts(reduced)
    both = lax.dot_general(high, grads_low, under, preferred_element_type=F32)
    both = both + lax.dot_general(low, grads_low, under, preferred_element_type=F32)
    return narrow, middle, 2.0 * both[offset : offset + rank]


def terms_kernel(
    grad_ref, z_ref, scale_ref, slope_ref, outer_ref, reduced_ref,
    rows_ref, sum_ref, product_ref, narrow_ref, middle_ref, *, offset,
):
    count = grad_ref.shape[0]
    rank = outer_ref.shape[0]
    grads = grad_ref[...]
    sums = jnp.sum(grads * z_ref[...], axis=0, keepdims=True)
    sum_ref[...] = sums
    low = (grads * scale_ref[...]).astype(BF)
    weighted = (sums * slope_ref[...]) * outer_ref[...]
    high_part, low_part = split_rows(weighted)
    rows_ref[:count, :] = low
    rows_ref[count : count + rank, :] = high_part
    rows_ref[count + rank :, :] = low_part
    narrow, middle, product = terms_of(
        low, weighted, outer_ref[...], reduced_ref[...], offset
    )
    product_ref[...] = product

    @pl.when(pl.program_id(0) == 0)
    def _():
        narrow_ref[...] = narrow
        middle_ref[...] = middle

    @pl.when(pl.program_id(0) > 0)
    def _():
        narrow_ref[...] += narrow
        middle_ref[...] += middle


def grad_terms(grads, z, scale, slope, outer, offset, reduced, tile=512):
    count, cols = grads.shape
    rank = outer.shape[0]
    tiled = lambda rows: pl.BlockSpec((rows, tile), lambda n: (0, n))
    fixed = lambda rows, width: pl.BlockSpec((rows, width), lambda n: (0, 0))
    return pl.pallas_call(
        functools.partial(terms_kernel, offset=offset),
        grid=(cols // tile,),
        in_specs=[
            tiled(count), tiled(count), tiled(1), tiled(1), tiled(rank),
            fixed(count, reduced.shape[1]),
        ],
        out_specs=[
            tiled(count + 2 * rank), tiled(1), tiled(rank), fixed(count, EXTRA), fixed(rank, EXTRA),
        ],
        out_shape=[
            jax.ShapeDtypeStruct((count + 2 * rank, cols), BF),
            jax.ShapeDtypeStruct((1, cols), F32),
            jax.ShapeDtypeStruct((rank, cols), F32),
            jax.ShapeDtypeStruct((count, EXTRA), F32),
            jax.ShapeDtypeStruct((rank, EXTRA), F32),
        ],
        compiler_params=pltpu.CompilerParams(vmem_limit_bytes=40 << 20),
        cost_estimate=pl.CostEstimate(flops=COST, bytes_accessed=COST, transcendentals=0),
    )(grads, z, scale, slope, outer, reduced)


def pack_kernel(inputs_ref, first_ref, out_ref, turned_ref, *, offset, rank):
    reduced = jnp.dot(inputs_ref[...], first_ref[...], preferred_element_type=F32)
    high, low = split_parts(reduced)
    pick = lambda part: part.astype(F32)[:, offset : offset + rank]
    count = inputs_ref.shape[0]
    packed = jnp.concatenate(
        [pick(high), pick(low), jnp.zeros((count, EXTRA - 2 * rank), F32)], axis=1
    )
    out_ref[...] = packed.astype(BF)
    turned_ref[...] = packed.T.astype(BF)


def pack_reduced(inputs, first, offset, rank):
    count = inputs.shape[0]
    return pl.pallas_call(
        functools.partial(pack_kernel, offset=offset, rank=rank),
        out_shape=[
            jax.ShapeDtypeStruct((count, EXTRA), BF),
            jax.ShapeDtypeStruct((EXTRA, count), BF),
        ],
        cost_estimate=pl.CostEstimate(flops=COST, bytes_accessed=COST, transcendentals=0),
    )(inputs, first)


def mlp_kernel(
    place_ref, inputs_ref, packed_ref, turned_ref, scale_ref, slope_ref, outer_ref,
    down_grad_ref, narrow_down_ref, first_ref, down_ref, *refs, offset,
):
    slots, kept = refs[:-8], refs[-8:]
    hidden_ref, rows_ref, sum_ref, product_ref, narrow_ref, middle_ref, z_ref, back_ref = kept
    rows = slots[0].shape[0]
    half = hidden_ref.shape[1]
    count = hidden_ref.shape[0]
    gate_lanes = lax.broadcasted_iota(jnp.int32, (RANK, 2 * half), 1) < half
    outer = jnp.concatenate(
        [
            jnp.where(gate_lanes, outer_ref[...], 0.0),
            jnp.where(gate_lanes, 0.0, outer_ref[...]),
        ],
        axis=0,
    )
    rank = outer.shape[0]
    doubled = 2.0 * outer.astype(BF).astype(F32)
    pad = jnp.zeros((EXTRA - 2 * rank, 2 * half), F32)
    z = jnp.dot(
        packed_ref[...],
        jnp.concatenate([doubled, doubled, pad], axis=0).astype(BF),
        preferred_element_type=F32,
    )
    for slot, ref in enumerate(slots):
        z = z + jnp.dot(
            inputs_ref[:, pl.ds(place_of(place_ref, slot, rows), rows)],
            ref[...],
            preferred_element_type=F32,
        )
    z_ref[...] = z
    back_ref[...] = lax.dot_general(
        down_grad_ref[...], down_ref[...], NT, preferred_element_type=F32
    ) + lax.dot_general(narrow_down_ref[...], first_ref[...], NT, preferred_element_type=F32)
    scale = scale_ref[...]
    step = 64
    gate_sums = jnp.zeros((8, half), F32)
    up_sums = jnp.zeros((8, half), F32)

    def eighth(values):
        return jnp.sum(values.reshape(step // 8, 8, half), axis=0)

    for begin in range(0, count, step):
        at = slice(begin, begin + step)
        gate_z, up_z = z_ref[at, :half], z_ref[at, half:]
        grad_hidden = back_ref[at, :]
        gate = gate_z * scale[:, :half]
        up = up_z * scale[:, half:]
        sigmoid = 0.5 * jnp.tanh(0.5 * gate) + 0.5
        silu = gate * sigmoid
        hidden_ref[at, :] = (silu * up).astype(BF)
        grad_up = grad_hidden * silu
        grad_gate = grad_hidden * up * (sigmoid + silu * (1.0 - sigmoid))
        gate_sums = gate_sums + eighth(grad_gate * gate_z)
        up_sums = up_sums + eighth(grad_up * up_z)
        rows_ref[at, :half] = (grad_gate * scale[:, :half]).astype(BF)
        rows_ref[at, half:] = (grad_up * scale[:, half:]).astype(BF)
    sums = jnp.concatenate(
        [
            jnp.sum(gate_sums, axis=0, keepdims=True),
            jnp.sum(up_sums, axis=0, keepdims=True),
        ],
        axis=1,
    )
    sum_ref[...] = sums
    low = rows_ref[:count, :]
    weighted = (sums * slope_ref[...]) * outer
    high_part, low_part = split_rows(weighted)
    rows_ref[count : count + rank, :] = high_part
    rows_ref[count + rank :, :] = low_part
    placed = set_rows(outer, offset)
    narrow = 2.0 * lax.dot_general(low, placed.astype(BF), NT, preferred_element_type=F32)
    middle = lax.dot_general(weighted, placed, NT, precision=PRECISE, preferred_element_type=F32)
    both = jnp.dot(turned_ref[...], low, preferred_element_type=F32)
    product = 2.0 * (both[:rank] + both[rank : 2 * rank])
    product_ref[:, :half] = product[: rank // 2, :half]
    product_ref[:, half:] = product[rank // 2 :, half:]

    @pl.when(pl.program_id(0) == 0)
    def _():
        narrow_ref[...] = narrow
        middle_ref[...] = middle

    @pl.when(pl.program_id(0) > 0)
    def _():
        narrow_ref[...] += narrow
        middle_ref[...] += middle


def mlp_block(
    place, inputs, packs, offset, scale, slope, outer, down_grad, narrow_down, down, slots, start
):
    rows, cols = slots[0].shape
    count = inputs.shape[0]
    rank = 2 * RANK
    tile = 256
    skip = start // tile
    fixed = lambda array: pl.BlockSpec(array.shape, lambda n, s: (0, 0))
    tiled = lambda rows: pl.BlockSpec((rows, tile), lambda n, s: (0, n))
    late = lambda rows: pl.BlockSpec((rows, tile), lambda n, s: (0, n + skip))
    kept = lambda rows: pl.BlockSpec((rows, EXTRA), lambda n, s: (0, 0))
    return pl.pallas_call(
        functools.partial(mlp_kernel, offset=offset),
        grid_spec=pltpu.PrefetchScalarGridSpec(
            num_scalar_prefetch=1,
            grid=(cols // tile,),
            in_specs=[
                fixed(inputs), fixed(packs[0]), fixed(packs[1]), late(1), late(1), late(RANK),
                fixed(down_grad), fixed(narrow_down),
                pl.BlockSpec((tile // 2, 128), lambda n, s: (n + skip, D // 128)),
                pl.BlockSpec((tile // 2, D), lambda n, s: (n + skip, 0)),
            ]
            + [tiled(rows) for _ in slots],
            out_specs=[
                pl.BlockSpec((count, tile // 2), lambda n, s: (0, n)),
                tiled(count + 2 * rank),
                tiled(1),
                tiled(RANK),
                kept(count),
                kept(rank),
            ],
            scratch_shapes=[
                pltpu.VMEM((count, tile), F32),
                pltpu.VMEM((count, tile // 2), F32),
            ],
        ),
        out_shape=[
            jax.ShapeDtypeStruct((count, cols // 2), BF),
            jax.ShapeDtypeStruct((count + 2 * rank, cols), BF),
            jax.ShapeDtypeStruct((1, cols), F32),
            jax.ShapeDtypeStruct((RANK, cols), F32),
            jax.ShapeDtypeStruct((count, EXTRA), F32),
            jax.ShapeDtypeStruct((rank, EXTRA), F32),
        ],
        compiler_params=pltpu.CompilerParams(vmem_limit_bytes=48 << 20),
        cost_estimate=pl.CostEstimate(flops=COST, bytes_accessed=COST, transcendentals=0),
    )(place, inputs, *packs, scale, slope, outer, down_grad, narrow_down, down, down, *slots)


def down_kernel(*refs, bounds):
    hiddens, (weights_ref, first_ref, outer_ref) = refs[:-6], refs[-6:-3]
    keep_ref, send_ref, reduced_ref = refs[-3:]

    @pl.when(pl.program_id(0) == 0)
    def _():
        reduced_ref[...] = jnp.zeros_like(reduced_ref)
        for (start, stop), ref in zip(bounds, hiddens):
            reduced_ref[...] += jnp.dot(
                ref[...], first_ref[start:stop, :], preferred_element_type=F32
            )

    lane = lax.broadcasted_iota(jnp.int32, reduced_ref.shape, 1)
    total = low_rank(jnp.where(lane < RANK, reduced_ref[...], 0.0), outer_ref[...], 0)
    for (start, stop), ref in zip(bounds, hiddens):
        total = total + jnp.dot(
            ref[...], weights_ref[start:stop, :], preferred_element_type=F32
        )
    count = keep_ref.shape[0]
    keep_ref[...] = total[:count]
    send_ref[...] = total[count:].astype(BF)


def down_forward(hiddens, bounds, down, outer, tile=256):
    count = hiddens[0].shape[0]
    rows = down.shape[0]
    return pl.pallas_call(
        functools.partial(down_kernel, bounds=bounds),
        grid=(D // tile,),
        in_specs=[pl.BlockSpec(hidden.shape, lambda n: (0, 0)) for hidden in hiddens]
        + [
            pl.BlockSpec((rows, tile), lambda n: (0, n)),
            pl.BlockSpec((rows, EXTRA), lambda n: (0, D // EXTRA)),
            pl.BlockSpec((RANK, tile), lambda n: (0, n)),
        ],
        out_specs=[
            pl.BlockSpec((count // 2, tile), lambda n: (0, n)),
            pl.BlockSpec((count // 2, tile), lambda n: (0, n)),
            pl.BlockSpec((count, EXTRA), lambda n: (0, 0)),
        ],
        out_shape=[
            jax.ShapeDtypeStruct((count // 2, D), F32),
            jax.ShapeDtypeStruct((count // 2, D), BF),
            jax.ShapeDtypeStruct((count, EXTRA), F32),
        ],
        compiler_params=pltpu.CompilerParams(vmem_limit_bytes=40 << 20),
        cost_estimate=pl.CostEstimate(flops=COST, bytes_accessed=COST, transcendentals=0),
    )(*hiddens, down, down, outer)


def kv_form_kernel(z_ref, scale_ref, cos_ref, sin_ref, out_ref):
    lane = lax.broadcasted_iota(jnp.int32, cos_ref.shape, 1)
    half = z_ref.shape[1] // 2
    for pair in range(half // 128):
        at = slice(pair * 128, (pair + 1) * 128)
        to = slice(half + pair * 128, half + (pair + 1) * 128)
        keys = turn_lanes(z_ref[:, at] * scale_ref[:, at], cos_ref[...], sin_ref[...])
        values = z_ref[:, to] * scale_ref[:, to]
        first = jnp.where(lane < HD, keys, pltpu.roll(values, HD, 1))
        second = jnp.where(lane < HD, pltpu.roll(keys, HD, 1), values)
        out_ref[:, 2 * pair * 128 : (2 * pair + 1) * 128] = first.astype(BF)
        out_ref[:, (2 * pair + 1) * 128 : (2 * pair + 2) * 128] = second.astype(BF)


def kv_form(z, scale, cosine, sine):
    return pl.pallas_call(
        kv_form_kernel,
        out_shape=jax.ShapeDtypeStruct(z.shape, BF),
        cost_estimate=pl.CostEstimate(flops=COST, bytes_accessed=COST, transcendentals=0),
    )(z, scale, cosine, sine)


def kv_back_kernel(sum_ref, cos_ref, sin_ref, out_ref):
    lane = lax.broadcasted_iota(jnp.int32, cos_ref.shape, 1)
    half = sum_ref.shape[1] // 2
    for pair in range(half // 128):
        first = sum_ref[:, 2 * pair * 128 : (2 * pair + 1) * 128].astype(F32)
        second = sum_ref[:, (2 * pair + 1) * 128 : (2 * pair + 2) * 128].astype(F32)
        keys = jnp.where(lane < HD, first, pltpu.roll(second, HD, 1))
        values = jnp.where(lane < HD, pltpu.roll(first, HD, 1), second)
        out_ref[:, pair * 128 : (pair + 1) * 128] = turn_lanes(keys, cos_ref[...], -sin_ref[...])
        out_ref[:, half + pair * 128 : half + (pair + 1) * 128] = values


def kv_back(sums, cosine, sine):
    return pl.pallas_call(
        kv_back_kernel,
        out_shape=jax.ShapeDtypeStruct(sums.shape, F32),
        cost_estimate=pl.CostEstimate(flops=COST, bytes_accessed=COST, transcendentals=0),
    )(sums, cosine, sine)


def pack_all_kernel(
    query_ref, kv_ref, out_ref_, mlp_ref, down_ref, one_ref, first_out_ref, pairs_ref, down_first_ref,
    place_ref, packed_ref, wide_rows, hold, down_rows, *, toks, part, layout,
):
    tall, low, lanes, share, hidden_share, outer_share = layout
    many = wide_rows.shape[0]
    wides = packed_ref.shape[0] // toks
    for n, ref in ((0, query_ref), (1, kv_ref), (3, out_ref_), (6, down_ref)):
        wide_rows[: RANK + 1, STARTS[n] : STARTS[n] + ref.shape[1]] = ref[...]
    blocks = FF // (4 * part)
    down_rows[...] = jnp.zeros_like(down_rows)
    for side in range(2):
        start = STARTS[4 + side]
        wide_rows[:, start : start + FF] = jnp.zeros((many, FF), F32)
        for tile in range(blocks * part // 128):
            hold[: RANK + 1, tile * 128 : (tile + 1) * 128] = mlp_ref[
                :, (2 * tile + side) * 128 : (2 * tile + side + 1) * 128
            ]
        for quarter in range(4):

            @pl.when(place_ref[2] == quarter)
            def _():
                for at in range(blocks):
                    to = start + (at * 4 + quarter) * part
                    wide_rows[: RANK + 1, to : to + part] = hold[
                        : RANK + 1, at * part : (at + 1) * part
                    ]
    for quarter in range(4):

        @pl.when(place_ref[2] == quarter)
        def _():
            for at in range(blocks):
                to = (at * 4 + quarter) * part
                down_rows[:, to : to + part] = down_first_ref[:, at * part : (at + 1) * part]

    packed_ref[...] = jnp.zeros_like(packed_ref)
    sources = [(0, one_ref), (3 * RANK, first_out_ref), (4 * RANK, pairs_ref)]

    def main_piece(start, rows, cols):
        parts = []
        while rows:
            base, ref = [pair for pair in sources if pair[0] <= start][-1]
            here = min(rows, base + ref.shape[0] - start)
            parts.append(ref[start - base : start - base + here, cols])
            start, rows = start + here, rows - here
        return parts[0] if len(parts) == 1 else jnp.concatenate(parts, axis=0)

    fit = lanes // share
    for tok in range(toks):
        for wide in range(wides):
            at = tok * wides + wide
            cols = slice(wide * share, (wide + 1) * share)
            for piece in range(fit):
                packed_ref[at, :tall, piece * share : (piece + 1) * share] = main_piece(
                    (tok * fit + piece) * tall, tall, cols
                )
            packed_ref[at, tall : tall + low, :hidden_share] = down_rows[
                tok * low : (tok + 1) * low, wide * hidden_share : (wide + 1) * hidden_share
            ]
            packed_ref[at, tall + low : tall + low + RANK + 1, :outer_share] = wide_rows[
                : RANK + 1, at * outer_share : (at + 1) * outer_share
            ]


def pack_all(place, pieces, toks, part, layout):
    tall, low, lanes, share, hidden_share, outer_share = layout
    owners = OUTS // outer_share
    rows = -(-(tall + low + RANK + 1) // 8) * 8
    fixed = lambda array: pl.BlockSpec(array.shape, lambda *n: (0,) * array.ndim)
    shape = jax.ShapeDtypeStruct((owners, rows, lanes), F32)
    return pl.pallas_call(
        functools.partial(pack_all_kernel, toks=toks, part=part, layout=layout),
        grid=(1,),
        in_specs=[fixed(piece) for piece in pieces]
        + [pl.BlockSpec(memory_space=pltpu.SMEM)],
        out_specs=fixed(shape),
        out_shape=shape,
        scratch_shapes=[
            pltpu.VMEM((RANK + 8, OUTS), F32),
            pltpu.VMEM((RANK + 8, FF // 4), F32),
            pltpu.VMEM((RANK, FF), F32),
        ],
        compiler_params=pltpu.CompilerParams(vmem_limit_bytes=40 << 20),
        cost_estimate=pl.CostEstimate(flops=COST, bytes_accessed=COST, transcendentals=0),
    )(*pieces, place)


def mlp_back_kernel(
    place_ref, one_ref, two_ref, narrow_ref, middle_ref, first_ref, inputs_ref, *refs, offset, rank
):
    slots, (keep_ref, send_ref, out_ref, held_one, held_two, arrived) = refs[:-6], refs[-6:]
    each = len(slots) // 2
    rows = held_one.shape[1]
    count = inputs_ref.shape[0]
    copies = []
    for half, held in enumerate((held_one, held_two)):
        copies.append(
            [
                pltpu.make_async_copy(slots[half * each + i], held.at[i], arrived.at[half * each + i])
                for i in range(each)
            ]
        )
    for i in range(each):
        copies[0][i].start()
        copies[1][i].start()
    narrow_high, narrow_low = split_parts(narrow_ref[...])
    turned_high = narrow_high.astype(F32).T.astype(BF)
    turned_low = narrow_low.astype(F32).T.astype(BF)
    middle_high, middle_low = split_parts(middle_ref[...])
    for i in range(each):
        copies[0][i].wait()
        copies[1][i].wait()
        at = pl.ds(place_of(place_ref, i, rows), rows)
        first = first_ref[at, :]
        total = lax.dot_general(one_ref[...], held_one[i], NT, preferred_element_type=F32)
        total = total + lax.dot_general(two_ref[...], held_two[i], NT, preferred_element_type=F32)
        grad = (
            total[:count]
            + lax.dot_general(narrow_high, first, NT, preferred_element_type=F32)
            + lax.dot_general(narrow_low, first, NT, preferred_element_type=F32)
        )
        keep_ref[:, at] = grad[: count // 2]
        send_ref[:, at] = grad[count // 2 :].astype(BF)
        weighted = total[count : count + rank] + total[count + rank :]
        middle = lax.dot_general(middle_high, first, NT, preferred_element_type=F32)
        middle = middle + lax.dot_general(middle_low, first, NT, preferred_element_type=F32)
        inputs = inputs_ref[:, at]
        product = jnp.dot(turned_high, inputs, preferred_element_type=F32)
        product = product + jnp.dot(turned_low, inputs, preferred_element_type=F32)
        out_ref[:, at] = product[offset : offset + rank] + 2.0 * (weighted + 2.0 * middle)


def mlp_back(place, grads, narrow, middle, first, inputs, slots, offset):
    count = inputs.shape[0]
    rank = middle.shape[0]
    rows = slots[0][0].shape[0]
    many = len(slots[0])
    operands = [*grads, narrow, middle, first, inputs]
    fixed = lambda array: pl.BlockSpec(array.shape, lambda n, s: (0, 0))
    shapes = [
        jax.ShapeDtypeStruct((count // 2, D), F32),
        jax.ShapeDtypeStruct((count // 2, D), BF),
        jax.ShapeDtypeStruct((rank, D), F32),
    ]
    return pl.pallas_call(
        functools.partial(mlp_back_kernel, offset=offset, rank=rank),
        grid_spec=pltpu.PrefetchScalarGridSpec(
            num_scalar_prefetch=1,
            grid=(1,),
            in_specs=[fixed(array) for array in operands]
            + [pl.BlockSpec(memory_space=pl.ANY) for _ in range(2 * many)],
            out_specs=[fixed(shape) for shape in shapes],
            scratch_shapes=[
                pltpu.VMEM((many, rows, grads[0].shape[1]), BF),
                pltpu.VMEM((many, rows, grads[1].shape[1]), BF),
                pltpu.SemaphoreType.DMA((2 * many,)),
            ],
        ),
        out_shape=shapes,
        compiler_params=pltpu.CompilerParams(vmem_limit_bytes=60 << 20),
        cost_estimate=pl.CostEstimate(flops=COST, bytes_accessed=COST, transcendentals=0),
    )(place, *operands, *slots[0], *slots[1])


def column_sums(base, first_high, first_low, outer, offset):
    outer_high, outer_low = split_parts(set_rows(outer, offset))
    product = (
        jnp.dot(first_high, outer_high, preferred_element_type=F32)
        + jnp.dot(first_high, outer_low, preferred_element_type=F32)
        + jnp.dot(first_low, outer_high, preferred_element_type=F32)
    )
    merged = base.astype(F32) + 2.0 * product
    merged_high, merged_low = split_parts(merged)
    under = (((0,), (0,)), ((), ()))
    cross = (
        lax.dot_general(first_high, merged_high, under, preferred_element_type=F32)
        + lax.dot_general(first_high, merged_low, under, preferred_element_type=F32)
        + lax.dot_general(first_low, merged_high, under, preferred_element_type=F32)
    )
    return jnp.sum(merged * merged, axis=0, keepdims=True), cross[offset : offset + RANK]


def widened(first):
    return jnp.concatenate(
        [first, jnp.zeros((first.shape[0], EXTRA - first.shape[1]), first.dtype)], axis=1
    )


def early_kernel(
    place_ref, query_ref, key_ref, value_ref, main_ref, outer_ref, shard_out, square_ref, cross_ref,
):
    half = query_ref.shape[1] // 2
    kv_cols = key_ref.shape[1]
    high, low = split_parts(widened(main_ref[...]))
    shard_out[:, half + kv_cols :] = high
    for core in range(2):

        @pl.when(place_ref[1] == core)
        def _():
            shard_out[:, :half] = query_ref[:, core * half : (core + 1) * half]
            kv = (key_ref, value_ref)[core][...]
            shard_out[:, half : half + kv_cols] = kv
            start = 2 * half + core * kv_cols
            square, cross = column_sums(
                kv, high, low, outer_ref[:, start : start + kv_cols], (1 + core) * RANK
            )
            square_ref[:, :kv_cols] = square
            cross_ref[:, :kv_cols] = cross
            for tile in range(half // 256):
                at = core * half + tile * 256
                square, cross = column_sums(
                    query_ref[:, at : at + 256], high, low, outer_ref[:, at : at + 256], 0
                )
                to = kv_cols + tile * 256
                square_ref[:, to : to + 256] = square
                cross_ref[:, to : to + 256] = cross


def early_work(place, query, key, value, main, outer):
    rows, cols = query.shape
    kv_cols = key.shape[1]
    fixed = lambda array: pl.BlockSpec(array.shape, lambda n, s: (0, 0))
    shapes = [
        jax.ShapeDtypeStruct((rows, cols // 2 + kv_cols + EXTRA), BF),
        jax.ShapeDtypeStruct((1, kv_cols + cols // 2), F32),
        jax.ShapeDtypeStruct((RANK, kv_cols + cols // 2), F32),
    ]
    return pl.pallas_call(
        early_kernel,
        grid_spec=pltpu.PrefetchScalarGridSpec(
            num_scalar_prefetch=1,
            grid=(1,),
            in_specs=[fixed(query), fixed(key), fixed(value), fixed(main)]
            + [pl.BlockSpec((RANK, cols + 2 * kv_cols), lambda n, s: (0, 0))],
            out_specs=[fixed(shape) for shape in shapes],
        ),
        out_shape=shapes,
        compiler_params=pltpu.CompilerParams(vmem_limit_bytes=32 << 20),
        cost_estimate=pl.CostEstimate(flops=COST, bytes_accessed=COST, transcendentals=0),
    )(place, query, key, value, main, outer)


def later_kernel(
    place_ref, out_w_ref, gate_ref, up_ref, down_w_ref, main_ref, first_ref, outer_ref, mags_ref,
    out_out, mlp_out, down_out, square_ref, cross_ref, picked_ref, hold, *, part,
):
    half = out_out.shape[1]
    width = gate_ref.shape[1]
    blocks = width // (4 * part)
    cols = blocks * part
    starts = [STARTS[n] for n in range(7)]
    high, low = split_parts(widened(main_ref[...]))
    down_first = widened(first_ref[...])
    down_high, down_low = split_parts(down_first)
    rows = gate_ref.shape[0]
    lanes = mags_ref.shape[0]
    for quarter in range(4):

        @pl.when(place_ref[2] == quarter)
        def _():
            for side, ref in enumerate((gate_ref, up_ref)):
                for at in range(blocks):
                    start = (at * 4 + quarter) * part
                    hold[side, :rows, at * part : (at + 1) * part] = ref[
                        :, start : start + part
                    ].astype(F32)
                    begin = starts[4 + side] + start
                    hold[side, rows : rows + RANK, at * part : (at + 1) * part] = outer_ref[
                        :, begin : begin + part
                    ]
                    hold[side, rows + RANK :, at * part : (at + 1) * part] = mags_ref[
                        :, begin : begin + part
                    ]
    for tile in range(cols // 128):
        for side in range(2):
            to = slice((2 * tile + side) * 128, (2 * tile + side + 1) * 128)
            taken = hold[side, :, tile * 128 : (tile + 1) * 128]
            base = taken[:rows].astype(BF)
            mlp_out[:, to] = base
            outer = taken[rows : rows + RANK]
            picked_ref[:RANK, to] = outer
            picked_ref[RANK:, to] = taken[rows + RANK :]
            square, cross = column_sums(base, high, low, outer, (4 + side) * RANK)
            square_ref[:, half + to.start : half + to.stop] = square
            cross_ref[:, half + to.start : half + to.stop] = cross
    down_at = pl.ds(pl.multiple_of(place_ref[2] * part, 16 if part % 16 == 0 else 8), part)
    down_out[:, : 2 * half] = down_w_ref[down_at, :]
    factor = first_ref[down_at, :]
    factor = jnp.concatenate([factor, factor], axis=1)
    down_out[:, 2 * half :] = widened(factor).astype(BF)
    for core in range(2):

        @pl.when(place_ref[1] == core)
        def _():
            out_out[...] = out_w_ref[:, core * half : (core + 1) * half]
            for tile in range(half // 256):
                at = core * half + tile * 256
                square, cross = column_sums(
                    out_w_ref[:, at : at + 256],
                    high,
                    low,
                    outer_ref[:, starts[3] + at : starts[3] + at + 256],
                    3 * RANK,
                )
                to = slice(tile * 256, (tile + 1) * 256)
                square_ref[:, to] = square
                cross_ref[:, to] = cross
                square, cross = column_sums(
                    down_w_ref[:, at : at + 256],
                    down_high,
                    down_low,
                    outer_ref[:, starts[6] + at : starts[6] + at + 256],
                    0,
                )
                begin = half + 2 * cols + tile * 256
                square_ref[:, begin : begin + 256] = square
                cross_ref[:, begin : begin + 256] = cross


def later_work(place, out_w, gate, up, down_w, main, first, outer, mags, part):
    rows, cols = out_w.shape
    half = cols // 2
    mlp = 2 * (gate.shape[1] // 4)
    total = 2 * half + mlp
    fixed = lambda array: pl.BlockSpec(array.shape, lambda n, s: (0, 0))
    inputs = [out_w, gate, up, down_w, main, first, outer, mags]
    shapes = [
        jax.ShapeDtypeStruct((rows, half), BF),
        jax.ShapeDtypeStruct((rows, mlp), BF),
        jax.ShapeDtypeStruct((part, cols + EXTRA), BF),
        jax.ShapeDtypeStruct((1, total), F32),
        jax.ShapeDtypeStruct((RANK, total), F32),
        jax.ShapeDtypeStruct((RANK + 8, mlp), F32),
    ]
    return pl.pallas_call(
        functools.partial(later_kernel, part=part),
        grid_spec=pltpu.PrefetchScalarGridSpec(
            num_scalar_prefetch=1,
            grid=(1,),
            in_specs=[fixed(array) for array in inputs],
            out_specs=[fixed(shape) for shape in shapes],
            scratch_shapes=[pltpu.VMEM((2, rows + RANK + 8, mlp // 2), F32)],
        ),
        out_shape=shapes,
        compiler_params=pltpu.CompilerParams(vmem_limit_bytes=48 << 20),
        cost_estimate=pl.CostEstimate(flops=COST, bytes_accessed=COST, transcendentals=0),
    )(place, *inputs)


def shards(
    tokens,
    cotangent,
    gain_attn,
    gain_ffn,
    w_query,
    w_key,
    w_value,
    w_output,
    w_gate,
    w_up,
    w_down,
    adapt_main,
    adapt_down,
    adapt_outer,
    magnitudes,
    main_first,
    main_second,
    down_first,
    down_second,
    outer_first,
    outer_second,
    mag_first,
    mag_second,
    segments,
):
    wide_count = lax.axis_size("wide")
    tok_count = lax.axis_size("tok")
    wide = lax.axis_index("wide")
    tok = lax.axis_index("tok")
    core = tok % 2
    place = jnp.stack([wide, core, tok % 4]).astype(jnp.int32)
    quarter = (tok % 4).astype(jnp.int32)[None]
    length, share = tokens.shape
    hidden_share = w_down.shape[0]
    part = hidden_share // 4
    block = length // (wide_count * CHUNKS)
    count = CHUNKS * block
    block_cols = wide_count * part
    half = D // 2
    kv_cols = KVH * HD

    def partner(array):
        return swap(array, "tok", 2)

    def other_core(array):
        return swap(array, "tok", 1)

    across = wide_count // 4
    deep, side = wide // across, wide % across

    def to_tokens(features):
        many = features.shape[0]
        pieces = features.reshape(many, CHUNKS, 4, across, block, share)
        rows = jnp.zeros((4, many, CHUNKS, block, across * share), features.dtype)
        for slot in range(across):
            piece = lax.dynamic_index_in_dim(pieces, side ^ slot, 3, keepdims=False)
            piece = jnp.moveaxis(piece, 2, 0)
            if slot:
                piece = swap(piece, "wide", slot)
            rows = lax.dynamic_update_slice(rows, piece, (0, 0, 0, 0, (side ^ slot) * share))
        whole = jnp.zeros((many, count, D), features.dtype)
        for slot in range(4):
            piece = lax.dynamic_index_in_dim(rows, deep ^ slot, 0, keepdims=False)
            piece = piece.reshape(many, count, across * share)
            if slot:
                piece = swap(piece, "wide", slot * across)
            whole = lax.dynamic_update_slice(
                whole, piece, (0, 0, (deep ^ slot) * across * share)
            )
        return whole

    def from_tokens_deep(rows):
        cols = across * share
        held = jnp.zeros((CHUNKS, 4, block, cols), rows.dtype)
        for slot in range(4):
            piece = lax.dynamic_slice(rows, (0, (deep ^ slot) * cols), (count, cols))
            if slot:
                piece = swap(piece, "wide", slot * across)
            piece = piece.reshape(CHUNKS, 1, block, cols)
            held = lax.dynamic_update_slice(held, piece, (0, deep ^ slot, 0, 0))
        return held

    def from_tokens(rows):
        return from_tokens_side(from_tokens_deep(rows))

    def from_tokens_side(held):
        whole = jnp.zeros((CHUNKS, 4, across, block, share), held.dtype)
        for slot in range(across):
            piece = lax.dynamic_slice_in_dim(held, (side ^ slot) * share, share, 3)
            if slot:
                piece = swap(piece, "wide", slot)
            whole = lax.dynamic_update_slice(whole, piece[:, :, None], (0, 0, side ^ slot, 0, 0))
        return whole.reshape(length, share)

    def own_half(array, axis=-1):
        size = array.shape[axis] // 2
        return lax.dynamic_slice_in_dim(array, core * size, size, axis)

    def in_order(blocks):
        return jnp.where(
            core == 0, jnp.concatenate(blocks, axis=-1), jnp.concatenate(blocks[::-1], axis=-1)
        )

    def by_core(zero, one, flip=0):
        return jnp.where(core == flip, zero, one)

    def sides(array, n):
        return array[..., STARTS[n] : STARTS[n] + WIDTHS[n]]

    ends = [0, kv_cols, kv_cols + half, kv_cols + 2 * half, kv_cols + 2 * half + 2 * block_cols]
    ends.append(ends[-1] + half)

    def cut(array, n):
        return array[..., ends[n] : ends[n + 1]]

    KV, QUERY, OUT, MLP, DOWN = range(5)

    both_rows = to_tokens(jnp.stack([tokens, cotangent]))
    residual, upstream = both_rows[0].astype(F32), both_rows[1].astype(F32)
    gain_parts = jnp.stack([gain_attn, gain_ffn], axis=1)
    split = [lax.reduce_precision(gain_parts, 8, 7)]
    split.append(lax.reduce_precision(gain_parts - split[0], 8, 7))
    split.append(gain_parts - split[0] - split[1])
    qkv_shard, squares, soon_cross = early_work(
        place, w_query, w_key, w_value, jnp.concatenate([adapt_main, *split], axis=1), adapt_outer
    )
    qkv_slots = [gather_slots(qkv_shard)]
    mags = magnitudes[None]
    out_shard, mlp_shard, down_shard, rest_squares, rest_cross, picked = later_work(
        place, after(w_output, *near(qkv_slots[0])), w_gate, w_up, w_down, adapt_main, adapt_down,
        adapt_outer, jnp.broadcast_to(mags, (8, OUTS)), part,
    )
    squares = jnp.concatenate([squares, rest_squares], axis=1)
    crosses = jnp.concatenate([soon_cross, rest_cross], axis=1)
    for bit in bits_of(wide_count):
        sent = jnp.concatenate([crosses.astype(BF), *two_parts(squares)])
        sent = swap(sent, "wide", bit).astype(F32)
        crosses = crosses + sent[:RANK]
        squares = squares + (sent[RANK : RANK + 1] + sent[RANK + 1 :])
    norms_own = jnp.sqrt(squares)
    mags_own = jnp.concatenate(
        [
            by_core(sides(mags, 1), sides(mags, 2)),
            own_half(sides(mags, 0)),
            own_half(sides(mags, 3)),
            picked[RANK : RANK + 1],
            own_half(sides(mags, 6)),
        ],
        axis=1,
    )
    own_rows = jnp.concatenate([crosses, mags_own, norms_own])
    rows_by = [own_rows, other_core(own_rows)]
    cross_by = [rows[:RANK] for rows in rows_by]
    scale_by, slope_by, norms_by = [], [], []
    for rows in rows_by:
        mags_row, norm = rows[RANK : RANK + 1], rows[RANK + 1 :]
        scale, slope = mags_row / norm, -mags_row / (norm * norm * norm)
        for found, row in ((scale_by, scale), (slope_by, slope), (norms_by, norm)):
            found.append([cut(row, n) for n in range(5)])
    mlp_outer = [picked[:RANK]]

    def natural_of(parts, n):
        return in_order([p[n] for p in parts])

    scales, slopes, norms = (
        [natural_of(parts, n) if n != MLP else None for n in range(5)]
        for parts in (scale_by, slope_by, norms_by)
    )
    outers = [sides(adapt_outer, n) for n in range(7)]
    outer_kv = jnp.concatenate(
        [jnp.pad(outers[1], ((0, 0), (0, kv_cols))), jnp.pad(outers[2], ((0, 0), (kv_cols, 0)))]
    )

    qkv_slots.append({s: other_core(held) for s, held in qkv_slots[0].items()})
    low_main = put_rows(
        {s: held[:, half + kv_cols :] for s, held in qkv_slots[0].items()},
        jnp.zeros((0, EXTRA), BF),
    )
    gains = low_main[:, 6 * RANK : 6 * RANK + 6].astype(F32).T
    gains = (gains[4:6] + gains[2:4]) + gains[:2]

    def main_cols(n, many=1):
        return low_main[:, n * RANK : (n + many) * RANK]

    def norm_rows(values, gain_row):
        inverse = lax.rsqrt(jnp.mean(values * values, axis=1, keepdims=True) + EPS_NORM)
        return (values * inverse * gain_row[None, :]).astype(BF), inverse

    def norm_rows_back(values, gain_row, inverse, grad_normed):
        inner = jnp.sum(values * gain_row[None, :] * grad_normed, axis=1, keepdims=True)
        return (
            grad_normed * gain_row[None, :] * inverse
            - values * (inverse * inverse * inverse * inner / D)
        )

    def ordered(slots):
        return [slots[s] for s in range(wide_count)]

    own_places = (
        jnp.arange(CHUNKS, dtype=jnp.int32)[:, None] * (wide_count * block)
        + wide * block
        + jnp.arange(block, dtype=jnp.int32)[None, :]
    ).reshape(count)
    segment_row = after(segments, residual)[0]
    own_segment = lax.dynamic_index_in_dim(
        segment_row.reshape(CHUNKS, wide_count, block), wide, 1, keepdims=False
    ).reshape(count)
    own_starts = jnp.sum(
        (segment_row[None, :] < own_segment[:, None]).astype(jnp.int32), axis=1
    )
    frequency = ROPE_BASE ** (-2.0 * jnp.arange(HD // 2, dtype=F32) / HD)
    angles = (own_places - own_starts).astype(F32)[:, None] * frequency[None, :]
    cosine = jnp.tile(jnp.cos(angles), (1, 4))
    sine = jnp.tile(jnp.concatenate([-jnp.sin(angles), jnp.sin(angles)], axis=1), (1, 2))
    place_rows = jnp.tile(own_places.reshape(CHUNKS, 1, block), (1, 1, GROUP))
    start_rows = jnp.tile(own_starts.reshape(CHUNKS, 1, block), (1, 1, GROUP))
    first_block = own_starts.reshape(CHUNKS, block)[:, 0] // (wide_count * block)

    ready = residual
    normed_one, inverse_one = norm_rows(ready, gains[0])
    kv_z, reduced_one = slot_mm(
        place, normed_one, low_main, outer_kv, RANK, [ordered(qkv_slots[k]) for k in range(2)], half
    )
    kv = kv_form(kv_z, scales[KV], cosine, sine)
    token_slots = gather_slots(kv.reshape(CHUNKS, 1, block, KVH * 2 * HD))

    kv = jnp.zeros((CHUNKS, wide_count, block, KVH * 2 * HD), BF)
    for slot, held in token_slots.items():
        kv = lax.dynamic_update_slice(kv, held, (0, wide ^ slot, 0, 0))
    kv = kv.reshape(length, KVH * 2 * HD)
    kvt = kv.T.reshape(KVH, 2 * HD, length)
    query_z, _ = slot_mm(
        place, normed_one, low_main, outers[0], 0, [ordered(qkv_slots[k]) for k in range(2)]
    )
    queries, attended, log_total = attend(
        first_block, query_z, scales[QUERY], cosine, sine, place_rows, start_rows, kv, kvt
    )

    down_slots = gather_slots(after(down_shard, *near(token_slots)))
    out_slots = [gather_slots(after(out_shard, qkv_slots[0][wide_count - 1]), True)]
    out_slots.append({s: other_core(held) for s, held in out_slots[0].items()})
    down_weights = put_rows(down_slots, jnp.zeros((0, D + EXTRA), BF))
    tiles = 2 * block_cols // 256
    cuts = [0, (tiles + 1) // 2 * 256, 2 * block_cols]
    spans = [slice(cuts[i], cuts[i + 1]) for i in range(2)]
    mlp_slots = []
    before = near(down_slots)
    for i, span in enumerate(spans):
        mlp_slots.append(gather_slots(after(mlp_shard[:, span], *before), i == 0))
        before = near(mlp_slots[-1])

    output_z, reduced_out = slot_mm(
        place, attended, low_main, outers[3], 3 * RANK, [ordered(out_slots[k]) for k in range(2)]
    )
    hidden_one = residual + output_z * scales[OUT]

    normed_own, inverse_two = norm_rows(hidden_one, gains[1])
    def of_four(rows):
        pair = jnp.concatenate([rows, partner(rows)])
        return jnp.concatenate([pair, other_core(pair)])

    normed_two = of_four(normed_own)
    down_low = (upstream * scales[DOWN]).astype(BF)
    down_low = of_four(down_low)
    narrow_down = 2.0 * mm_t(down_low, outers[6].astype(BF))
    narrow_down_lanes = lanes_of(narrow_down)
    packs = pack_reduced(normed_two, low_main, 4 * RANK, 2 * RANK)
    blocks = [
        mlp_block(
            place,
            normed_two,
            packs,
            4 * RANK,
            scale_by[0][MLP],
            slope_by[0][MLP],
            mlp_outer[0],
            down_low,
            narrow_down_lanes,
            down_weights,
            ordered(mlp_slots[i]),
            span.start,
        )
        for i, span in enumerate(spans)
    ]

    pairs = 2 * RANK
    keep, sent, first_pairs = mlp_back(
        place,
        [b[1] for b in blocks],
        sum(b[4] for b in blocks),
        sum(b[5] for b in blocks),
        low_main,
        normed_two,
        [ordered(slots) for slots in mlp_slots],
        4 * RANK,
    )
    pair = keep + other_core(sent).astype(F32)
    swapped = partner(pair[count:].astype(BF))
    grad_normed = pair[:count] + swapped.astype(F32)
    bounds = [(span.start // 2, span.stop // 2) for span in spans]
    down_keep, down_sent, reduced_down = down_forward([b[0] for b in blocks], bounds, down_weights, after(outers[6], pair))
    reduced_down = reduced_down[:, :RANK]
    grad_mid = upstream + norm_rows_back(hidden_one, gains[1], inverse_two, grad_normed)
    down_pair = down_keep + other_core(after(down_sent, swapped)).astype(F32)

    def first_grads(rows, inputs, narrow, middle, factors, many):
        size = many * RANK
        parts = jnp.concatenate(two_parts(narrow), axis=1)
        product = fold_parts(t_mm(parts, inputs), size)
        same = jnp.arange(size)[:, None] // RANK == jnp.arange(size)[None, :] // RANK
        middle = jnp.where(same, middle[:, :size], 0.0)
        term = fold_parts(mm_t(jnp.concatenate(two_parts(middle)), factors), size)
        return product + 2.0 * (fold_parts(rows, size) + 2.0 * term)

    def twice(cols):
        return jnp.concatenate([cols, cols], axis=1)

    out_rows, scale_out, outer_out, narrow_out, middle_out = grad_terms(
        grad_mid, output_z, scales[OUT], slopes[OUT], outers[3], 3 * RANK, reduced_out
    )
    back_out = slot_back(place, out_rows, [ordered(out_slots[k]) for k in range(2)])
    grad_mixed, first_out = finish_back(
        [back_out], [RANK], narrow_out, middle_out, low_main, attended, 3 * RANK
    )
    grad_mixed = after(grad_mixed.astype(BF), down_pair)
    down_far = partner(down_pair[count:].astype(BF))
    down_z = down_pair[:count] + down_far.astype(F32)
    layer_rows = (hidden_one + down_z * scales[DOWN]).astype(BF)

    query_grad, kv_grad = attend_back(
        first_block, queries, cosine, sine, place_rows, start_rows, kv, kvt, log_total, attended,
        grad_mixed,
    )
    kv_grad = kv_grad.reshape(CHUNKS, wide_count, block, KVH * 2 * HD)
    kv_grad = jnp.swapaxes(after(kv_grad, down_far), 0, 1).astype(F32)
    bits = bits_of(wide_count)
    kv_half = KVH * HD
    kv_grad = jnp.concatenate(
        [
            scatter_sum(kv_grad[..., :kv_half], "wide", BF),
            scatter_sum(kv_grad[..., kv_half:], "wide", BF, [bits[-2], *bits[:-2], bits[-1]]),
        ],
        axis=-1,
    )
    layer_deep = from_tokens_deep(after(layer_rows, kv_grad))
    scale_down = jnp.sum(upstream * down_z, axis=0, keepdims=True)
    pair_down = scale_down + partner(scale_down)
    pair_down = pair_down + other_core(pair_down)
    weighted = (pair_down * slopes[DOWN]) * outers[6]
    middle_down = gram_of(weighted, outers[6])
    weighted_parts = jnp.pad(jnp.concatenate(two_parts(weighted)), ((0, 0), (0, EXTRA)))
    first_down = first_grads(
        mm_t(weighted_parts, down_weights),
        jnp.concatenate([b[0] for b in blocks], axis=1),
        narrow_down,
        middle_down,
        down_weights[:, D : D + RANK],
        1,
    )
    kv_grad = kv_back(
        after(kv_grad, first_down).reshape(count, KVH * 2 * HD), cosine, sine
    )
    layer_out = from_tokens_side(after(layer_deep, kv_grad))

    query_rows_low, scale_query, outer_query, narrow_query, middle_query = grad_terms(
        query_grad, query_z, scales[QUERY], slopes[QUERY], outers[0], 0, reduced_one
    )
    back_query = slot_back(place, query_rows_low, [ordered(qkv_slots[k]) for k in range(2)])
    kv_rows_low, scale_kv, outer_kv_grad, narrow_kv, middle_kv = grad_terms(
        kv_grad, kv_z, scales[KV], slopes[KV], outer_kv,
        RANK, reduced_one,
    )
    back_kv = slot_back(place, kv_rows_low, [ordered(qkv_slots[k]) for k in range(2)], half)
    grad_normed, first_one = finish_back(
        [back_query, after(back_kv, layer_deep)],
        [RANK, pairs],
        narrow_query + narrow_kv,
        jnp.concatenate([middle_query, middle_kv]),
        low_main,
        normed_one,
        0,
    )
    grad_tokens = from_tokens(
        (grad_mid + norm_rows_back(residual, gains[0], inverse_one, grad_normed)).astype(BF)
    )

    outer_down = 2.0 * fold_parts(
        t_mm(jnp.concatenate(two_parts(reduced_down), axis=1), down_low), RANK
    )
    of_keys = (jnp.arange(2 * kv_cols) < kv_cols)[None, :]
    outer_kv_grad = jnp.where(of_keys, outer_kv_grad[:RANK], outer_kv_grad[RANK:])
    def second_grads(product, sums, slope, norm, cross):
        return jnp.concatenate([product + 2.0 * (sums * slope) * cross, sums / norm])

    plain = {
        n: second_grads(
            product, sums, slopes[n], norms[n], in_order([cut(c, n) for c in cross_by])
        )
        for n, product, sums in (
            (KV, outer_kv_grad, scale_kv),
            (QUERY, outer_query, scale_query),
            (OUT, outer_out, scale_out),
            (DOWN, outer_down, scale_down),
        )
    }
    mlp_grads = second_grads(
        jnp.concatenate([b[3] for b in blocks], axis=1),
        jnp.concatenate([b[2] for b in blocks], axis=1),
        slope_by[0][MLP],
        norms_by[0][MLP],
        cut(cross_by[0], MLP),
    )
    main_width = 6 * RANK // tok_count
    down_width = RANK // tok_count
    outer_share = OUTS // (tok_count * wide_count)

    lanes = 768
    fit = lanes // share
    tall = main_width // fit
    packed = pack_all(
        place,
        [
            plain[QUERY], plain[KV], plain[OUT], mlp_grads, plain[DOWN], first_one, first_out,
            first_pairs, first_down,
        ],
        tok_count,
        part,
        (tall, down_width, lanes, share, hidden_share, outer_share),
    )
    packed = packed.reshape((tok_count, wide_count) + packed.shape[1:])
    packed = scatter_sum(scatter_sum(packed, "tok", BF), "wide", BF)
    main_part = jnp.swapaxes(packed[:tall].reshape(tall, fit, share), 0, 1)
    main_part = main_part.reshape(main_width, share).T
    down_part = packed[tall : tall + down_width, :hidden_share].T
    outer_sum = packed[tall + down_width : tall + down_width + RANK + 1, :outer_share]
    outer_part = outer_sum[:RANK]
    block_start = (tok * wide_count + wide) * outer_share
    mag_part = outer_sum[RANK]

    local_squares = (
        squared_sum(main_part)
        + squared_sum(down_part)
        + squared_sum(outer_part)
        + squared_sum(mag_part)
    )
    grad_total = all_sum(jnp.full((8, 128), local_squares), ["tok", "wide"])[0, 0]
    grad_norm = jnp.sqrt(grad_total)
    clip_factor = CLIP_MAX / jnp.maximum(grad_norm, CLIP_MAX)
    main_param = lax.dynamic_slice_in_dim(adapt_main, tok * main_width, main_width, 1)
    down_param = lax.dynamic_slice_in_dim(adapt_down, tok * down_width, down_width, 1)
    outer_param = lax.dynamic_slice_in_dim(adapt_outer, block_start, outer_share, 1)
    mag_param = lax.dynamic_slice_in_dim(magnitudes, block_start, outer_share, 0)
    main_new, main_first_new, main_second_new = adam(
        main_param, main_part, main_first, main_second, RATE_ADAPT, clip_factor
    )
    down_new, down_first_new, down_second_new = adam(
        down_param, down_part, down_first, down_second, RATE_ADAPT, clip_factor
    )
    outer_new, outer_first_new, outer_second_new = adam(
        outer_param, outer_part, outer_first, outer_second, RATE_OUTER, clip_factor
    )
    mag_new, mag_first_new, mag_second_new = adam(
        mag_param, mag_part, mag_first, mag_second, RATE_MAGNITUDE, clip_factor
    )
    mag_clipped = mag_part * clip_factor
    return (
        layer_out,
        grad_tokens,
        grad_norm,
        main_new,
        main_first_new,
        main_second_new,
        down_new,
        down_first_new,
        down_second_new,
        outer_new,
        outer_first_new,
        outer_second_new,
        mag_new,
        mag_clipped,
        mag_second_new,
    )


def solution(mesh):
    return jax.shard_map(
        shards,
        mesh=mesh,
        in_specs=(
            P("tok", "wide"),
            P("tok", "wide"),
            P("wide"),
            P("wide"),
            P("wide", None),
            P("wide", None),
            P("wide", None),
            P("wide", None),
            P("wide", None),
            P("wide", None),
            P("wide", None),
            P("wide", None),
            P("wide", None),
            P(),
            P(),
            P("wide", "tok"),
            P("wide", "tok"),
            P("wide", "tok"),
            P("wide", "tok"),
            P(None, ("tok", "wide")),
            P(None, ("tok", "wide")),
            P(("tok", "wide")),
            P(("tok", "wide")),
            P("tok", None),
        ),
        out_specs=(
            P("tok", "wide"),
            P("tok", "wide"),
            P(),
            P("wide", "tok"),
            P("wide", "tok"),
            P("wide", "tok"),
            P("wide", "tok"),
            P("wide", "tok"),
            P("wide", "tok"),
            P(None, ("tok", "wide")),
            P(None, ("tok", "wide")),
            P(None, ("tok", "wide")),
            P(("tok", "wide")),
            P(("tok", "wide")),
            P(("tok", "wide")),
        ),
        check_vma=False,
    )
```
